32 devices in a mesh: dp: 2 (over y), row: 4 (over z), col: 4 (over x, core).
Axes of the slice: x: 2, y: 2, z: 4, core: 2. Of those that a mesh axis runs over, the one named last changes fastest.
Arguments:
- hidden_in: bfloat16 [1024, 768], P(('dp', 'row'), 'col'), may hold values from -6 to 6
- lengths: int32 [8], P('dp'), may hold values from 16 to 128, as said below
- w_attn: bfloat16 [2, 768, 3072], P(None, 'col', 'row'), as said below
- b_qv: bfloat16 [2, 2, 768], P(None, None, 'row'), may hold values from -3 to 3
- b_out: bfloat16 [2, 768], P(None, 'col'), may hold values from -2 to 2
- ln_gain: bfloat16 [2, 2, 768], P(None, None, 'col'), may hold values from 0.5 to 1.5
- ln_bias: bfloat16 [2, 2, 768], P(None, None, 'col'), may hold values from -2 to 2
- w_up: bfloat16 [2, 768, 3072], P(None, 'col', 'row'), may hold values from -0.21875 to 0.21875
- b_up: bfloat16 [2, 3072], P(None, 'row'), may hold values from -3 to 3
- w_down: bfloat16 [2, 768, 3072], P(None, 'col', 'row'), may hold values from -0.15625 to 0.15625
- b_down: bfloat16 [2, 768], P(None, 'col'), may hold values from -2 to 2
- cotangent: bfloat16 [1024, 768], P(('dp', 'row'), 'col'), may hold values from -6 to 6
Outputs:
- out_hidden: bfloat16 [1024, 768], P(('dp', 'row'), 'col')
- grad_input: float32 [1024, 768], P(('dp', 'row'), 'col')
- grad_w_attn: float32 [2, 768, 3072], P(None, 'col', 'row')
- grad_b_qv: float32 [2, 2, 768], P(None, None, 'row')
- grad_b_out: float32 [2, 768], P(None, 'col')
- grad_ln_gain: float32 [2, 2, 768], P(None, None, 'col')
- grad_ln_bias: float32 [2, 2, 768], P(None, None, 'col')
- grad_w_up: float32 [2, 768, 3072], P(None, 'col', 'row')
- grad_b_up: float32 [2, 3072], P(None, 'row')
- grad_w_down: float32 [2, 768, 3072], P(None, 'col', 'row')
- grad_b_down: float32 [2, 768], P(None, 'col')
The draws below stay inside these ranges and needn't reach their ends.
Inputs may be any that keep to these rules, and one draw needn't show every extreme that they name: `lengths`: each sequence's number of leading valid tokens; only keys before it are attended to. `w_attn`: independent entries.
All inputs are finite; a program needn't handle non-finite values.
Results may differ from the reference program's by a relative error of at most 0.03.
Values may be sent and summed in bfloat16 or wider, within the bound.
No kernel may reach another device: no remote copies, remote signals or barrier semaphores. Data moves between devices by JAX's collectives and lax.ppermute only.
A program may use at most 64 MiB of HBM per device.

```python
import jax
import jax.numpy as jnp
from jax import lax

D = 768
HEADS = 12
HEAD_DIM = 64
FF = 3072
LAYERS = 2
SEQ_LEN = 128
SEQS = 8
TOKENS = 1024
FEAT_BLOCK = 192
N_DP = 2
N_ROW = 4


def draw_lengths(key, part):
    key = jax.random.fold_in(key, 11)
    base_key, long_key, short_key = jax.random.split(key, 3)
    shortest = max(SEQ_LEN // 8, 1)
    values = jax.random.randint(base_key, (SEQS,), shortest, SEQ_LEN + 1)
    longest_at = jax.random.randint(long_key, (), 0, SEQS)
    shortest_at = (longest_at + 1 + jax.random.randint(short_key, (), 0, SEQS - 1)) % SEQS
    return values.at[longest_at].set(SEQ_LEN).at[shortest_at].set(shortest).astype(jnp.int32)


def draw_w_attn(key, part):
    key = jax.random.fold_in(key, 23)
    normal_draw = jnp.clip(jax.random.normal(key, (LAYERS, D, 4 * D), jnp.float32), -3.0, 3.0)
    member = jnp.arange(4 * D) % (4 * FEAT_BLOCK) // FEAT_BLOCK
    column_scale = jnp.where(member == 3, float((D // 16) ** (-0.5)), float(D ** (-0.5))).astype(jnp.float32)
    return (normal_draw * column_scale[None, None, :]).astype(jnp.bfloat16)


def shard_levels(key, shape, pieces, low, top_value):
    def one(axis_at, shards_of):
        steps = jax.random.uniform(jax.random.fold_in(jax.random.fold_in(key, 6), axis_at), (shards_of,), jnp.float32, low / len(pieces), top_value / len(pieces))
        return jnp.repeat(jnp.exp(steps), shape[axis_at] // shards_of).reshape((-1,) + (1,) * (len(shape) - axis_at - 1))

    level = one(*pieces[0])
    for cut in pieces[1:]:
        level = level * one(*cut)
    return level


def scatter_about(key, dims, deviation, most, cuts=(), dtype=jnp.bfloat16):
    factor_of = shard_levels(key, dims, cuts, -0.22, 0.18) if cuts else 1.0
    values = jax.random.normal(key, dims, jnp.float32) * deviation * factor_of
    return jnp.minimum(jnp.maximum(values, -most), most).astype(dtype)


def setup_inputs(seed: int = 0) -> dict:
    keys = jax.random.split(jax.random.key(seed), 13)
    return {
        "hidden_in": scatter_about(keys[0], (TOKENS, D), 1.0, 6.0, ((0, 8), (1, 4))),
        "lengths": draw_lengths(jax.random.fold_in(keys[12], 71), 0),
        "w_attn": draw_w_attn(jax.random.fold_in(keys[12], 71), 0),
        "b_qv": scatter_about(keys[3], (LAYERS, 2, D), 0.5, 3.0, ((2, 4),)),
        "b_out": scatter_about(keys[4], (LAYERS, D), 0.3, 2.0, ((1, 4),)),
        "ln_gain": jnp.clip(1.0 + 0.1 * jax.random.normal(keys[5], (LAYERS, 2, D), jnp.float32), 0.5, 1.5).astype(jnp.bfloat16),
        "ln_bias": scatter_about(keys[6], (LAYERS, 2, D), 0.3, 2.0, ((2, 4),)),
        "w_up": scatter_about(keys[7], (LAYERS, D, FF), D ** -0.5, 0.21875, ((1, 4), (2, 4))),
        "b_up": scatter_about(keys[8], (LAYERS, FF), 0.5, 3.0, ((1, 4),)),
        "w_down": scatter_about(keys[9], (LAYERS, D, FF), (FF // 2) ** -0.5, 0.15625, ((1, 4), (2, 4))),
        "b_down": scatter_about(keys[10], (LAYERS, D), 0.3, 2.0, ((1, 4),)),
        "cotangent": scatter_about(keys[11], (TOKENS, D), 1.0, 6.0, ((0, 8), (1, 4))),
    }


@jax.custom_vjp
def low(v):
    return lax.optimization_barrier(v.astype(jnp.bfloat16)).astype(jnp.float32)

@jax.custom_vjp
def low_back(v):
    return v

def low_keep(v):
    return (low(v), None)

def low_pass(kept, grad):
    return (grad,)

def back_keep(v):
    return (v, None)

def back_low(kept, grad):
    return (low(grad),)
low.defvjp(low_keep, low_pass)
low_back.defvjp(back_keep, back_low)
epsilon = 1e-05
masked_score = -1e+30

def product(left_side, right_side):
    return jnp.dot(left_side, right_side, precision=lax.Precision.HIGHEST)

def layer_norm(operand, gain_row, shift_row):
    average = lax.optimization_barrier(jnp.mean(operand, axis=-1, keepdims=True))
    centred = operand - average
    variance = lax.optimization_barrier(jnp.mean(centred * centred, axis=-1, keepdims=True))
    return centred * lax.rsqrt(variance + epsilon) * gain_row + shift_row

def attend_one(operands):
    queries, keyset, values, length = operands
    seq_rows = queries.shape[0]
    head_shape = (seq_rows, HEADS, HEAD_DIM)
    scores = jnp.einsum('qhd,khd->hqk', queries.reshape(head_shape), keyset.reshape(head_shape), precision=lax.Precision.HIGHEST) * HEAD_DIM ** (-0.5)
    scores = low_back(scores)
    visible = jnp.arange(seq_rows) < length
    scores = jnp.where(visible[None, None, :], scores, masked_score)
    weights = low(jax.nn.softmax(scores, axis=-1))
    mixture = jnp.einsum('hqk,khd->qhd', weights, values.reshape(head_shape), precision=lax.Precision.HIGHEST)
    return mixture.reshape(seq_rows, HEADS * HEAD_DIM)

def unpack_attn(w_attn):
    members = w_attn.reshape(D, N_ROW, 4, FEAT_BLOCK).transpose(2, 0, 1, 3)
    return members.reshape(4, D, D)

def block(hidden, length_row, w_attn, b_qv, b_out, gains, shifts, w_up, b_up, w_down, b_down):
    members = unpack_attn(w_attn)
    hidden_low = low(hidden)
    queries = low(low_back(product(hidden_low, members[0]) + b_qv[0]))
    keyset = low(low_back(product(hidden_low, members[1])))
    values = low(low_back(product(hidden_low, members[2]) + b_qv[1]))
    seq_shape = (N_ROW, SEQ_LEN, D)
    attended = lax.map(jax.checkpoint(attend_one), (queries.reshape(seq_shape), keyset.reshape(seq_shape), values.reshape(seq_shape), length_row))
    attended = low(low_back(attended.reshape(N_ROW * SEQ_LEN, D)))
    branch = low_back(product(attended, members[3].T) + b_out)
    normed = layer_norm(hidden + branch, gains[0], shifts[0])
    normed_low = low(normed)
    inner_pre = low_back(product(normed_low, w_up) + b_up)
    active = low(jax.nn.gelu(inner_pre, approximate=False))
    outer_sum = low_back(product(active, w_down.T) + b_down)
    return layer_norm(normed + outer_sum, gains[1], shifts[1])

def forward(hidden, length_row, params):
    for layer_at in range(LAYERS):
        hidden = block(hidden, length_row, *[member[layer_at] for member in params])
    return hidden

def reference(hidden_in, lengths, w_attn, b_qv, b_out, ln_gain, ln_bias, w_up, b_up, w_down, b_down, cotangent):
    params = tuple((member.astype(jnp.float32) for member in (w_attn, b_qv, b_out, ln_gain, ln_bias, w_up, b_up, w_down, b_down)))
    group_shape = (N_DP, N_ROW * SEQ_LEN, D)
    inputs = hidden_in.astype(jnp.float32).reshape(group_shape)
    cotangents = cotangent.astype(jnp.float32).reshape(group_shape)
    group_lengths = lengths.reshape(N_DP, N_ROW)

    def group_step(running, scan_item):
        hidden, cotan_rows, length_row = scan_item

        def run_group(hidden_rows, weights_all):
            return forward(hidden_rows, length_row, weights_all)
        outputs, pullback = jax.vjp(run_group, hidden, params)
        grad_hidden, grad_params = pullback(cotan_rows)
        summed = tuple((earlier + grad_part for earlier, grad_part in zip(running, grad_params)))
        return (summed, (outputs.astype(jnp.bfloat16), grad_hidden))
    zeros_start = tuple((jnp.zeros_like(member) for member in params))
    totals, (outputs, grad_rows) = lax.scan(group_step, zeros_start, (inputs, cotangents, group_lengths))
    return (outputs.reshape(TOKENS, D), grad_rows.reshape(TOKENS, D), totals[0], totals[1], totals[2], totals[3], totals[4], totals[5], totals[6], totals[7], totals[8])
```

```python
from functools import partial

import jax
import jax.numpy as jnp
from jax import lax
from jax.experimental import pallas as pl
from jax.experimental.pallas import tpu as pltpu
from jax.sharding import PartitionSpec as P


HEAD_DIM = 64
EPS = 1e-5
MASKED = -1e30
F32 = jnp.float32
BF16 = jnp.bfloat16


def exchange(x, axis, bit):
    n = lax.axis_size(axis)
    return lax.ppermute(x, axis, [(i, i ^ bit) for i in range(n)])


def turned(x, bit):
    n = lax.axis_size("row")
    pairs = [(a * n + b, (b ^ bit) * n + a) for a in range(n) for b in range(n)]
    return lax.ppermute(x, ("row", "col"), pairs)


def turned_back(x, bit):
    n = lax.axis_size("row")
    pairs = [(a * n + b, b * n + (a ^ bit)) for a in range(n) for b in range(n)]
    return lax.ppermute(x, ("row", "col"), pairs)


def gather_col(x):
    far = exchange(x, "col", 2)
    return [x, exchange(x, "col", 1), far, exchange(far, "col", 1)]


def gather_row(x):
    return [x] + [exchange(x, "row", k) for k in range(1, lax.axis_size("row"))]


def scatter_row(pieces):
    return [pieces[0]] + [exchange(pieces[k], "row", k) for k in range(1, len(pieces))]


def call(kernel, outs, *args, scalars=None):
    vmem = pl.BlockSpec(memory_space=pltpu.VMEM)
    specs = [vmem] * len(args)
    if scalars is not None:
        args = (scalars,) + args
        specs = [pl.BlockSpec(memory_space=pltpu.SMEM)] + specs
    read = sum(a.size * a.dtype.itemsize for a in args)
    wrote = sum(o.size * o.dtype.itemsize for o in outs)
    return pl.pallas_call(
        kernel,
        out_shape=outs,
        in_specs=specs,
        out_specs=[vmem] * len(outs),
        compiler_params=pltpu.CompilerParams(vmem_limit_bytes=40 * 1024 * 1024),
        cost_estimate=pl.CostEstimate(
            flops=200_000_000, bytes_accessed=read + wrote, transcendentals=0
        ),
    )(*args)


def sds(shape, dtype):
    return jax.ShapeDtypeStruct(shape, dtype)


def rows_of(refs):
    return jnp.concatenate([r[...] for r in refs], axis=0)


def lanes_of(refs):
    return jnp.concatenate([r[...] for r in refs], axis=1)


def dot(a, b):
    return jnp.dot(a, b, preferred_element_type=F32)


def dot_t(a, b):
    return lax.dot_general(a, b, (((1,), (1,)), ((), ())), preferred_element_type=F32)


def t_dot(a, b):
    return lax.dot_general(a, b, (((0,), (0,)), ((), ())), preferred_element_type=F32)


def prep_kernel(n, sc, *refs):
    pieces, outs, full = refs[:n], refs[n : 2 * n], refs[2 * n]
    row, col = sc[0], sc[1]
    width = pieces[0].shape[1]
    block = outs[0].shape[0]
    for k in range(n):
        for j in range(n):

            @pl.when((col ^ row ^ k) == j)
            def _():
                full[:, j * width : (j + 1) * width] = pieces[k][...].astype(F32)

    for k in range(n):
        outs[k][...] = full[pl.ds(pl.multiple_of((row ^ k) * block, block), block), :].astype(BF16)


def turn_in_kernel(n, sc, *refs):
    pieces, out = refs[:n], refs[n]
    row, col = sc[0], sc[1]
    width = pieces[0].shape[1]
    for k in range(n):
        for j in range(n):

            @pl.when((col ^ row ^ k) == j)
            def _():
                out[:, j * width : (j + 1) * width] = pieces[k][...].astype(F32)


def turn_out_kernel(n, sc, x, *outs):
    row, col = sc[0], sc[1]
    width = outs[0].shape[1]
    for k in range(n):
        for j in range(n):

            @pl.when((col ^ row ^ k) == j)
            def _():
                outs[k][...] = x[:, j * width : (j + 1) * width].astype(outs[k].dtype)


def sum_turn_out_kernel(n, sc, *refs):
    pieces, base, outs = refs[:n], refs[n], refs[n + 1 : 2 * n + 1]
    total = refs[2 * n + 1]
    total[...] = base[...] + tree(pieces)
    turn_out_kernel(n, sc, total, *outs)


def assemble_kernel(n, sc, *refs):
    pieces, out = refs[:n], refs[n]
    col = sc[1]
    block = pieces[0].shape[0]
    for k in range(n):
        out[pl.ds(pl.multiple_of((col ^ k) * block, block), block), :] = pieces[k][...]


def tree(pieces):
    values = [p[...].astype(F32) for p in pieces]
    while len(values) > 1:
        values = [values[i] + values[i + 1] for i in range(0, len(values), 2)]
    return values[0]


def attend_kernel(n, m, layer, sc, *refs):
    x_refs, w_refs = refs[:n], refs[n : n + m]
    bias = refs[n + m]
    outs = refs[n + m + 1 :]
    z_refs, (qkv_ref, p_ref, o_ref) = outs[:n], outs[n:]
    row, length = sc[0], sc[2]
    x = rows_of(x_refs)
    w = rows_of(w_refs)
    width = w.shape[1] // 4
    both = bias[layer].astype(F32)
    shift = jnp.concatenate([both[0:1], jnp.zeros((1, width), F32), both[1:2]], axis=1)
    qkv = (dot(x, w[:, : 3 * width]) + shift).astype(BF16)
    qkv_ref[...] = qkv
    tokens = x.shape[0]
    block = tokens // n
    key_at = lax.broadcasted_iota(jnp.int32, (tokens, tokens), 1)
    place = ((key_at // block) ^ row) * block + key_at % block
    visible = place < length
    mixed = []
    for h in range(width // HEAD_DIM):
        q = qkv[:, h * HEAD_DIM : (h + 1) * HEAD_DIM]
        k = qkv[:, width + h * HEAD_DIM : width + (h + 1) * HEAD_DIM]
        v = qkv[:, 2 * width + h * HEAD_DIM : 2 * width + (h + 1) * HEAD_DIM]
        s = jnp.where(visible, dot_t(q, k) * HEAD_DIM ** (-0.5), MASKED)
        e = jnp.exp(s - jnp.max(s, axis=-1, keepdims=True))
        p = e / jnp.sum(e, axis=-1, keepdims=True)
        p_ref[h] = p
        mixed.append(dot(p.astype(BF16), v))
    o = jnp.concatenate(mixed, axis=1).astype(BF16)
    o_ref[...] = o
    z = dot_t(o, w[:, 3 * width :])
    for k in range(n):
        z_refs[k][...] = z[k * block : (k + 1) * block].astype(z_refs[k].dtype)


def norm_kernel(n, at, *refs):
    pieces, base, bias, gain, shift = refs[:n], refs[n], refs[n + 1], refs[n + 2], refs[n + 3]
    out32, out16, unit, inverse = refs[n + 4 :]
    layer, which = at
    b = bias[layer : layer + 1, :].astype(F32)
    g = gain[2 * layer + which : 2 * layer + which + 1, :].astype(F32)
    c = shift[2 * layer + which : 2 * layer + which + 1, :].astype(F32)
    v = base[...].astype(F32) + (tree(pieces) + b)
    mean = jnp.mean(v, axis=-1, keepdims=True)
    centred = v - mean
    r = lax.rsqrt(jnp.mean(centred * centred, axis=-1, keepdims=True) + EPS)
    normed = centred * r
    y = normed * g + c
    out32[...] = y
    out16[...] = y.astype(BF16)
    unit[...] = normed
    inverse[...] = jnp.broadcast_to(r, inverse.shape)


def norm_back_kernel(n, at, *refs):
    pieces, base, unit, inverse, gain = refs[:n], refs[n], refs[n + 1], refs[n + 2], refs[n + 3]
    out32, out16, sums = refs[n + 4 :]
    layer, which = at
    g = gain[2 * layer + which : 2 * layer + which + 1, :].astype(F32)
    e = base[...]
    if n:
        e = e + tree(pieces)
    normed = unit[...]
    r = inverse[:, 0:1]
    c = e * g
    grad = r * (
        c
        - jnp.mean(c, axis=-1, keepdims=True)
        - normed * jnp.mean(c * normed, axis=-1, keepdims=True)
    )
    low = grad.astype(BF16)
    out32[...] = grad
    out16[...] = low
    sums[0:1, :] = jnp.sum(e * normed, axis=0, keepdims=True)
    sums[1:2, :] = jnp.sum(e, axis=0, keepdims=True)
    sums[2:3, :] = jnp.sum(low.astype(F32), axis=0, keepdims=True)
    sums[3:8, :] = jnp.zeros((5, sums.shape[1]), F32)


def feed_kernel(n, m, layer, *refs):
    h_refs, up_refs, down_refs = refs[:n], refs[n : n + m], refs[n + m : n + 2 * m]
    bias = refs[n + 2 * m]
    outs = refs[n + 2 * m + 1 :]
    f_refs, (g_ref, slope_ref) = outs[:n], outs[n:]
    u = dot(rows_of(h_refs), rows_of(up_refs)) + bias[layer : layer + 1, :].astype(F32)
    cdf = 0.5 * (1.0 + lax.erf(u * (0.5**0.5)))
    g = (u * cdf).astype(BF16)
    g_ref[...] = g
    slope_ref[...] = cdf + u * (jnp.exp(-0.5 * u * u) * 0.3989422804014327)
    f = dot_t(g, rows_of(down_refs))
    block = f_refs[0].shape[0]
    for k in range(n):
        f_refs[k][...] = f[k * block : (k + 1) * block].astype(f_refs[k].dtype)


def feed_back_kernel(n, m, *refs):
    d_refs, up_refs, down_refs = refs[:n], refs[n : n + m], refs[n + m : n + 2 * m]
    slope = refs[n + 2 * m]
    outs = refs[n + 2 * m + 1 :]
    h_refs, du_ref = outs[:n], outs[n]
    dg = dot(rows_of(d_refs), rows_of(down_refs))
    du = (dg * slope[...]).astype(BF16)
    du_ref[...] = du
    dh = dot_t(du, rows_of(up_refs))
    block = h_refs[0].shape[0]
    for k in range(n):
        h_refs[k][...] = dh[k * block : (k + 1) * block].astype(h_refs[k].dtype)


def split_blocks(grad, m, at, keep, send):
    block = grad.shape[0] // m
    half = m // 2
    for k in range(m):
        target = send if k % 2 else keep
        start = (at * half + k // 2) * block
        target[start : start + block, :] = grad[k * block : (k + 1) * block].astype(target.dtype)


def feed_weight_kernel(n, m, *refs):
    d_refs, h_refs, g, du = refs[:n], refs[n : 2 * n], refs[2 * n], refs[2 * n + 1]
    keep, send, sums = refs[2 * n + 2 :]
    split_blocks(t_dot(rows_of(d_refs), g[...]), m, 0, keep, send)
    split_blocks(t_dot(rows_of(h_refs), du[...]), m, 1, keep, send)
    sums[0:1, :] = jnp.sum(du[...].astype(F32), axis=0, keepdims=True)
    sums[1:8, :] = jnp.zeros((7, sums.shape[1]), F32)


def attend_back_kernel(n, m, *refs):
    d_refs, w_refs = refs[:n], refs[n : n + m]
    qkv_ref, p_ref = refs[n + m], refs[n + m + 1]
    outs = refs[n + m + 2 :]
    x_refs, grads = outs[:n], outs[n]
    w = rows_of(w_refs)
    width = w.shape[1] // 4
    do = dot(rows_of(d_refs), w[:, 3 * width :]).astype(BF16)
    qkv = qkv_ref[...]
    dq, dk, dv = [], [], []
    for h in range(width // HEAD_DIM):
        q = qkv[:, h * HEAD_DIM : (h + 1) * HEAD_DIM]
        k = qkv[:, width + h * HEAD_DIM : width + (h + 1) * HEAD_DIM]
        v = qkv[:, 2 * width + h * HEAD_DIM : 2 * width + (h + 1) * HEAD_DIM]
        d = do[:, h * HEAD_DIM : (h + 1) * HEAD_DIM]
        p = p_ref[h]
        dv.append(t_dot(p.astype(BF16), d))
        dp = dot_t(d, v)
        ds = (p * (dp - jnp.sum(p * dp, axis=-1, keepdims=True))).astype(BF16)
        dq.append(dot(ds, k) * HEAD_DIM ** (-0.5))
        dk.append(t_dot(ds, q) * HEAD_DIM ** (-0.5))
    low = jnp.concatenate(dq + dk + dv, axis=1).astype(BF16)
    grads[...] = low
    dx = dot_t(low, w[:, : 3 * width])
    block = x_refs[0].shape[0]
    for k in range(n):
        x_refs[k][...] = dx[k * block : (k + 1) * block].astype(x_refs[k].dtype)


def attend_weight_kernel(n, m, *refs):
    x_refs, d_refs, o, grads = refs[:n], refs[n : 2 * n], refs[2 * n], refs[2 * n + 1]
    keep, send, sums = refs[2 * n + 2 :]
    low = grads[...]
    first = t_dot(rows_of(x_refs), low)
    second = t_dot(rows_of(d_refs), o[...])
    split_blocks(jnp.concatenate([first, second], axis=1), m, 0, keep, send)
    sums[...] = jnp.zeros(sums.shape, F32)
    sums[0:1, 0 : low.shape[1]] = jnp.sum(low.astype(F32), axis=0, keepdims=True)


def reduce_dp(x):
    bit = 1
    while bit < lax.axis_size("dp"):
        x = x + exchange(x, "dp", bit)
        bit *= 2
    return x


def reduce_blocks(keep, send, parts):
    total = keep + exchange(send, "col", 1).astype(F32)
    block = keep.shape[0] // (2 * parts)
    total = total.reshape(parts, 2, block, keep.shape[1])
    mine = total[:, 0] + exchange(total[:, 1].astype(BF16), "col", 2).astype(F32)
    low = mine.astype(BF16)
    if lax.axis_size("dp") == 2:
        return low.astype(F32) + exchange(low, "dp", 1).astype(F32)
    return reduce_dp(low.astype(F32))


def per_device(
    hidden_in, lengths, w_attn, b_qv, b_out, ln_gain, ln_bias, w_up, b_up, w_down, b_down, cotangent
):
    layers = w_attn.shape[0]
    n, m = lax.axis_size("row"), lax.axis_size("col")
    row, col = lax.axis_index("row"), lax.axis_index("col")
    tokens, piece = hidden_in.shape
    block = tokens // n
    model = piece * m
    hidden = w_up.shape[2]
    length = lax.dynamic_index_in_dim(lengths, col, 0, keepdims=False)
    scalars = jnp.stack([row, col, length]).astype(jnp.int32)

    x_in = [turned(hidden_in, k) for k in range(n)]
    attn = [gather_col(w_attn[0])]
    rows = jnp.concatenate(
        [
            b_out,
            b_down,
            ln_gain.reshape(2 * layers, piece),
            ln_bias.reshape(2 * layers, piece),
        ]
    )
    rows = jnp.concatenate(gather_col(rows), axis=1)
    b_out_all, b_down_all = rows[:layers], rows[layers : 2 * layers]
    gains, shifts = rows[2 * layers : 4 * layers], rows[4 * layers :]
    ups, downs = [], []
    for layer in range(layers):
        if layer:
            attn.append(gather_col(w_attn[layer]))
        ups.append(gather_col(w_up[layer]))
        downs.append(gather_col(w_down[layer]))
    ct_in = [
        turned(lax.dynamic_slice_in_dim(cotangent, (col ^ k) * block, block, 0), k)
        for k in range(n)
    ]

    low_block = sds((block, model), BF16)
    full_block = sds((block, model), F32)
    pieces_out = [full_block] + [low_block] * (n - 1)
    inverse_out = sds((block, 128), F32)
    norm_out = [full_block, low_block, full_block, inverse_out]

    *x_low, _ = call(
        partial(prep_kernel, n),
        [low_block] * n + [sds((tokens, model), F32)],
        *x_in,
        scalars=scalars,
    )
    base = x_low[0]
    saved = []
    for layer in range(layers):
        *z, qkv, probs, mixed = call(
            partial(attend_kernel, n, m, layer),
            pieces_out
            + [
                sds((tokens, 3 * piece), BF16),
                sds((piece // HEAD_DIM, tokens, tokens), F32),
                sds((tokens, piece), BF16),
            ],
            *x_low,
            *attn[layer],
            b_qv,
            scalars=scalars,
        )
        z = scatter_row(z)
        h32, h16, unit_one, inverse_one = call(
            partial(norm_kernel, n, (layer, 0)), norm_out, *z, base, b_out_all, gains, shifts
        )
        h_low = gather_row(h16)
        *f, active, slope = call(
            partial(feed_kernel, n, m, layer),
            pieces_out + [sds((tokens, hidden), BF16), sds((tokens, hidden), F32)],
            *h_low,
            *ups[layer],
            *downs[layer],
            b_up,
        )
        f = scatter_row(f)
        base, low, unit_two, inverse_two = call(
            partial(norm_kernel, n, (layer, 1)), norm_out, *f, h32, b_down_all, gains, shifts
        )
        saved.append(
            (x_low, qkv, probs, mixed, unit_one, inverse_one, h_low, active, slope, unit_two, inverse_two)
        )
        if layer + 1 < layers:
            x_low = gather_row(low)

    outs = call(
        partial(turn_out_kernel, n), [sds((block, piece), BF16)] * n, base, scalars=scalars
    )
    (out_hidden,) = call(
        partial(assemble_kernel, n),
        [sds((tokens, piece), BF16)],
        *[turned_back(o, k) for k, o in enumerate(outs)],
        scalars=scalars,
    )

    (flow,) = call(partial(turn_in_kernel, n), [full_block], *ct_in, scalars=scalars)
    sums_out = sds((8, model), F32)
    back_out = [full_block, low_block, sums_out]
    flow_pieces = []
    norm_sums, up_sums, qv_sums = [None] * layers, [None] * layers, [None] * layers
    attn_grads, up_grads, down_grads = [None] * layers, [None] * layers, [None] * layers
    for layer in reversed(range(layers)):
        x_low, qkv, probs, mixed, unit_one, inverse_one, h_low, active, slope, unit_two, inverse_two = (
            saved[layer]
        )
        df, df_low, sums_two = call(
            partial(norm_back_kernel, len(flow_pieces), (layer, 1)),
            back_out,
            *flow_pieces,
            flow,
            unit_two,
            inverse_two,
            gains,
        )
        df_all = gather_row(df_low)
        *dh, du = call(
            partial(feed_back_kernel, n, m),
            pieces_out + [sds((tokens, hidden), BF16)],
            *df_all,
            *ups[layer],
            *downs[layer],
            slope,
        )
        dh = scatter_row(dh)
        keep, send, up_sums[layer] = call(
            partial(feed_weight_kernel, n, m),
            [sds((model, hidden), F32), sds((model, hidden), BF16), sds((8, hidden), F32)],
            *df_all,
            *h_low,
            active,
            du,
        )
        both = reduce_blocks(keep, send, 2)
        down_grads[layer], up_grads[layer] = both[0], both[1]
        da, da_low, sums_one = call(
            partial(norm_back_kernel, n, (layer, 0)),
            back_out,
            *dh,
            df,
            unit_one,
            inverse_one,
            gains,
        )
        norm_sums[layer] = (sums_one, sums_two)
        da_all = gather_row(da_low)
        *dx, grads = call(
            partial(attend_back_kernel, n, m),
            pieces_out + [sds((tokens, 3 * piece), BF16)],
            *da_all,
            *attn[layer],
            qkv,
            probs,
        )
        flow_pieces = scatter_row(dx)
        flow = da
        keep, send, qv_sums[layer] = call(
            partial(attend_weight_kernel, n, m),
            [
                sds((model // 2, 4 * piece), F32),
                sds((model // 2, 4 * piece), BF16),
                sds((8, model), F32),
            ],
            *x_low,
            *da_all,
            mixed,
            grads,
        )
        attn_grads[layer] = reduce_blocks(keep, send, 1)[0]

    *outs, _ = call(
        partial(sum_turn_out_kernel, n),
        [sds((block, piece), F32)] * n + [full_block],
        *flow_pieces,
        flow,
        scalars=scalars,
    )
    (grad_input,) = call(
        partial(assemble_kernel, n),
        [sds((tokens, piece), F32)],
        *[turned_back(o, k) for k, o in enumerate(outs)],
        scalars=scalars,
    )

    sums = jnp.concatenate([s[:3] for pair in norm_sums for s in pair])
    others = [exchange(sums, "row", k) for k in range(1, n)]
    sums = (sums + others[0]) + (others[1] + others[2])
    sums = sums.reshape(sums.shape[0], m, piece)
    sums = sums[:, 0::2] + exchange(sums[:, 1::2], "col", 1)
    sums = sums[:, 0] + exchange(sums[:, 1], "col", 2)
    sums = reduce_dp(sums).reshape(layers, 2, 3, piece)
    wide = jnp.concatenate([s[0:1] for s in up_sums] + [s[0:1] for s in qv_sums])
    wide = wide + exchange(wide, "col", 1)
    wide = wide + exchange(wide, "col", 2)
    wide = reduce_dp(wide)
    qv = wide[layers:, : 3 * piece].reshape(layers, 3, piece)
    return (
        out_hidden,
        grad_input,
        jnp.stack(attn_grads),
        qv[:, 0::2],
        sums[:, 0, 2],
        sums[:, :, 0],
        sums[:, :, 1],
        jnp.stack(up_grads),
        wide[:layers],
        jnp.stack(down_grads),
        sums[:, 1, 2],
    )


def solution(mesh):
    in_specs = (
        P(("dp", "row"), "col"),
        P("dp"),
        P(None, "col", "row"),
        P(None, None, "row"),
        P(None, "col"),
        P(None, None, "col"),
        P(None, None, "col"),
        P(None, "col", "row"),
        P(None, "row"),
        P(None, "col", "row"),
        P(None, "col"),
        P(("dp", "row"), "col"),
    )
    out_specs = (
        P(("dp", "row"), "col"),
        P(("dp", "row"), "col"),
        P(None, "col", "row"),
        P(None, None, "row"),
        P(None, "col"),
        P(None, None, "col"),
        P(None, None, "col"),
        P(None, "col", "row"),
        P(None, "row"),
        P(None, "col", "row"),
        P(None, "col"),
    )
    return jax.shard_map(
        per_device, mesh=mesh, in_specs=in_specs, out_specs=out_specs, check_vma=False
    )
```

```python
import math
from functools import partial

import jax
import jax.numpy as jnp
from jax import lax
from jax.experimental import pallas as pl
from jax.experimental.pallas import tpu as pltpu
from jax.sharding import PartitionSpec as P


HEAD_DIM = 64
EPS = 1e-5
MASKED = -1e30
F32 = jnp.float32
BF16 = jnp.bfloat16


def exchange(x, axis, bit):
    n = lax.axis_size(axis)
    return lax.ppermute(x, axis, [(i, i ^ bit) for i in range(n)])


def turned(x, bit):
    n = lax.axis_size("row")
    pairs = [(a * n + b, (b ^ bit) * n + a) for a in range(n) for b in range(n)]
    return lax.ppermute(x, ("row", "col"), pairs)


def last_of_dp(low):
    bit = 1
    while 2 * bit < lax.axis_size("dp"):
        low = (low.astype(F32) + exchange(low, "dp", bit).astype(F32)).astype(BF16)
        bit *= 2
    return low, exchange(low, "dp", bit)


def sds(shape, dtype):
    return jax.ShapeDtypeStruct(shape, dtype)


def whole(array):
    return (array, array.shape, (0,) * array.ndim)


def call(kernel, outs, ins, scratch=(), after=(), final=False):
    vmem = pl.BlockSpec(memory_space=pltpu.VMEM)
    specs, args = [], []
    moved = 0
    for item in ins:
        if isinstance(item, tuple):
            array, shape, index = item
            specs.append(pl.BlockSpec(shape, lambda i, index=index: index))
            moved += math.prod(shape) * array.dtype.itemsize
            args.append(array)
            continue
        args.append(item)
        if item.dtype == jnp.int32:
            specs.append(pl.BlockSpec(memory_space=pltpu.SMEM))
        else:
            specs.append(vmem)
            moved += item.size * item.dtype.itemsize
    moved += sum(o.size * o.dtype.itemsize for o in outs)
    n_in, n_after, n_out = len(ins), len(after), len(outs)

    def body(*refs):
        kernel(
            refs[:n_in],
            refs[n_in + n_after : n_in + n_after + n_out],
            refs[n_in + n_after + n_out :],
        )

    return pl.pallas_call(
        body,
        grid=(1,),
        out_shape=outs,
        in_specs=specs + [pl.BlockSpec(memory_space=pl.ANY)] * n_after,
        out_specs=[
            pl.BlockSpec(o.shape, lambda i, d=len(o.shape): (0,) * d) if final else vmem
            for o in outs
        ],
        scratch_shapes=list(scratch),
        compiler_params=pltpu.CompilerParams(vmem_limit_bytes=32 * 1024 * 1024),
        cost_estimate=pl.CostEstimate(
            flops=200_000_000, bytes_accessed=moved, transcendentals=0
        ),
    )(*args, *after)


def rows_of(refs):
    rows = refs[0].shape[0] // 64 * 64
    return jnp.concatenate([r[:rows, :] for r in refs], axis=0)


def dot(a, b):
    return jnp.dot(a, b, preferred_element_type=F32)


def dot_t(a, b):
    return lax.dot_general(a, b, (((1,), (1,)), ((), ())), preferred_element_type=F32)


def t_dot(a, b):
    return lax.dot_general(a, b, (((0,), (0,)), ((), ())), preferred_element_type=F32)


def f32(ref):
    return ref[...].astype(F32)


def tree(refs):
    values = [f32(r) for r in refs]
    while len(values) > 1:
        values = [values[i] + values[i + 1] for i in range(0, len(values), 2)]
    return values[0]


def params_of(prm, layer, which):
    rows = (2 * which + layer, 4 + 2 * layer + which, 8 + 2 * layer + which)
    return [prm[i : i + 1, :] for i in rows]


def norm_of(v):
    mean = jnp.mean(v, axis=-1, keepdims=True)
    centred = v - mean
    r = lax.rsqrt(jnp.mean(centred * centred, axis=-1, keepdims=True) + EPS)
    return centred * r, r


def norm_back(e, unit, r, gain):
    c = e * gain
    return r * (
        c
        - jnp.mean(c, axis=-1, keepdims=True)
        - unit * jnp.mean(c * unit, axis=-1, keepdims=True)
    )


def put_unit(ref, unit, r):
    model = unit.shape[1]
    ref[:, :model] = unit
    ref[:, model:] = jnp.broadcast_to(r, (unit.shape[0], 128))


def get_unit(ref):
    model = ref.shape[1] - 128
    return ref[:, :model], ref[:, model : model + 1]


def put_sums(ref, e, unit, low):
    ref[0:1, :] = jnp.sum(e * unit, axis=0, keepdims=True)
    ref[1:2, :] = jnp.sum(e, axis=0, keepdims=True)
    ref[2:3, :] = jnp.sum(low.astype(F32), axis=0, keepdims=True)
    ref[3:8, :] = jnp.zeros((5, ref.shape[1]), F32)


def place_features(sc, pieces, target):
    place = sc[0] ^ sc[1]
    width = pieces[0].shape[1]
    for k, piece in enumerate(pieces):
        for j in range(len(pieces)):

            @pl.when((place ^ k) == j)
            def _():
                target[:, j * width : (j + 1) * width] = piece[...].astype(target.dtype)


def pick_features(at, count, value, target):
    width = value.shape[1] // count
    for j in range(count):

        @pl.when(at == j)
        def _():
            target[...] = value[:, j * width : (j + 1) * width].astype(target.dtype)


def project(sc, layer, x, w, rowwise, qkv_ref, p_ref):
    tokens = x.shape[0]
    width = w.shape[1] // 4
    b = rowwise[2 + layer : 3 + layer, : 2 * width].astype(F32)
    shift = jnp.concatenate([b[:, :width], jnp.zeros((1, width), F32), b[:, width:]], axis=1)
    qkv = (dot(x, w[:, : 3 * width]) + shift).astype(BF16)
    qkv_ref[...] = qkv
    visible = lax.broadcasted_iota(jnp.int32, (tokens, tokens), 1) < sc[2]
    mixed = []
    for h in range(width // HEAD_DIM):
        q = qkv[:, h * HEAD_DIM : (h + 1) * HEAD_DIM]
        k = qkv[:, width + h * HEAD_DIM : width + (h + 1) * HEAD_DIM]
        v = qkv[:, 2 * width + h * HEAD_DIM : 2 * width + (h + 1) * HEAD_DIM]
        s = jnp.where(visible, dot_t(q, k) * HEAD_DIM ** (-0.5), MASKED)
        e = jnp.exp(s - jnp.max(s, axis=-1, keepdims=True))
        p = e / jnp.sum(e, axis=-1, keepdims=True)
        p_ref[h] = p
        mixed.append(dot(p.astype(BF16), v))
    return jnp.concatenate(mixed, axis=1).astype(BF16)


def mix_out(o, w):
    return dot_t(o, w[:, 3 * (w.shape[1] // 4) :])


def attend_back(d, w, qkv_ref, p_ref):
    width = w.shape[1] // 4
    do = dot(d, w[:, 3 * width :]).astype(BF16)
    qkv = qkv_ref[...]
    dq, dk, dv = [], [], []
    for h in range(width // HEAD_DIM):
        q = qkv[:, h * HEAD_DIM : (h + 1) * HEAD_DIM]
        k = qkv[:, width + h * HEAD_DIM : width + (h + 1) * HEAD_DIM]
        v = qkv[:, 2 * width + h * HEAD_DIM : 2 * width + (h + 1) * HEAD_DIM]
        g = do[:, h * HEAD_DIM : (h + 1) * HEAD_DIM]
        p = p_ref[h]
        dv.append(t_dot(p.astype(BF16), g))
        dp = dot_t(g, v)
        ds = (p * (dp - jnp.sum(p * dp, axis=-1, keepdims=True))).astype(BF16)
        dq.append(dot(ds, k) * HEAD_DIM ** (-0.5))
        dk.append(t_dot(ds, q) * HEAD_DIM ** (-0.5))
    return jnp.concatenate(dq + dk + dv, axis=1).astype(BF16)


def heads_back(low, w):
    return dot_t(low, w[:, : 3 * (w.shape[1] // 4)])


def raise_hidden(layer, h, up, rowwise):
    u = dot(h, up) + rowwise[layer : layer + 1, :].astype(F32)
    cdf = 0.5 * (1.0 + lax.erf(u * (0.5**0.5)))
    slope = cdf + u * (jnp.exp(-0.5 * u * u) * 0.3989422804014327)
    return (u * cdf).astype(BF16), slope


def split_blocks(grad, count, part, parts, keep, send):
    block = grad.shape[0] // count
    each = keep.shape[0] // (2 * parts)
    for k in range(count):
        target = send if k % 2 else keep
        start = ((k // 2) * parts + part) * each
        target[start : start + block, :] = grad[k * block : (k + 1) * block].astype(BF16)


def k_start(ins, outs, scr):
    w, b_out, b_down, gain, shift, b_up, b_qv, hidden_in, cotangent = ins
    block, rowwise, pair = outs
    rows, piece = w.shape[1], b_out.shape[1]
    block[:rows, :] = w[0]
    norms = [b_out[...], b_down[...], gain[0], gain[1], shift[0], shift[1]]
    norms = jnp.concatenate([x.astype(F32) for x in norms] + [jnp.zeros((4, piece), F32)], axis=0)
    block[rows:, :piece] = norms.astype(BF16)
    block[rows:, piece:] = jnp.zeros((16, block.shape[1] - piece), BF16)
    qv = [b_qv[i].astype(F32) for i in range(2)]
    qv = [jnp.concatenate([x[0:1], x[1:2]], axis=1) for x in qv]
    rest = b_up.shape[1] - qv[0].shape[1]
    qv = jnp.concatenate([jnp.concatenate(qv, axis=0), jnp.zeros((2, rest), F32)], axis=1)
    low = jnp.concatenate([b_up[...].astype(F32), qv, jnp.zeros((12, b_up.shape[1]), F32)], axis=0)
    rowwise[...] = low.astype(BF16)
    tokens = hidden_in.shape[0]
    pair[:tokens, :] = hidden_in[...]
    pair[tokens:, :] = cotangent[...]


def k_pack(ins, outs, scr):
    at = 0
    for ref in ins:
        value = ref[0] if len(ref.shape) == 3 else ref[...]
        outs[0][at : at + value.shape[0], :] = value
        at += value.shape[0]


def k_prep(ins, outs, scr):
    sc, *pieces = ins
    tokens = outs[0].shape[0]
    place_features(sc, [p.at[:tokens] for p in pieces], outs[0])
    place_features(sc, [p.at[tokens:] for p in pieces], outs[1])


def k_sum(ins, outs, scr):
    outs[0][...] = (f32(ins[0]) + f32(ins[1])).astype(BF16)


def k_attend_first(m, ins, outs, scr):
    sc, x = ins[:2]
    w_refs, rowwise = ins[2 : 2 + m], ins[2 + m]
    z_ref, prm, o_ref, qkv, p = outs
    piece = w_refs[0].shape[0] - 16
    prm[...] = jnp.concatenate([w[piece:, :piece].astype(F32) for w in w_refs], axis=1)
    w = rows_of(w_refs)
    o = project(sc, 0, x[...], w, rowwise, qkv, p)
    o_ref[...] = o
    z_ref[...] = mix_out(o, w).astype(BF16)


def k_feed(m, layer, ins, outs, scr):
    z, z_other, base = ins[:3]
    up, down = ins[3 : 3 + m], ins[3 + m : 3 + 2 * m]
    rowwise, prm = ins[3 + 2 * m :]
    f_ref, unit_ref, h_ref, g_ref, slope_ref = outs
    if layer:
        _, gain, shift = params_of(prm, layer - 1, 1)
        x = get_unit(base)[0] * gain + shift
    else:
        x = f32(base)
    bias, gain, shift = params_of(prm, layer, 0)
    unit, r = norm_of(x + (f32(z) + f32(z_other) + bias))
    put_unit(unit_ref, unit, r)
    h = (unit * gain + shift).astype(BF16)
    h_ref[...] = h
    g, slope = raise_hidden(layer, h, rows_of(up), rowwise)
    g_ref[...] = g
    slope_ref[...] = slope
    f_ref[...] = dot_t(g, rows_of(down)).astype(BF16)


def k_attend(m, layer, ins, outs, scr):
    sc, f, f_other, unit_ref = ins[:4]
    own = ins[4 : 4 + m]
    rowwise, prm = ins[4 + m :]
    z_ref, unit_out, x_ref, o_ref, qkv, p = outs
    _, gain, shift = params_of(prm, layer - 1, 0)
    h = get_unit(unit_ref)[0] * gain + shift
    bias, gain, shift = params_of(prm, layer - 1, 1)
    unit, r = norm_of(h + (f32(f) + f32(f_other) + bias))
    put_unit(unit_out, unit, r)
    x = (unit * gain + shift).astype(BF16)
    x_ref[...] = x
    w = rows_of(own)
    o = project(sc, layer, x, w, rowwise, qkv, p)
    o_ref[...] = o
    z_ref[...] = mix_out(o, w).astype(BF16)


def feed_back(e, unit, r, gain, ws, slope, outs):
    up, down = ws
    df_ref, low_ref, dh_ref, du_ref, sums = outs
    df = norm_back(e, unit, r, gain)
    low = df.astype(BF16)
    df_ref[...] = df
    low_ref[...] = low
    put_sums(sums, e, unit, low)
    du = (dot(low, rows_of(down)) * slope[...]).astype(BF16)
    du_ref[...] = du
    dh_ref[...] = dot_t(du, rows_of(up)).astype(BF16)


def k_turn(m, layer, ins, outs, scr):
    sc, f, f_other, unit_ref, cotan = ins[:5]
    ws = [ins[5 + i * m : 5 + (i + 1) * m] for i in range(2)]
    slope, prm = ins[5 + 2 * m :]
    _, gain, shift = params_of(prm, layer, 0)
    h = get_unit(unit_ref)[0] * gain + shift
    bias, gain, shift = params_of(prm, layer, 1)
    unit, r = norm_of(h + (f32(f) + f32(f_other) + bias))
    pick_features(sc[0] ^ sc[1], m, unit * gain + shift, outs[0])
    feed_back(f32(cotan), unit, r, gain, ws, slope, outs[1:])


def k_feed_back(m, layer, ins, outs, scr):
    dx, dx_other, da, full = ins[:4]
    ws = [ins[4 + i * m : 4 + (i + 1) * m] for i in range(2)]
    slope, prm = ins[4 + 2 * m :]
    _, gain, _ = params_of(prm, layer, 1)
    e = da[...] + (f32(dx) + f32(dx_other))
    unit, r = get_unit(full)
    feed_back(e, unit, r, gain, ws, slope, outs)


def k_attend_back(m, layer, ins, outs, scr):
    dh, dh_other, df, unit_ref = ins[:4]
    qkv, p, prm = ins[4 + m :]
    da_ref, low_ref, dx_ref, grads_ref, sums = outs
    _, gain, _ = params_of(prm, layer, 0)
    e = df[...] + (f32(dh) + f32(dh_other))
    unit, r = get_unit(unit_ref)
    da = norm_back(e, unit, r, gain)
    low = da.astype(BF16)
    da_ref[...] = da
    low_ref[...] = low
    put_sums(sums, e, unit, low)
    w = rows_of(ins[4 : 4 + m])
    grads = attend_back(low, w, qkv, p)
    grads_ref[...] = grads
    dx_ref[...] = heads_back(grads, w).astype(BF16)


def k_attend_back_last(n, m, ins, outs, scr):
    sc, dh, dh_other, df, unit_ref = ins[:5]
    qkv, p, prm = ins[5 + m :]
    low_ref, grads_ref, sums = outs[n:]
    _, gain, _ = params_of(prm, 0, 0)
    e = df[...] + (f32(dh) + f32(dh_other))
    unit, r = get_unit(unit_ref)
    da = norm_back(e, unit, r, gain)
    low = da.astype(BF16)
    low_ref[...] = low
    put_sums(sums, e, unit, low)
    w = rows_of(ins[5 : 5 + m])
    grads = attend_back(low, w, qkv, p)
    grads_ref[...] = grads
    dx = heads_back(grads, w)
    place = sc[0] ^ sc[1]
    pick_features(place, m, da + dx, outs[0])
    for k in range(1, n):
        pick_features(place ^ k, m, dx, outs[k])


def k_total(ins, outs, scr):
    outs[0][...] = ins[0][...] + ((f32(ins[1]) + f32(ins[2])) + f32(ins[3]))


def k_feed_weight(m, ins, outs, scr):
    low, g, h, du = ins
    keep, send, sums = outs
    split_blocks(t_dot(low[...], g[...]), m, 0, 2, keep, send)
    split_blocks(t_dot(h[...], du[...]), m, 1, 2, keep, send)
    sums[0:1, :] = jnp.sum(f32(du), axis=0, keepdims=True)
    sums[1:8, :] = jnp.zeros((7, sums.shape[1]), F32)


def k_attend_weight(m, ins, outs, scr):
    x, grads, low, o = ins[:4]
    keep, send, sums = outs
    first = t_dot(x[...], grads[...])
    second = t_dot(low[...], o[...])
    split_blocks(jnp.concatenate([first, second], axis=1), m, 0, 1, keep, send)
    sums[...] = jnp.zeros(sums.shape, F32)
    sums[0:1, : grads.shape[1]] = jnp.sum(f32(grads), axis=0, keepdims=True)


def k_attend_weight_last(m, ins, outs, scr):
    x, grads, low, o = ins[:4]
    hidden_sums, head_sums, norm_sums = ins[4:6], ins[6], ins[7:]
    keep, send = outs
    first = t_dot(x[...], grads[...])
    second = t_dot(low[...], o[...])
    split_blocks(jnp.concatenate([first, second], axis=1), m, 0, 1, keep, send)
    model = x.shape[1]
    piece = model // m
    width = grads.shape[1]
    own = jnp.sum(f32(grads), axis=0, keepdims=True)
    own = jnp.concatenate([own, jnp.zeros((1, model - width), F32)], axis=1)
    common = [r[0:1, :] for r in hidden_sums] + [own, head_sums[0:1, :]]
    common = jnp.concatenate(common, axis=0)
    each = jnp.concatenate([r[0:3, :] for r in norm_sums], axis=0)
    rows = keep.shape[0] // 2
    for k in range(m):
        target = send if k % 2 else keep
        start = (k // 2) * rows + piece
        block = jnp.concatenate(
            [each[:, k * piece : (k + 1) * piece], jnp.zeros((each.shape[0], model - piece), F32)],
            axis=1,
        )
        target[start : start + 16, :] = jnp.concatenate([common, block], axis=0).astype(BF16)


def k_middle(ins, outs, scr):
    keep, got = ins
    total = f32(keep) + f32(got)
    rows = outs[0].shape[0]
    for i, out in enumerate(outs):
        out[...] = total[i * rows : (i + 1) * rows].astype(BF16)


def k_add(ins, outs, scr):
    outs[0][...] = (f32(ins[0]) + f32(ins[1])).astype(outs[0].dtype)


def k_feed_outputs(ins, outs, scr):
    for i, out in enumerate(outs):
        for layer in range(2):
            at = 4 * layer + 2 * i
            out[layer] = f32(ins[at]) + f32(ins[at + 1])


def k_attend_outputs(ins, outs, scr):
    grad_w, qv, b_out, gains, shifts, b_up, b_down = outs
    piece = grad_w.shape[1]
    total = f32(ins[0]) + f32(ins[1])
    grad_w[0] = total[:piece]
    grad_w[1] = f32(ins[2]) + f32(ins[3])
    small = total[piece:]
    b_up[...] = small[0:2]
    for layer in range(2):
        heads = small[2 + layer : 3 + layer]
        qv[layer, 0:1, :] = heads[:, :piece]
        qv[layer, 1:2, :] = heads[:, 2 * piece : 3 * piece]
        at = 4 + 6 * layer
        b_out[layer : layer + 1, :] = small[at + 2 : at + 3, :piece]
        b_down[layer : layer + 1, :] = small[at + 5 : at + 6, :piece]
        for which in range(2):
            start = at + 3 * which
            gains[layer, which : which + 1, :] = small[start : start + 1, :piece]
            shifts[layer, which : which + 1, :] = small[start + 1 : start + 2, :piece]


def per_device(
    hidden_in, lengths, w_attn, b_qv, b_out, ln_gain, ln_bias, w_up, b_up, w_down, b_down, cotangent
):
    layers = w_attn.shape[0]
    n, m = lax.axis_size("row"), lax.axis_size("col")
    row, col = lax.axis_index("row"), lax.axis_index("col")
    tokens, piece = hidden_in.shape
    model = piece * m
    hidden = w_up.shape[2]
    width = w_attn.shape[2] // 4
    heads = width // HEAD_DIM
    length = lax.dynamic_index_in_dim(lengths, col, 0, keepdims=False)
    sc = jnp.stack([row, col, length]).astype(jnp.int32)

    tile = (tokens, model)

    def layer_of(array, layer):
        return (array, (1,) + array.shape[1:], (layer, 0, 0))

    def pack(rows, arrays, after=()):
        return call(k_pack, [sds((rows, hidden), BF16)], arrays, after=after, final=True)[0]

    def held(array, after):
        return pack(array.shape[0], [whole(array)], after)

    def blocks(own, along, near, rows=piece):
        views = [(own, 0), (near, 0), (along, 0), (near, 1)]
        return [(a, (rows, hidden), (i, 0)) for a, i in views]

    def near_of(own, along, after=()):
        both = pack(2 * own.shape[0], [whole(own), whole(along)], after)
        return exchange(both, "col", 1)

    def sent(array, layer, after):
        own = pack(piece, [layer_of(array, layer)], after)
        return own, exchange(own, "col", 2)

    def pair_sum(value, after=()):
        return call(k_sum, [low_tile], [value, exchange(value, "row", 1)], after=after)[0]

    def both(value):
        return [value, exchange(value, "row", 2)]

    block, rowwise, pair = call(
        k_start,
        [sds((piece + 16, hidden), BF16), sds((16, hidden), BF16), sds((2 * tokens, piece), BF16)],
        [
            layer_of(w_attn, 0),
            *map(whole, (b_out, b_down, ln_gain, ln_bias, b_up, b_qv, hidden_in, cotangent)),
        ],
    )
    along = exchange(block, "col", 2)
    x_in = [turned(pair, k) for k in range(n)]
    x, cotan = call(k_prep, [sds(tile, BF16)] * 2, [sc, *x_in])
    near = near_of(block, along, [x])
    up0, up0_along = sent(w_up, 0, [x])

    low_tile = sds(tile, BF16)
    low_block, low_tail = sds((piece, hidden), BF16), sds((piece + 16, hidden), BF16)
    unit_out = sds((tokens, model + 128), F32)
    qkv_out, p_out, o_out = (
        sds((tokens, 3 * width), BF16),
        sds((heads, tokens, tokens), F32),
        sds((tokens, width), BF16),
    )
    g_out, slope_out = sds((tokens, hidden), BF16), sds((tokens, hidden), F32)
    feed_out = [low_tile, unit_out, low_tile, g_out, slope_out]

    attn0 = blocks(block, along, near, piece + 16)
    z, prm, o0, qkv0, p0 = call(
        partial(k_attend_first, m),
        [low_tile, sds((16, model), F32), o_out, qkv_out, p_out],
        [sc, x, *attn0, rowwise],
        after=[up0_along],
    )
    down0, down0_along = sent(w_down, 0, [z])
    up0_near = near_of(up0, up0_along, [z])
    z = pair_sum(z, [down0_along, up0_near])
    down0_near = near_of(down0, down0_along, [z])
    attn1, attn1_along = sent(w_attn, 1, [z])
    up0 = blocks(up0, up0_along, up0_near)
    down0 = blocks(down0, down0_along, down0_near)
    f, unit_a0, h0, g0, slope0 = call(
        partial(k_feed, m, 0),
        feed_out,
        [*both(z), x, *up0, *down0, rowwise, prm],
        after=[attn1_along],
    )
    attn1_near = near_of(attn1, attn1_along, [f])
    attn1 = blocks(attn1, attn1_along, attn1_near)
    f = pair_sum(f, [attn1_near])
    up1, up1_along = sent(w_up, 1, [f])
    z, unit_b0, x1, o1, qkv1, p1 = call(
        partial(k_attend, m, 1),
        [low_tile, unit_out, low_tile, o_out, qkv_out, p_out],
        [sc, *both(f), unit_a0, *attn1, rowwise, prm],
        after=[up1_along],
    )
    down1, down1_along = sent(w_down, 1, [z])
    up1_near = near_of(up1, up1_along, [z])
    z = pair_sum(z, [down1_along, up1_near])
    down1_near = near_of(down1, down1_along, [z])
    up1 = blocks(up1, up1_along, up1_near)
    down1 = blocks(down1, down1_along, down1_near)
    f, unit_a1, h1, g1, slope1 = call(
        partial(k_feed, m, 1),
        feed_out,
        [*both(z), unit_b0, *up1, *down1, rowwise, prm],
    )

    sums_out = sds((8, model), F32)
    feed_back_out = [sds(tile, F32), low_tile, low_tile, sds((tokens, hidden), BF16), sums_out]
    out, df, df_low, dh, du, sums_b1 = call(
        partial(k_turn, m, 1),
        [sds((tokens, piece), BF16)] + feed_back_out,
        [sc, *both(pair_sum(f)), unit_a1, cotan, *up1, *down1, slope1, prm],
    )
    out_hidden = turned(out, 0)
    weight_out = [sds((4 * piece, hidden), BF16)] * 2 + [sds((8, hidden), F32)]
    keep, send, hidden_sums1 = call(
        partial(k_feed_weight, m), weight_out, [df_low, g1, h1, du]
    )
    got = exchange(send, "col", 1)
    dh = pair_sum(dh, [got])
    down1_stay, up1_stay, down1_go, up1_go = call(k_middle, [low_block] * 4, [keep, got], after=[dh])
    down1_more = exchange(down1_go, "col", 2)
    da, da_low, dx, grads1, sums_a1 = call(
        partial(k_attend_back, m, 1),
        [sds(tile, F32), low_tile, low_tile, qkv_out, sums_out],
        [*both(dh), df, unit_a1, *attn1, qkv1, p1, prm],
        after=[down1_more, out_hidden],
    )
    keep, send, head_sums1 = call(
        partial(k_attend_weight, m),
        [sds((2 * piece, 4 * width), BF16)] * 2 + [sums_out],
        [x1, grads1, da_low, o1],
    )
    got = exchange(send, "col", 1)
    up1_more = exchange(held(up1_go, [dx]), "col", 2)
    dx = pair_sum(dx, [got, up1_more])
    attn1_stay, attn1_go = call(k_middle, [low_block] * 2, [keep, got], after=[dx])
    attn1_more = exchange(attn1_go, "col", 2)
    (down1_low,) = call(k_add, [low_block], [down1_stay, down1_more], after=[dx])
    down1_terms = last_of_dp(down1_low)

    df, df_low, dh, du, sums_b0 = call(
        partial(k_feed_back, m, 0),
        feed_back_out,
        [*both(dx), da, unit_b0, *up0, *down0, slope0, prm],
        after=[attn1_more, down1_terms[1]],
    )
    keep, send, hidden_sums0 = call(
        partial(k_feed_weight, m), weight_out, [df_low, g0, h0, du]
    )
    got = exchange(send, "col", 1)
    (up1_low,) = call(k_add, [low_block], [up1_stay, up1_more], after=[dh])
    up1_terms = last_of_dp(up1_low)
    dh = pair_sum(dh, [got, up1_terms[1]])
    down0_stay, up0_stay, down0_go, up0_go = call(k_middle, [low_block] * 4, [keep, got], after=[dh])
    down0_more = exchange(down0_go, "col", 2)
    (attn1_low,) = call(k_add, [low_block], [attn1_stay, attn1_more], after=[dh])
    attn1_terms = last_of_dp(attn1_low)
    *dx, low_last, grads0, sums_a0 = call(
        partial(k_attend_back_last, n, m),
        [sds((tokens, piece), F32)]
        + [sds((tokens, piece), BF16)] * (n - 1)
        + [low_tile, qkv_out, sums_out],
        [sc, *both(dh), df, unit_a0, *attn0, qkv0, p0, prm],
        after=[down0_more, attn1_terms[1]],
    )
    up0_more = exchange(held(up0_go, [dx[0]]), "col", 2)
    (grad_input,) = call(
        k_total,
        [sds((tokens, piece), F32)],
        [dx[0]] + [exchange(dx[k], "row", k) for k in range(1, n)],
        after=[up0_more],
    )
    grad_input = turned(grad_input, 0)

    keep, send = call(
        partial(k_attend_weight_last, m),
        [sds((2 * (piece + 16), 4 * width), BF16)] * 2,
        [
            x,
            grads0,
            low_last,
            o0,
            hidden_sums0,
            hidden_sums1,
            head_sums1,
            sums_a0,
            sums_b0,
            sums_a1,
            sums_b1,
        ],
    )
    got = exchange(send, "col", 1)
    attn0_stay, attn0_go = call(k_middle, [low_tail] * 2, [keep, got])
    (down0_low,) = call(k_add, [low_block], [down0_stay, down0_more])
    down0_terms = last_of_dp(down0_low)
    (up0_low,) = call(k_add, [low_block], [up0_stay, up0_more])
    up0_terms = last_of_dp(up0_low)
    (attn0_low,) = call(k_add, [low_tail], [attn0_stay, exchange(attn0_go, "col", 2)])
    attn0_terms = last_of_dp(attn0_low)
    grad_down, grad_up = call(
        k_feed_outputs,
        [sds((layers, piece, hidden), F32)] * 2,
        [*down0_terms, *up0_terms, *down1_terms, *up1_terms],
        final=True,
    )
    grad_attn, grad_qv, grad_out, grad_gain, grad_shift, grad_b_up, grad_b_down = call(
        k_attend_outputs,
        [
            sds(w_attn.shape, F32),
            sds(b_qv.shape, F32),
            sds(b_out.shape, F32),
            sds(ln_gain.shape, F32),
            sds(ln_bias.shape, F32),
            sds(b_up.shape, F32),
            sds(b_down.shape, F32),
        ],
        [*attn0_terms, *attn1_terms],
        final=True,
    )
    return (
        out_hidden,
        grad_input,
        grad_attn,
        grad_qv,
        grad_out,
        grad_gain,
        grad_shift,
        grad_up,
        grad_b_up,
        grad_down,
        grad_b_down,
    )


def solution(mesh):
    in_specs = (
        P(("dp", "row"), "col"),
        P("dp"),
        P(None, "col", "row"),
        P(None, None, "row"),
        P(None, "col"),
        P(None, None, "col"),
        P(None, None, "col"),
        P(None, "col", "row"),
        P(None, "row"),
        P(None, "col", "row"),
        P(None, "col"),
        P(("dp", "row"), "col"),
    )
    out_specs = (
        P(("dp", "row"), "col"),
        P(("dp", "row"), "col"),
        P(None, "col", "row"),
        P(None, None, "row"),
        P(None, "col"),
        P(None, None, "col"),
        P(None, None, "col"),
        P(None, "col", "row"),
        P(None, "row"),
        P(None, "col", "row"),
        P(None, "col"),
    )
    return jax.shard_map(
        per_device, mesh=mesh, in_specs=in_specs, out_specs=out_specs, check_vma=False
    )
```

```python
import math
from functools import partial

import jax
import jax.numpy as jnp
from jax import lax
from jax.experimental import pallas as pl
from jax.experimental.pallas import tpu as pltpu
from jax.sharding import PartitionSpec as P


HEAD_DIM = 64
EPS = 1e-5
MASKED = -1e30
F32 = jnp.float32
BF16 = jnp.bfloat16


def exchange(x, axis, bit):
    n = lax.axis_size(axis)
    return lax.ppermute(x, axis, [(i, i ^ bit) for i in range(n)])


def turned(x):
    n = lax.axis_size("row")
    pairs = [(a * n + b, b * n + a) for a in range(n) for b in range(n)]
    return lax.ppermute(x, ("row", "col"), pairs)


def last_of_dp(low):
    bit = 1
    while 2 * bit < lax.axis_size("dp"):
        low = (low.astype(F32) + exchange(low, "dp", bit).astype(F32)).astype(BF16)
        bit *= 2
    return low, exchange(low, "dp", bit)


def sds(shape, dtype):
    return jax.ShapeDtypeStruct(shape, dtype)


def whole(array):
    return (array, array.shape, (0,) * array.ndim)


def call(kernel, outs, ins, scratch=(), after=(), final=False, vmem_mib=32):
    vmem = pl.BlockSpec(memory_space=pltpu.VMEM)
    specs, args = [], []
    moved = 0
    for item in ins:
        if isinstance(item, tuple):
            array, shape, index = item
            specs.append(pl.BlockSpec(shape, lambda i, index=index: index))
            moved += math.prod(shape) * array.dtype.itemsize
            args.append(array)
            continue
        if isinstance(item, list):
            args.append(item[0])
            specs.append(pl.BlockSpec(memory_space=pltpu.HBM))
            continue
        args.append(item)
        if item.dtype == jnp.int32:
            specs.append(pl.BlockSpec(memory_space=pltpu.SMEM))
        else:
            specs.append(vmem)
            moved += item.size * item.dtype.itemsize
    moved += sum(o.size * o.dtype.itemsize for o in outs)
    n_in, n_after, n_out = len(ins), len(after), len(outs)

    def body(*refs):
        kernel(
            refs[:n_in],
            refs[n_in + n_after : n_in + n_after + n_out],
            refs[n_in + n_after + n_out :],
        )

    return pl.pallas_call(
        body,
        grid=(1,),
        out_shape=outs,
        in_specs=specs + [pl.BlockSpec(memory_space=pl.ANY)] * n_after,
        out_specs=[
            pl.BlockSpec(o.shape, lambda i, d=len(o.shape): (0,) * d)
            if final
            else vmem
            for o in outs
        ],
        scratch_shapes=list(scratch),
        compiler_params=pltpu.CompilerParams(vmem_limit_bytes=vmem_mib * 1024 * 1024),
        cost_estimate=pl.CostEstimate(
            flops=200_000_000, bytes_accessed=moved, transcendentals=0
        ),
    )(*args, *after)


def rows_of(refs):
    rows = refs[0].shape[0] // 64 * 64
    return jnp.concatenate([r[:rows, :] for r in refs], axis=0)


def dot(a, b):
    return jnp.dot(a, b, preferred_element_type=F32)


def dot_t(a, b):
    return lax.dot_general(a, b, (((1,), (1,)), ((), ())), preferred_element_type=F32)


def t_dot(a, b):
    return lax.dot_general(a, b, (((0,), (0,)), ((), ())), preferred_element_type=F32)


def f32(ref):
    return ref[...].astype(F32)


def tree(refs):
    values = [f32(r) for r in refs]
    while len(values) > 1:
        values = [values[i] + values[i + 1] for i in range(0, len(values), 2)]
    return values[0]


def params_of(prm, layer, which):
    rows = (2 * which + layer, 4 + 2 * layer + which, 8 + 2 * layer + which)
    return [prm[i : i + 1, :] for i in rows]


def norm_of(v):
    mean = jnp.mean(v, axis=-1, keepdims=True)
    centred = v - mean
    r = lax.rsqrt(jnp.mean(centred * centred, axis=-1, keepdims=True) + EPS)
    return centred * r, r


def norm_back(e, unit, r, gain):
    c = e * gain
    return r * (
        c
        - jnp.mean(c, axis=-1, keepdims=True)
        - unit * jnp.mean(c * unit, axis=-1, keepdims=True)
    )


def put_unit(ref, unit, r):
    model = unit.shape[1]
    ref[:, :model] = unit
    ref[:, model:] = jnp.broadcast_to(r, (unit.shape[0], 128))


def get_unit(ref):
    model = ref.shape[1] - 128
    return ref[:, :model], ref[:, model : model + 1]


def put_sums(ref, e, unit, low):
    ref[0:1, :] = jnp.sum(e * unit, axis=0, keepdims=True)
    ref[1:2, :] = jnp.sum(e, axis=0, keepdims=True)
    ref[2:3, :] = jnp.sum(low.astype(F32), axis=0, keepdims=True)
    ref[3:8, :] = jnp.zeros((5, ref.shape[1]), F32)


def place_features(sc, pieces, target):
    place = sc[0] ^ sc[1]
    width = pieces[0].shape[1]
    for k, piece in enumerate(pieces):
        for j in range(len(pieces)):

            @pl.when((place ^ k) == j)
            def _():
                target[:, j * width : (j + 1) * width] = piece[...].astype(target.dtype)


def pick_features(at, count, value, target):
    width = value.shape[1] // count
    for j in range(count):

        @pl.when(at == j)
        def _():
            target[...] = value[:, j * width : (j + 1) * width].astype(target.dtype)


def project(sc, layer, x, w, rowwise, qkv_ref, p_ref):
    tokens = x.shape[0]
    width = w.shape[1] // 4
    b = rowwise[2 + layer : 3 + layer, : 2 * width].astype(F32)
    shift = jnp.concatenate([b[:, :width], jnp.zeros((1, width), F32), b[:, width:]], axis=1)
    qkv = (dot(x, w[:, : 3 * width]) + shift).astype(BF16)
    qkv_ref[...] = qkv
    visible = lax.broadcasted_iota(jnp.int32, (tokens, tokens), 1) < sc[2]
    mixed = []
    for h in range(width // HEAD_DIM):
        q = qkv[:, h * HEAD_DIM : (h + 1) * HEAD_DIM]
        k = qkv[:, width + h * HEAD_DIM : width + (h + 1) * HEAD_DIM]
        v = qkv[:, 2 * width + h * HEAD_DIM : 2 * width + (h + 1) * HEAD_DIM]
        s = jnp.where(visible, dot_t(q, k) * HEAD_DIM ** (-0.5), MASKED)
        e = jnp.exp(s - jnp.max(s, axis=-1, keepdims=True))
        p = e / jnp.sum(e, axis=-1, keepdims=True)
        p_ref[h] = p
        mixed.append(dot(p.astype(BF16), v))
    return jnp.concatenate(mixed, axis=1).astype(BF16)


def mix_out(o, w):
    return dot_t(o, w[:, 3 * (w.shape[1] // 4) :])


def attend_back(d, w, qkv_ref, p_ref):
    width = w.shape[1] // 4
    do = dot(d, w[:, 3 * width :]).astype(BF16)
    qkv = qkv_ref[...]
    dq, dk, dv = [], [], []
    for h in range(width // HEAD_DIM):
        q = qkv[:, h * HEAD_DIM : (h + 1) * HEAD_DIM]
        k = qkv[:, width + h * HEAD_DIM : width + (h + 1) * HEAD_DIM]
        v = qkv[:, 2 * width + h * HEAD_DIM : 2 * width + (h + 1) * HEAD_DIM]
        g = do[:, h * HEAD_DIM : (h + 1) * HEAD_DIM]
        p = p_ref[h]
        dv.append(t_dot(p.astype(BF16), g))
        dp = dot_t(g, v)
        ds = (p * (dp - jnp.sum(p * dp, axis=-1, keepdims=True))).astype(BF16)
        dq.append(dot(ds, k) * HEAD_DIM ** (-0.5))
        dk.append(t_dot(ds, q) * HEAD_DIM ** (-0.5))
    return jnp.concatenate(dq + dk + dv, axis=1).astype(BF16)


def heads_back(low, w):
    return dot_t(low, w[:, : 3 * (w.shape[1] // 4)])


def raise_hidden(layer, h, up, rowwise):
    u = dot(h, up) + rowwise[layer : layer + 1, :].astype(F32)
    cdf = 0.5 * (1.0 + lax.erf(u * (0.5**0.5)))
    slope = cdf + u * (jnp.exp(-0.5 * u * u) * 0.3989422804014327)
    return (u * cdf).astype(BF16), slope


def split_blocks(grad, count, part, parts, keep, send):
    block = grad.shape[0] // count
    each = keep.shape[0] // (2 * parts)
    for k in range(count):
        target = send if k % 2 else keep
        start = ((k // 2) * parts + part) * each
        target[start : start + block, :] = grad[k * block : (k + 1) * block].astype(BF16)


def k_start(ins, outs, scr):
    attn, hidden_in, small = ins[0], ins[1], scr[:-1]
    block, rowwise, x = outs
    fetched = [
        pltpu.make_async_copy(a, b, scr[-1].at[i]) for i, (a, b) in enumerate(zip(ins[2:], small))
    ]
    for copy in fetched:
        copy.start()
    rows = attn.shape[1]
    block[:rows, :] = attn[0]
    x[...] = hidden_in[...].astype(F32).T.astype(BF16)
    for copy in fetched:
        copy.wait()
    b_out, b_down, gain, shift, b_up, b_qv = small
    piece = b_out.shape[1]
    norms = [b_out[...], b_down[...], gain[0], gain[1], shift[0], shift[1]]
    norms = jnp.concatenate([x.astype(F32) for x in norms] + [jnp.zeros((4, piece), F32)], axis=0)
    block[rows:, :piece] = norms.astype(BF16)
    block[rows:, piece:] = jnp.zeros((16, block.shape[1] - piece), BF16)
    qv = [b_qv[i].astype(F32) for i in range(2)]
    qv = [jnp.concatenate([x[0:1], x[1:2]], axis=1) for x in qv]
    rest = b_up.shape[1] - qv[0].shape[1]
    qv = jnp.concatenate([jnp.concatenate(qv, axis=0), jnp.zeros((2, rest), F32)], axis=1)
    low = jnp.concatenate([b_up[...].astype(F32), qv, jnp.zeros((12, b_up.shape[1]), F32)], axis=0)
    rowwise[...] = low.astype(BF16)


def k_pack(ins, outs, scr):
    at = 0
    for ref in ins:
        value = ref[0] if len(ref.shape) == 3 else ref[...]
        outs[0][at : at + value.shape[0], :] = value
        at += value.shape[0]


def k_turned(ins, outs, scr):
    outs[0][...] = ins[0][...].astype(F32).T.astype(BF16)


def k_prep(ins, outs, scr):
    sc, *pieces = ins
    place_features(sc, pieces, outs[0])


def k_sum(ins, outs, scr):
    outs[0][...] = (f32(ins[0]) + f32(ins[1])).astype(BF16)


def k_attend_first(m, ins, outs, scr):
    sc, x = ins[:2]
    w_refs, rowwise = ins[2 : 2 + m], ins[2 + m]
    z_ref, prm, o_ref, qkv, p = outs
    piece = w_refs[0].shape[0] - 16
    prm[...] = jnp.concatenate([w[piece:, :piece].astype(F32) for w in w_refs], axis=1)
    w = rows_of(w_refs)
    o = project(sc, 0, x[...], w, rowwise, qkv, p)
    o_ref[...] = o
    z_ref[...] = mix_out(o, w).astype(BF16)


def k_feed(m, layer, ins, outs, scr):
    z, z_other, base = ins[:3]
    up, down = ins[3 : 3 + m], ins[3 + m : 3 + 2 * m]
    rowwise, prm = ins[3 + 2 * m :]
    f_ref, unit_ref, h_ref, g_ref, slope_ref = outs
    if layer:
        _, gain, shift = params_of(prm, layer - 1, 1)
        x = get_unit(base)[0] * gain + shift
    else:
        x = f32(base)
    bias, gain, shift = params_of(prm, layer, 0)
    unit, r = norm_of(x + (f32(z) + f32(z_other) + bias))
    put_unit(unit_ref, unit, r)
    h = (unit * gain + shift).astype(BF16)
    h_ref[...] = h
    g, slope = raise_hidden(layer, h, rows_of(up), rowwise)
    g_ref[...] = g
    slope_ref[...] = slope
    f_ref[...] = dot_t(g, rows_of(down)).astype(BF16)


def k_attend(m, layer, ins, outs, scr):
    sc, f, f_other, unit_ref = ins[:4]
    own = ins[4 : 4 + m]
    rowwise, prm = ins[4 + m :]
    z_ref, unit_out, x_ref, o_ref, qkv, p = outs
    _, gain, shift = params_of(prm, layer - 1, 0)
    h = get_unit(unit_ref)[0] * gain + shift
    bias, gain, shift = params_of(prm, layer - 1, 1)
    unit, r = norm_of(h + (f32(f) + f32(f_other) + bias))
    put_unit(unit_out, unit, r)
    x = (unit * gain + shift).astype(BF16)
    x_ref[...] = x
    w = rows_of(own)
    o = project(sc, layer, x, w, rowwise, qkv, p)
    o_ref[...] = o
    z_ref[...] = mix_out(o, w).astype(BF16)


def feed_back(e, unit, r, gain, ws, slope, outs):
    up, down = ws
    df_ref, low_ref, dh_ref, du_ref, sums = outs
    df = norm_back(e, unit, r, gain)
    low = df.astype(BF16)
    df_ref[...] = df
    low_ref[...] = low
    put_sums(sums, e, unit, low)
    du = (dot(low, rows_of(down)) * slope[...]).astype(BF16)
    du_ref[...] = du
    dh_ref[...] = dot_t(du, rows_of(up)).astype(BF16)


def k_turn(m, layer, ins, outs, scr):
    sc, f, f_other, unit_ref, cotan = ins[:5]
    ws = [ins[5 + i * m : 5 + (i + 1) * m] for i in range(2)]
    slope, prm = ins[5 + 2 * m :]
    _, gain, shift = params_of(prm, layer, 0)
    h = get_unit(unit_ref)[0] * gain + shift
    bias, gain, shift = params_of(prm, layer, 1)
    unit, r = norm_of(h + (f32(f) + f32(f_other) + bias))
    pick_features(sc[0] ^ sc[1], m, unit * gain + shift, scr[0])
    outs[0][...] = scr[0][...].T.astype(BF16)
    feed_back(f32(cotan), unit, r, gain, ws, slope, outs[1:])


def k_feed_back(m, layer, ins, outs, scr):
    dx, dx_other, da, full = ins[:4]
    ws = [ins[4 + i * m : 4 + (i + 1) * m] for i in range(2)]
    slope, prm = ins[4 + 2 * m :]
    _, gain, _ = params_of(prm, layer, 1)
    e = da[...] + (f32(dx) + f32(dx_other))
    unit, r = get_unit(full)
    feed_back(e, unit, r, gain, ws, slope, outs)


def k_attend_back(m, layer, ins, outs, scr):
    dh, dh_other, df, unit_ref = ins[:4]
    qkv, p, prm = ins[4 + m :]
    da_ref, low_ref, dx_ref, grads_ref, sums = outs
    _, gain, _ = params_of(prm, layer, 0)
    e = df[...] + (f32(dh) + f32(dh_other))
    unit, r = get_unit(unit_ref)
    da = norm_back(e, unit, r, gain)
    low = da.astype(BF16)
    da_ref[...] = da
    low_ref[...] = low
    put_sums(sums, e, unit, low)
    w = rows_of(ins[4 : 4 + m])
    grads = attend_back(low, w, qkv, p)
    grads_ref[...] = grads
    dx_ref[...] = heads_back(grads, w).astype(BF16)


def k_attend_back_last(n, m, ins, outs, scr):
    sc, dh, dh_other, df, unit_ref = ins[:5]
    qkv, p, prm = ins[5 + m :]
    low_ref, grads_ref, sums = outs[n:]
    _, gain, _ = params_of(prm, 0, 0)
    e = df[...] + (f32(dh) + f32(dh_other))
    unit, r = get_unit(unit_ref)
    da = norm_back(e, unit, r, gain)
    low = da.astype(BF16)
    low_ref[...] = low
    put_sums(sums, e, unit, low)
    w = rows_of(ins[5 : 5 + m])
    grads = attend_back(low, w, qkv, p)
    grads_ref[...] = grads
    dx = heads_back(grads, w)
    place = sc[0] ^ sc[1]
    pick_features(place, m, da + dx, outs[0])
    for k in range(1, n):
        pick_features(place ^ k, m, dx, outs[k])


def k_total(ins, outs, scr):
    outs[0][...] = (ins[0][...] + ((f32(ins[1]) + f32(ins[2])) + f32(ins[3]))).T


def k_feed_weight(m, ins, outs, scr):
    low, g, h, du = ins
    keep, send, sums = outs
    split_blocks(t_dot(low[...], g[...]), m, 0, 2, keep, send)
    split_blocks(t_dot(h[...], du[...]), m, 1, 2, keep, send)
    sums[0:1, :] = jnp.sum(f32(du), axis=0, keepdims=True)
    sums[1:8, :] = jnp.zeros((7, sums.shape[1]), F32)


def k_attend_weight(m, ins, outs, scr):
    x, grads, low, o = ins[:4]
    keep, send, sums = outs
    first = t_dot(x[...], grads[...])
    second = t_dot(low[...], o[...])
    split_blocks(jnp.concatenate([first, second], axis=1), m, 0, 1, keep, send)
    sums[...] = jnp.zeros(sums.shape, F32)
    sums[0:1, : grads.shape[1]] = jnp.sum(f32(grads), axis=0, keepdims=True)


def k_attend_weight_last(m, ins, outs, scr):
    x, grads, low, o = ins[:4]
    hidden_sums, head_sums, norm_sums = ins[4:6], ins[6], ins[7:]
    keep, send = outs
    first = t_dot(x[...], grads[...])
    second = t_dot(low[...], o[...])
    split_blocks(jnp.concatenate([first, second], axis=1), m, 0, 1, keep, send)
    model = x.shape[1]
    piece = model // m
    width = grads.shape[1]
    own = jnp.sum(f32(grads), axis=0, keepdims=True)
    own = jnp.concatenate([own, jnp.zeros((1, model - width), F32)], axis=1)
    common = [r[0:1, :] for r in hidden_sums] + [own, head_sums[0:1, :]]
    common = jnp.concatenate(common, axis=0)
    each = jnp.concatenate([r[0:3, :] for r in norm_sums], axis=0)
    rows = keep.shape[0] // 2
    for k in range(m):
        target = send if k % 2 else keep
        start = (k // 2) * rows + piece
        block = jnp.concatenate(
            [each[:, k * piece : (k + 1) * piece], jnp.zeros((each.shape[0], model - piece), F32)],
            axis=1,
        )
        target[start : start + 16, :] = jnp.concatenate([common, block], axis=0).astype(BF16)


def k_middle(ins, outs, scr):
    keep, got = ins
    total = f32(keep) + f32(got)
    at = 0
    for out in outs:
        out[...] = total[at : at + out.shape[0]].astype(BF16)
        at += out.shape[0]


def k_add(ins, outs, scr):
    count = len(ins) // 2
    at = 0
    for first, second in zip(ins[:count], ins[count:]):
        rows = first.shape[0]
        outs[0][at : at + rows, :] = (f32(first) + f32(second)).astype(BF16)
        at += rows


def k_feed_outputs(ins, outs, scr):
    half = ins[0].shape[0]
    for layer in range(2):
        for i, out in enumerate(outs):
            for j in range(2):
                at = 4 * layer + 2 * i + j
                out[layer, j * half : (j + 1) * half, :] = f32(ins[at]) + f32(ins[8 + at])


def k_attend_outputs(ins, outs, scr):
    grad_w, qv, b_out, gains, shifts, b_up, b_down = outs
    piece = grad_w.shape[1]
    total = f32(ins[0]) + f32(ins[1])
    grad_w[0] = total[:piece]
    half = piece // 2
    grad_w[1, :half, :] = f32(ins[2]) + f32(ins[4])
    grad_w[1, half:, :] = f32(ins[3]) + f32(ins[5])
    small = total[piece:]
    b_up[...] = small[0:2]
    for layer in range(2):
        heads = small[2 + layer : 3 + layer]
        qv[layer, 0:1, :] = heads[:, :piece]
        qv[layer, 1:2, :] = heads[:, 2 * piece : 3 * piece]
        at = 4 + 6 * layer
        b_out[layer : layer + 1, :] = small[at + 2 : at + 3, :piece]
        b_down[layer : layer + 1, :] = small[at + 5 : at + 6, :piece]
        for which in range(2):
            start = at + 3 * which
            gains[layer, which : which + 1, :] = small[start : start + 1, :piece]
            shifts[layer, which : which + 1, :] = small[start + 1 : start + 2, :piece]


def per_device(
    hidden_in, lengths, w_attn, b_qv, b_out, ln_gain, ln_bias, w_up, b_up, w_down, b_down, cotangent
):
    layers = w_attn.shape[0]
    n, m = lax.axis_size("row"), lax.axis_size("col")
    row, col = lax.axis_index("row"), lax.axis_index("col")
    tokens, piece = hidden_in.shape
    model = piece * m
    hidden = w_up.shape[2]
    width = w_attn.shape[2] // 4
    heads = width // HEAD_DIM
    length = lax.dynamic_index_in_dim(lengths, col, 0, keepdims=False)
    sc = jnp.stack([row, col, length]).astype(jnp.int32)

    tile = (tokens, model)

    def layer_of(array, layer):
        return (array, (1,) + array.shape[1:], (layer, 0, 0))

    half_block = sds((piece // 2, hidden), BF16)

    def pack(rows, arrays, after=()):
        return call(k_pack, [sds((rows, hidden), BF16)], arrays, after=after, final=True)[0]

    def held(arrays, after):
        return [
            call(k_pack, [sds(a.shape, a.dtype)], [whole(a)], after=after, final=True)[0]
            for a in arrays
        ]

    def along_of(arrays):
        return [exchange(a, "col", 2) for a in arrays]

    def half_of(array, layer, which, after):
        view = (array, (1, piece // 2, hidden), (layer, which, 0))
        return pack(piece // 2, [view], after)

    def gathered(own, along, rows=piece, after=()):
        both = pack(2 * rows, [whole(a) for a in [*own, *along]], after)
        near = exchange(both, "col", 1)
        views = [(both, 0), (near, 0), (both, 1), (near, 1)]
        return [(a, (rows, hidden), (i, 0)) for a, i in views]

    def pair_sum(value, after=()):
        return call(k_sum, [low_tile], [value, exchange(value, "row", 1)], after=after)[0]

    def both(value):
        return [value, exchange(value, "row", 2)]

    smalls = [b_out, b_down, ln_gain, ln_bias, b_up, b_qv]
    block, rowwise, mine = call(
        k_start,
        [sds((piece + 16, hidden), BF16), sds((16, hidden), BF16), sds((tokens, piece), BF16)],
        [layer_of(w_attn, 0), whole(hidden_in.T), *[[a] for a in smalls]],
        [pltpu.VMEM(a.shape, a.dtype) for a in smalls] + [pltpu.SemaphoreType.DMA((6,))],
        final=True,
        vmem_mib=60,
    )
    along = exchange(block, "col", 2)
    mine = turned(mine)
    x_in = [mine] + [exchange(mine, "row", k) for k in range(1, n)]
    (x,) = call(k_prep, [sds(tile, BF16)], [sc, *x_in])
    up0 = pack(piece, [layer_of(w_up, 0)], [mine])
    (up0_along,) = along_of([up0])
    attn0 = gathered([block], [along], piece + 16, [*x_in[1:], up0_along])

    low_tile = sds(tile, BF16)
    unit_out = sds((tokens, model + 128), F32)
    qkv_out, p_out, o_out = (
        sds((tokens, 3 * width), BF16),
        sds((heads, tokens, tokens), F32),
        sds((tokens, width), BF16),
    )
    g_out, slope_out = sds((tokens, hidden), BF16), sds((tokens, hidden), F32)
    feed_out = [low_tile, unit_out, low_tile, g_out, slope_out]

    z, prm, o0, qkv0, p0 = call(
        partial(k_attend_first, m),
        [low_tile, sds((16, model), F32), o_out, qkv_out, p_out],
        [sc, x, *attn0, rowwise],
    )
    down0 = [half_of(w_down, 0, i, [z]) for i in range(2)]
    down0_along = along_of(down0)
    z = pair_sum(z, down0_along)
    up0 = gathered([up0], [up0_along], after=[z])
    down0 = gathered(down0, down0_along, after=[z])
    attn1 = [half_of(w_attn, 1, i, [z]) for i in range(2)]
    attn1_along = along_of(attn1)
    f, unit_a0, h0, g0, slope0 = call(
        partial(k_feed, m, 0),
        feed_out,
        [*both(z), x, *up0, *down0, rowwise, prm],
        after=attn1_along,
    )
    attn1 = gathered(attn1, attn1_along, after=[f])
    up1 = [half_of(w_up, 1, 0, [f])]
    up1_along = along_of(up1)
    f = pair_sum(f, [attn1[1][0], *up1_along])
    up1 += [half_of(w_up, 1, 1, [f])]
    up1_along += along_of(up1[1:])
    down1 = [half_of(w_down, 1, 0, [f])]
    down1_along = along_of(down1)
    z, unit_b0, x1, o1, qkv1, p1 = call(
        partial(k_attend, m, 1),
        [low_tile, unit_out, low_tile, o_out, qkv_out, p_out],
        [sc, *both(f), unit_a0, *attn1, rowwise, prm],
        after=[up1_along[1], *down1_along],
    )
    down1 += [half_of(w_down, 1, 1, [z])]
    down1_along += along_of(down1[1:])
    up1 = gathered(up1, up1_along, after=[z])
    z = pair_sum(z, [down1_along[1], up1[1][0]])
    down1 = gathered(down1, down1_along, after=[z])
    (low,) = call(k_turned, [sds((tokens, piece), BF16)], [whole(cotangent.T)], after=[z], final=True)
    cotan = turned(low)
    f, unit_a1, h1, g1, slope1 = call(
        partial(k_feed, m, 1),
        feed_out,
        [*both(z), unit_b0, *up1, *down1, rowwise, prm],
        after=[cotan],
    )
    cotan = [cotan, *held([cotan], [f])]
    cotan = [cotan[0]] + [exchange(cotan[1], "row", k) for k in range(1, n)]
    f = pair_sum(f, cotan[1:])
    (cotan,) = call(k_prep, [sds(tile, BF16)], [sc, *cotan], after=[f])

    sums_out = sds((8, model), F32)
    feed_back_out = [sds(tile, F32), low_tile, low_tile, sds((tokens, hidden), BF16), sums_out]
    out, df, df_low, dh, du, sums_b1 = call(
        partial(k_turn, m, 1),
        [sds((piece, tokens), BF16)] + feed_back_out,
        [sc, *both(f), unit_a1, cotan, *up1, *down1, slope1, prm],
        [pltpu.VMEM((tokens, piece), F32)],
    )
    out_hidden = turned(out)
    weight_out = [sds((4 * piece, hidden), BF16)] * 2 + [sds((8, hidden), F32)]
    keep, send, hidden_sums1 = call(
        partial(k_feed_weight, m), weight_out, [df_low, g1, h1, du]
    )
    got = exchange(send, "col", 1)
    dh = pair_sum(dh, [got])
    stay1 = call(k_middle, [half_block] * 8, [keep, got], after=[dh])
    more1 = along_of(stay1[4:6])
    da, da_low, dx, grads1, sums_a1 = call(
        partial(k_attend_back, m, 1),
        [sds(tile, F32), low_tile, low_tile, qkv_out, sums_out],
        [*both(dh), df, unit_a1, *attn1, qkv1, p1, prm],
        after=more1,
    )
    keep, send, head_sums1 = call(
        partial(k_attend_weight, m),
        [sds((2 * piece, 4 * width), BF16)] * 2 + [sums_out],
        [x1, grads1, da_low, o1],
    )
    got = exchange(send, "col", 1)
    more1 += along_of(held(stay1[6:7], [dx]))
    (low,) = call(k_add, [half_block], [stay1[0], more1[0]], after=[dx])
    terms1 = [last_of_dp(low)]
    dx = pair_sum(dx, [got, more1[2], terms1[0][1]])
    (out_hidden,) = held([out_hidden], [dx])
    attn1_stay = call(k_middle, [half_block] * 4, [keep, got], after=[dx])
    more1 += along_of(held(stay1[7:], [dx]))
    attn1_more = along_of(attn1_stay[2:3])
    for i in (1, 2):
        (low,) = call(k_add, [half_block], [stay1[i], more1[i]], after=[dx])
        terms1 += [last_of_dp(low)]

    df, df_low, dh, du, sums_b0 = call(
        partial(k_feed_back, m, 0),
        feed_back_out,
        [*both(dx), da, unit_b0, *up0, *down0, slope0, prm],
        after=[more1[3], *attn1_more, terms1[1][1], terms1[2][1], out_hidden],
    )
    keep, send, hidden_sums0 = call(
        partial(k_feed_weight, m), weight_out, [df_low, g0, h0, du]
    )
    got = exchange(send, "col", 1)
    attn1_more += along_of(held(attn1_stay[3:], [dh]))
    (low,) = call(k_add, [half_block], [stay1[3], more1[3]], after=[dh])
    terms1 += [last_of_dp(low)]
    (low,) = call(k_add, [half_block], [attn1_stay[0], attn1_more[0]], after=[dh])
    attn1_terms = [last_of_dp(low)]
    dh = pair_sum(dh, [got, attn1_more[1], terms1[3][1], attn1_terms[0][1]])
    stay0 = call(k_middle, [half_block] * 8, [keep, got], after=[dh])
    more0 = along_of(stay0[4:7])
    (low,) = call(k_add, [half_block], [attn1_stay[1], attn1_more[1]], after=[dh])
    attn1_terms += [last_of_dp(low)]
    *dx, low_last, grads0, sums_a0 = call(
        partial(k_attend_back_last, n, m),
        [sds((tokens, piece), F32)]
        + [sds((tokens, piece), BF16)] * (n - 1)
        + [low_tile, qkv_out, sums_out],
        [sc, *both(dh), df, unit_a0, *attn0, qkv0, p0, prm],
        after=[*more0, attn1_terms[1][1]],
    )
    more0 += along_of(held(stay0[7:], [dx[0]]))
    most = [sds((3 * piece // 2, hidden), BF16)]
    (low,) = call(k_add, most, [*stay0[:3], *more0[:3]])
    most0_terms = last_of_dp(low)
    (grad_total,) = call(
        k_total,
        [sds((piece, tokens), F32)],
        [dx[0]] + [exchange(dx[k], "row", k) for k in range(1, n)],
    )
    grad_input = turned(grad_total)

    keep, send = call(
        partial(k_attend_weight_last, m),
        [sds((2 * (piece + 16), 4 * width), BF16)] * 2,
        [
            x,
            grads0,
            low_last,
            o0,
            hidden_sums0,
            hidden_sums1,
            head_sums1,
            sums_a0,
            sums_b0,
            sums_a1,
            sums_b1,
        ],
    )
    got = exchange(send, "col", 1)
    low_tail = sds((piece + 16, hidden), BF16)
    attn0_stay, attn0_go = call(k_middle, [low_tail] * 2, [keep, got])
    (attn0_more,) = along_of([attn0_go])
    (low,) = call(k_add, [half_block], [stay0[3], more0[3]], after=[grad_total])
    rest0_terms = last_of_dp(low)
    (low,) = call(k_add, [low_tail], [attn0_stay, attn0_more])
    attn0_terms = [last_of_dp(low)]
    def halves_of(array):
        return [(array, (piece // 2, hidden), (i, 0)) for i in range(3)]

    first = [halves_of(a) + [b] for a, b in zip(most0_terms, rest0_terms)]
    second = [[t[side] for t in terms1] for side in range(2)]
    grad_down, grad_up = call(
        k_feed_outputs,
        [sds((layers, piece, hidden), F32)] * 2,
        [*first[0], *second[0], *first[1], *second[1]],
        after=[grad_input],
        final=True,
    )
    grad_attn, grad_qv, grad_out, grad_gain, grad_shift, grad_b_up, grad_b_down = call(
        k_attend_outputs,
        [
            sds(w_attn.shape, F32),
            sds(b_qv.shape, F32),
            sds(b_out.shape, F32),
            sds(ln_gain.shape, F32),
            sds(ln_bias.shape, F32),
            sds(b_up.shape, F32),
            sds(b_down.shape, F32),
        ],
        [t[side] for terms in (attn0_terms, attn1_terms) for side in range(2) for t in terms],
        final=True,
    )
    return (
        out_hidden.T,
        grad_input.T,
        grad_attn,
        grad_qv,
        grad_out,
        grad_gain,
        grad_shift,
        grad_up,
        grad_b_up,
        grad_down,
        grad_b_down,
    )


def solution(mesh):
    in_specs = (
        P(("dp", "row"), "col"),
        P("dp"),
        P(None, "col", "row"),
        P(None, None, "row"),
        P(None, "col"),
        P(None, None, "col"),
        P(None, None, "col"),
        P(None, "col", "row"),
        P(None, "row"),
        P(None, "col", "row"),
        P(None, "col"),
        P(("dp", "row"), "col"),
    )
    out_specs = (
        P(("dp", "row"), "col"),
        P(("dp", "row"), "col"),
        P(None, "col", "row"),
        P(None, None, "row"),
        P(None, "col"),
        P(None, None, "col"),
        P(None, None, "col"),
        P(None, "col", "row"),
        P(None, "row"),
        P(None, "col", "row"),
        P(None, "col"),
    )
    return jax.shard_map(
        per_device, mesh=mesh, in_specs=in_specs, out_specs=out_specs, check_vma=False
    )
```

```python
import math
from functools import partial

import jax
import jax.numpy as jnp
from jax import lax
from jax.experimental import pallas as pl
from jax.experimental.pallas import tpu as pltpu
from jax.sharding import PartitionSpec as P


HEAD_DIM = 64
EPS = 1e-5
MASKED = -1e30
F32 = jnp.float32
BF16 = jnp.bfloat16


def exchange(x, axis, bit):
    n = lax.axis_size(axis)
    return lax.ppermute(x, axis, [(i, i ^ bit) for i in range(n)])


def turned(x):
    n = lax.axis_size("row")
    pairs = [(a * n + b, b * n + a) for a in range(n) for b in range(n)]
    return lax.ppermute(x, ("row", "col"), pairs)


def last_of_dp(low):
    bit = 1
    while 2 * bit < lax.axis_size("dp"):
        low = (low.astype(F32) + exchange(low, "dp", bit).astype(F32)).astype(BF16)
        bit *= 2
    return low, exchange(low, "dp", bit)


def sds(shape, dtype):
    return jax.ShapeDtypeStruct(shape, dtype)


def whole(array):
    return (array, array.shape, (0,) * array.ndim)


def call(kernel, outs, ins, scratch=(), after=(), final=False, vmem_mib=32):
    vmem = pl.BlockSpec(memory_space=pltpu.VMEM)
    specs, args = [], []
    moved = 0
    for item in ins:
        if isinstance(item, tuple):
            array, shape, index = item
            specs.append(pl.BlockSpec(shape, lambda i, index=index: index))
            moved += math.prod(shape) * array.dtype.itemsize
            args.append(array)
            continue
        if isinstance(item, list):
            args.append(item[0])
            specs.append(pl.BlockSpec(memory_space=pltpu.HBM))
            continue
        args.append(item)
        if item.dtype == jnp.int32:
            specs.append(pl.BlockSpec(memory_space=pltpu.SMEM))
        else:
            specs.append(vmem)
            moved += item.size * item.dtype.itemsize
    moved += sum(o.size * o.dtype.itemsize for o in outs)
    n_in, n_after, n_out = len(ins), len(after), len(outs)

    def body(*refs):
        inputs = list(refs[:n_in])
        if args[0].dtype == jnp.int32:
            col = lax.axis_index("col")
            inputs[0] = (lax.axis_index("row"), col, refs[0][col])
        kernel(
            inputs,
            refs[n_in + n_after : n_in + n_after + n_out],
            refs[n_in + n_after + n_out :],
        )

    return pl.pallas_call(
        body,
        grid=(1,),
        out_shape=outs,
        in_specs=specs + [pl.BlockSpec(memory_space=pl.ANY)] * n_after,
        out_specs=[
            pl.BlockSpec(o.shape, lambda i, d=len(o.shape): (0,) * d)
            if final
            else vmem
            for o in outs
        ],
        scratch_shapes=list(scratch),
        compiler_params=pltpu.CompilerParams(vmem_limit_bytes=vmem_mib * 1024 * 1024),
        cost_estimate=pl.CostEstimate(
            flops=200_000_000, bytes_accessed=moved, transcendentals=0
        ),
    )(*args, *after)


def rows_of(refs):
    rows = refs[0].shape[0] // 64 * 64
    return jnp.concatenate([r[:rows, :] for r in refs], axis=0)


def dot(a, b):
    return jnp.dot(a, b, preferred_element_type=F32)


def dot_t(a, b):
    return lax.dot_general(a, b, (((1,), (1,)), ((), ())), preferred_element_type=F32)


def t_dot(a, b):
    return lax.dot_general(a, b, (((0,), (0,)), ((), ())), preferred_element_type=F32)


def f32(ref):
    return ref[...].astype(F32)


def tree(refs):
    values = [f32(r) for r in refs]
    while len(values) > 1:
        values = [values[i] + values[i + 1] for i in range(0, len(values), 2)]
    return values[0]


def params_of(prm, layer, which):
    rows = (2 * which + layer, 4 + 2 * layer + which, 8 + 2 * layer + which)
    return [prm[i : i + 1, :] for i in rows]


def norm_of(v):
    mean = jnp.mean(v, axis=-1, keepdims=True)
    centred = v - mean
    r = lax.rsqrt(jnp.mean(centred * centred, axis=-1, keepdims=True) + EPS)
    return centred * r, r


def norm_back(e, unit, r, gain):
    c = e * gain
    return r * (
        c
        - jnp.mean(c, axis=-1, keepdims=True)
        - unit * jnp.mean(c * unit, axis=-1, keepdims=True)
    )


def put_unit(ref, unit, r):
    model = unit.shape[1]
    ref[:, :model] = unit
    ref[:, model:] = jnp.broadcast_to(r, (unit.shape[0], 128))


def get_unit(ref):
    model = ref.shape[1] - 128
    return ref[:, :model], ref[:, model : model + 1]


def put_sums(ref, e, unit, low):
    ref[0:1, :] = jnp.sum(e * unit, axis=0, keepdims=True)
    ref[1:2, :] = jnp.sum(e, axis=0, keepdims=True)
    ref[2:3, :] = jnp.sum(low.astype(F32), axis=0, keepdims=True)
    ref[3:8, :] = jnp.zeros((5, ref.shape[1]), F32)


def place_features(sc, pieces, target):
    place = sc[0] ^ sc[1]
    width = pieces[0].shape[1]
    for k, piece in enumerate(pieces):
        for j in range(len(pieces)):

            @pl.when((place ^ k) == j)
            def _():
                target[:, j * width : (j + 1) * width] = piece[...].astype(target.dtype)


def pick_features(at, count, value, target):
    width = value.shape[1] // count
    for j in range(count):

        @pl.when(at == j)
        def _():
            target[...] = value[:, j * width : (j + 1) * width].astype(target.dtype)


def project(sc, layer, x, w, rowwise, qkv_ref, p_ref):
    tokens = x.shape[0]
    width = w.shape[1] // 4
    b = rowwise[2 + layer : 3 + layer, : 2 * width].astype(F32)
    shift = jnp.concatenate([b[:, :width], jnp.zeros((1, width), F32), b[:, width:]], axis=1)
    qkv = (dot(x, w[:, : 3 * width]) + shift).astype(BF16)
    qkv_ref[...] = qkv
    visible = lax.broadcasted_iota(jnp.int32, (tokens, tokens), 1) < sc[2]
    mixed = []
    for h in range(width // HEAD_DIM):
        q = qkv[:, h * HEAD_DIM : (h + 1) * HEAD_DIM]
        k = qkv[:, width + h * HEAD_DIM : width + (h + 1) * HEAD_DIM]
        v = qkv[:, 2 * width + h * HEAD_DIM : 2 * width + (h + 1) * HEAD_DIM]
        s = jnp.where(visible, dot_t(q, k) * HEAD_DIM ** (-0.5), MASKED)
        e = jnp.exp(s - jnp.max(s, axis=-1, keepdims=True))
        p = e / jnp.sum(e, axis=-1, keepdims=True)
        p_ref[h] = p
        mixed.append(dot(p.astype(BF16), v))
    return jnp.concatenate(mixed, axis=1).astype(BF16)


def mix_out(o, w):
    return dot_t(o, w[:, 3 * (w.shape[1] // 4) :])


def attend_back(d, w, qkv_ref, p_ref):
    width = w.shape[1] // 4
    do = dot(d, w[:, 3 * width :]).astype(BF16)
    qkv = qkv_ref[...]
    dq, dk, dv = [], [], []
    for h in range(width // HEAD_DIM):
        q = qkv[:, h * HEAD_DIM : (h + 1) * HEAD_DIM]
        k = qkv[:, width + h * HEAD_DIM : width + (h + 1) * HEAD_DIM]
        v = qkv[:, 2 * width + h * HEAD_DIM : 2 * width + (h + 1) * HEAD_DIM]
        g = do[:, h * HEAD_DIM : (h + 1) * HEAD_DIM]
        p = p_ref[h]
        dv.append(t_dot(p.astype(BF16), g))
        dp = dot_t(g, v)
        ds = (p * (dp - jnp.sum(p * dp, axis=-1, keepdims=True))).astype(BF16)
        dq.append(dot(ds, k) * HEAD_DIM ** (-0.5))
        dk.append(t_dot(ds, q) * HEAD_DIM ** (-0.5))
    return jnp.concatenate(dq + dk + dv, axis=1).astype(BF16)


def heads_back(low, w):
    return dot_t(low, w[:, : 3 * (w.shape[1] // 4)])


def raise_hidden(layer, h, up, rowwise):
    u = dot(h, up) + rowwise[layer : layer + 1, :].astype(F32)
    cdf = 0.5 * (1.0 + lax.erf(u * (0.5**0.5)))
    slope = cdf + u * (jnp.exp(-0.5 * u * u) * 0.3989422804014327)
    return (u * cdf).astype(BF16), slope


def split_blocks(grad, count, part, parts, keep, send):
    block = grad.shape[0] // count
    each = keep.shape[0] // (2 * parts)
    for k in range(count):
        target = send if k % 2 else keep
        start = ((k // 2) * parts + part) * each
        target[start : start + block, :] = grad[k * block : (k + 1) * block].astype(BF16)


def k_start(ins, outs, scr):
    attn, hidden_in, small = ins[0], ins[1], scr[:-1]
    block, rowwise, x = outs
    fetched = [
        pltpu.make_async_copy(a, b, scr[-1].at[i]) for i, (a, b) in enumerate(zip(ins[2:], small))
    ]
    for copy in fetched:
        copy.start()
    rows = attn.shape[1]
    block[:rows, :] = attn[0]
    x[...] = hidden_in[...].astype(F32).T.astype(BF16)
    for copy in fetched:
        copy.wait()
    b_out, b_down, gain, shift, b_up, b_qv = small
    piece = b_out.shape[1]
    norms = [b_out[...], b_down[...], gain[0], gain[1], shift[0], shift[1]]
    norms = jnp.concatenate([x.astype(F32) for x in norms] + [jnp.zeros((4, piece), F32)], axis=0)
    block[rows:, :piece] = norms.astype(BF16)
    block[rows:, piece:] = jnp.zeros((16, block.shape[1] - piece), BF16)
    qv = [b_qv[i].astype(F32) for i in range(2)]
    qv = [jnp.concatenate([x[0:1], x[1:2]], axis=1) for x in qv]
    rest = b_up.shape[1] - qv[0].shape[1]
    qv = jnp.concatenate([jnp.concatenate(qv, axis=0), jnp.zeros((2, rest), F32)], axis=1)
    low = jnp.concatenate([b_up[...].astype(F32), qv, jnp.zeros((12, b_up.shape[1]), F32)], axis=0)
    rowwise[...] = low.astype(BF16)


def k_split(ins, outs, scr):
    attn, up, down = ins
    half = outs[0].shape[0]
    for i, (ref, layer) in enumerate(((down, 0), (attn, 1), (up, 1), (down, 1))):
        for j in range(2):
            outs[2 * i + j][...] = ref[layer, j * half : (j + 1) * half, :]


def k_pack(ins, outs, scr):
    at = 0
    for ref in ins:
        value = ref[0] if len(ref.shape) == 3 else ref[...]
        outs[0][at : at + value.shape[0], :] = value
        at += value.shape[0]


def k_turned(ins, outs, scr):
    outs[0][...] = ins[0][...].astype(F32).T.astype(BF16)


def k_prep(ins, outs, scr):
    sc, *pieces = ins
    place_features(sc, pieces, outs[0])


def k_sum(ins, outs, scr):
    outs[0][...] = (f32(ins[0]) + f32(ins[1])).astype(BF16)


def k_attend_first(m, ins, outs, scr):
    sc, x = ins[:2]
    w_refs, rowwise = ins[2 : 2 + m], ins[2 + m]
    z_ref, prm, o_ref, qkv, p = outs
    piece = w_refs[0].shape[0] - 16
    prm[...] = jnp.concatenate([w[piece:, :piece].astype(F32) for w in w_refs], axis=1)
    w = rows_of(w_refs)
    o = project(sc, 0, x[...], w, rowwise, qkv, p)
    o_ref[...] = o
    z_ref[...] = mix_out(o, w).astype(BF16)


def k_feed(m, layer, ins, outs, scr):
    z, z_other, base = ins[:3]
    up, down = ins[3 : 3 + m], ins[3 + m : 3 + 2 * m]
    rowwise, prm = ins[3 + 2 * m :]
    f_ref, unit_ref, h_ref, g_ref, slope_ref = outs
    if layer:
        _, gain, shift = params_of(prm, layer - 1, 1)
        x = get_unit(base)[0] * gain + shift
    else:
        x = f32(base)
    bias, gain, shift = params_of(prm, layer, 0)
    unit, r = norm_of(x + (f32(z) + f32(z_other) + bias))
    put_unit(unit_ref, unit, r)
    h = (unit * gain + shift).astype(BF16)
    h_ref[...] = h
    g, slope = raise_hidden(layer, h, rows_of(up), rowwise)
    g_ref[...] = g
    slope_ref[...] = slope
    f_ref[...] = dot_t(g, rows_of(down)).astype(BF16)


def k_attend(m, layer, ins, outs, scr):
    sc, f, f_other, unit_ref = ins[:4]
    own = ins[4 : 4 + m]
    rowwise, prm = ins[4 + m :]
    z_ref, unit_out, x_ref, o_ref, qkv, p = outs
    _, gain, shift = params_of(prm, layer - 1, 0)
    h = get_unit(unit_ref)[0] * gain + shift
    bias, gain, shift = params_of(prm, layer - 1, 1)
    unit, r = norm_of(h + (f32(f) + f32(f_other) + bias))
    put_unit(unit_out, unit, r)
    x = (unit * gain + shift).astype(BF16)
    x_ref[...] = x
    w = rows_of(own)
    o = project(sc, layer, x, w, rowwise, qkv, p)
    o_ref[...] = o
    z_ref[...] = mix_out(o, w).astype(BF16)


def feed_back(e, unit, r, gain, ws, slope, outs):
    up, down = ws
    df_ref, low_ref, dh_ref, du_ref, sums = outs
    df = norm_back(e, unit, r, gain)
    low = df.astype(BF16)
    df_ref[...] = df
    low_ref[...] = low
    put_sums(sums, e, unit, low)
    du = (dot(low, rows_of(down)) * slope[...]).astype(BF16)
    du_ref[...] = du
    dh_ref[...] = dot_t(du, rows_of(up)).astype(BF16)


def k_turn(m, layer, ins, outs, scr):
    sc, f, f_other, unit_ref, cotan = ins[:5]
    ws = [ins[5 + i * m : 5 + (i + 1) * m] for i in range(2)]
    slope, prm = ins[5 + 2 * m :]
    _, gain, shift = params_of(prm, layer, 0)
    h = get_unit(unit_ref)[0] * gain + shift
    bias, gain, shift = params_of(prm, layer, 1)
    unit, r = norm_of(h + (f32(f) + f32(f_other) + bias))
    pick_features(sc[0] ^ sc[1], m, unit * gain + shift, scr[0])
    outs[0][...] = scr[0][...].T.astype(BF16)
    feed_back(f32(cotan), unit, r, gain, ws, slope, outs[1:])


def k_feed_back(m, layer, ins, outs, scr):
    dx, dx_other, da, full = ins[:4]
    ws = [ins[4 + i * m : 4 + (i + 1) * m] for i in range(2)]
    slope, prm = ins[4 + 2 * m :]
    _, gain, _ = params_of(prm, layer, 1)
    e = da[...] + (f32(dx) + f32(dx_other))
    unit, r = get_unit(full)
    feed_back(e, unit, r, gain, ws, slope, outs)


def k_attend_back(m, layer, ins, outs, scr):
    dh, dh_other, df, unit_ref = ins[:4]
    qkv, p, prm = ins[4 + m :]
    da_ref, low_ref, dx_ref, grads_ref, sums = outs
    _, gain, _ = params_of(prm, layer, 0)
    e = df[...] + (f32(dh) + f32(dh_other))
    unit, r = get_unit(unit_ref)
    da = norm_back(e, unit, r, gain)
    low = da.astype(BF16)
    da_ref[...] = da
    low_ref[...] = low
    put_sums(sums, e, unit, low)
    w = rows_of(ins[4 : 4 + m])
    grads = attend_back(low, w, qkv, p)
    grads_ref[...] = grads
    dx_ref[...] = heads_back(grads, w).astype(BF16)


def k_attend_back_last(n, m, ins, outs, scr):
    sc, dh, dh_other, df, unit_ref = ins[:5]
    qkv, p, prm = ins[5 + m :]
    low_ref, grads_ref, sums = outs[n:]
    _, gain, _ = params_of(prm, 0, 0)
    e = df[...] + (f32(dh) + f32(dh_other))
    unit, r = get_unit(unit_ref)
    da = norm_back(e, unit, r, gain)
    low = da.astype(BF16)
    low_ref[...] = low
    put_sums(sums, e, unit, low)
    w = rows_of(ins[5 : 5 + m])
    grads = attend_back(low, w, qkv, p)
    grads_ref[...] = grads
    dx = heads_back(grads, w)
    place = sc[0] ^ sc[1]
    pick_features(place, m, da + dx, outs[0])
    for k in range(1, n):
        pick_features(place ^ k, m, dx, outs[k])


def k_total(ins, outs, scr):
    outs[0][...] = (ins[0][...] + ((f32(ins[1]) + f32(ins[2])) + f32(ins[3]))).T


def k_feed_weight(m, ins, outs, scr):
    low, g, h, du = ins
    keep, send, sums = outs
    split_blocks(t_dot(low[...], g[...]), m, 0, 2, keep, send)
    split_blocks(t_dot(h[...], du[...]), m, 1, 2, keep, send)
    sums[0:1, :] = jnp.sum(f32(du), axis=0, keepdims=True)
    sums[1:8, :] = jnp.zeros((7, sums.shape[1]), F32)


def k_attend_weight(m, ins, outs, scr):
    x, grads, low, o = ins[:4]
    keep, send, sums = outs
    first = t_dot(x[...], grads[...])
    second = t_dot(low[...], o[...])
    split_blocks(jnp.concatenate([first, second], axis=1), m, 0, 1, keep, send)
    sums[...] = jnp.zeros(sums.shape, F32)
    sums[0:1, : grads.shape[1]] = jnp.sum(f32(grads), axis=0, keepdims=True)


def k_attend_weight_last(m, ins, outs, scr):
    x, grads, low, o = ins[:4]
    hidden_sums, head_sums, norm_sums = ins[4:6], ins[6], ins[7:]
    keep, send = outs
    first = t_dot(x[...], grads[...])
    second = t_dot(low[...], o[...])
    split_blocks(jnp.concatenate([first, second], axis=1), m, 0, 1, keep, send)
    model = x.shape[1]
    piece = model // m
    width = grads.shape[1]
    own = jnp.sum(f32(grads), axis=0, keepdims=True)
    own = jnp.concatenate([own, jnp.zeros((1, model - width), F32)], axis=1)
    common = [r[0:1, :] for r in hidden_sums] + [own, head_sums[0:1, :]]
    common = jnp.concatenate(common, axis=0)
    each = jnp.concatenate([r[0:3, :] for r in norm_sums], axis=0)
    rows = keep.shape[0] // 2
    for k in range(m):
        target = send if k % 2 else keep
        start = (k // 2) * rows + piece
        block = jnp.concatenate(
            [each[:, k * piece : (k + 1) * piece], jnp.zeros((each.shape[0], model - piece), F32)],
            axis=1,
        )
        target[start : start + 16, :] = jnp.concatenate([common, block], axis=0).astype(BF16)


def k_middle(ins, outs, scr):
    keep, got = ins
    total = f32(keep) + f32(got)
    at = 0
    for out in outs:
        out[...] = total[at : at + out.shape[0]].astype(BF16)
        at += out.shape[0]


def k_add(ins, outs, scr):
    count = len(ins) // 2
    at = 0
    for first, second in zip(ins[:count], ins[count:]):
        rows = first.shape[0]
        outs[0][at : at + rows, :] = (f32(first) + f32(second)).astype(BF16)
        at += rows


def k_add_whole(ins, outs, scr):
    at = 0
    for ref in ins[:3]:
        outs[0][at : at + ref.shape[0], :] = ref[...]
        at += ref.shape[0]
    at = 0
    for ref in ins[3:]:
        rows = ref.shape[0]
        total = f32(outs[0].at[at : at + rows]) + f32(ref)
        outs[0][at : at + rows, :] = total.astype(BF16)
        at += rows


def k_feed_outputs(ins, outs, scr):
    half = ins[0].shape[0]
    for layer in range(2):
        for i, out in enumerate(outs):
            for j in range(2):
                at = 4 * layer + 2 * i + j
                out[layer, j * half : (j + 1) * half, :] = f32(ins[at]) + f32(ins[8 + at])


def k_attend_outputs(ins, outs, scr):
    grad_w, qv, b_out, gains, shifts, b_up, b_down = outs
    piece = grad_w.shape[1]
    total = f32(ins[0]) + f32(ins[1])
    grad_w[0] = total[:piece]
    half = piece // 2
    grad_w[1, :half, :] = f32(ins[2]) + f32(ins[4])
    grad_w[1, half:, :] = f32(ins[3]) + f32(ins[5])
    small = total[piece:]
    b_up[...] = small[0:2]
    for layer in range(2):
        heads = small[2 + layer : 3 + layer]
        qv[layer, 0:1, :] = heads[:, :piece]
        qv[layer, 1:2, :] = heads[:, 2 * piece : 3 * piece]
        at = 4 + 6 * layer
        b_out[layer : layer + 1, :] = small[at + 2 : at + 3, :piece]
        b_down[layer : layer + 1, :] = small[at + 5 : at + 6, :piece]
        for which in range(2):
            start = at + 3 * which
            gains[layer, which : which + 1, :] = small[start : start + 1, :piece]
            shifts[layer, which : which + 1, :] = small[start + 1 : start + 2, :piece]


def per_device(
    hidden_in, lengths, w_attn, b_qv, b_out, ln_gain, ln_bias, w_up, b_up, w_down, b_down, cotangent
):
    layers = w_attn.shape[0]
    n, m = lax.axis_size("row"), lax.axis_size("col")
    tokens, piece = hidden_in.shape
    model = piece * m
    hidden = w_up.shape[2]
    width = w_attn.shape[2] // 4
    heads = width // HEAD_DIM
    sc = lengths

    tile = (tokens, model)

    def layer_of(array, layer):
        return (array, (1,) + array.shape[1:], (layer, 0, 0))

    half_block, low_block = sds((piece // 2, hidden), BF16), sds((piece, hidden), BF16)

    def pack(rows, arrays, after=()):
        return call(k_pack, [sds((rows, hidden), BF16)], arrays, after=after, final=True)[0]

    def held(arrays, after):
        return [
            call(k_pack, [sds(a.shape, a.dtype)], [whole(a)], after=after, final=True)[0]
            for a in arrays
        ]

    def along_of(arrays):
        return [exchange(a, "col", 2) for a in arrays]

    def gathered(own, along, rows=piece, after=()):
        both = pack(2 * rows, [whole(a) for a in [*own, *along]], after)
        near = exchange(both, "col", 1)
        views = [(both, 0), (near, 0), (both, 1), (near, 1)]
        return [(a, (rows, hidden), (i, 0)) for a, i in views]

    def pair_sum(value, after=()):
        return call(k_sum, [low_tile], [value, exchange(value, "row", 1)], after=after)[0]

    def both(value):
        return [value, exchange(value, "row", 2)]

    smalls = [b_out, b_down, ln_gain, ln_bias, b_up, b_qv]
    block, rowwise, mine = call(
        k_start,
        [sds((piece + 16, hidden), BF16), sds((16, hidden), BF16), sds((tokens, piece), BF16)],
        [layer_of(w_attn, 0), whole(hidden_in.T), *[[a] for a in smalls]],
        [pltpu.VMEM(a.shape, a.dtype) for a in smalls] + [pltpu.SemaphoreType.DMA((6,))],
        final=True,
        vmem_mib=60,
    )
    along = exchange(block, "col", 2)
    mine = turned(mine)
    x_in = [mine] + [exchange(mine, "row", k) for k in range(1, n)]
    (x,) = call(k_prep, [sds(tile, BF16)], [sc, *x_in])
    weights = [whole(a) for a in (w_attn, w_up, w_down)]
    halves = call(k_split, [half_block] * 8, weights, after=x_in[1:], final=True)
    down0, attn1, up1, down1 = [halves[2 * i : 2 * i + 2] for i in range(4)]
    up0 = pack(piece, [layer_of(w_up, 0)], [mine])
    (up0_along,) = along_of([up0])
    attn0 = gathered([block], [along], piece + 16, [*x_in[1:], up0_along])

    low_tile = sds(tile, BF16)
    unit_out = sds((tokens, model + 128), F32)
    qkv_out, p_out, o_out = (
        sds((tokens, 3 * width), BF16),
        sds((heads, tokens, tokens), F32),
        sds((tokens, width), BF16),
    )
    g_out, slope_out = sds((tokens, hidden), BF16), sds((tokens, hidden), F32)
    feed_out = [low_tile, unit_out, low_tile, g_out, slope_out]

    z, prm, o0, qkv0, p0 = call(
        partial(k_attend_first, m),
        [low_tile, sds((16, model), F32), o_out, qkv_out, p_out],
        [sc, x, *attn0, rowwise],
        after=[down0[0]],
    )
    down0_along = along_of(down0)
    z = pair_sum(z, down0_along)
    up0 = gathered([up0], [up0_along], after=[z])
    down0 = gathered(down0, down0_along, after=[z])
    attn1_along = along_of(attn1)
    f, unit_a0, h0, g0, slope0 = call(
        partial(k_feed, m, 0),
        feed_out,
        [*both(z), x, *up0, *down0, rowwise, prm],
        after=attn1_along,
    )
    attn1 = gathered(attn1, attn1_along, after=[f])
    up1_along = along_of(up1[:1])
    (low,) = call(k_turned, [sds((tokens, piece), BF16)], [whole(cotangent.T)], after=[f], final=True)
    cotan = turned(low)
    f = pair_sum(f, [attn1[1][0], *up1_along, cotan])
    up1_along += along_of(up1[1:])
    down1_along = along_of(down1[:1])
    z, unit_b0, x1, o1, qkv1, p1 = call(
        partial(k_attend, m, 1),
        [low_tile, unit_out, low_tile, o_out, qkv_out, p_out],
        [sc, *both(f), unit_a0, *attn1, rowwise, prm],
        after=[up1_along[1], *down1_along],
    )
    down1_along += along_of(down1[1:])
    up1 = gathered(up1, up1_along, after=[z])
    z = pair_sum(z, [down1_along[1], up1[1][0]])
    down1 = gathered(down1, down1_along, after=[z])
    f, unit_a1, h1, g1, slope1 = call(
        partial(k_feed, m, 1),
        feed_out,
        [*both(z), unit_b0, *up1, *down1, rowwise, prm],
    )
    (again,) = held([cotan], [f])
    cotan = [cotan] + [exchange(again, "row", k) for k in range(1, n)]
    f = pair_sum(f, cotan[1:])
    (cotan,) = call(k_prep, [sds(tile, BF16)], [sc, *cotan], after=[f])

    sums_out = sds((8, model), F32)
    feed_back_out = [sds(tile, F32), low_tile, low_tile, sds((tokens, hidden), BF16), sums_out]
    out, df, df_low, dh, du, sums_b1 = call(
        partial(k_turn, m, 1),
        [sds((piece, tokens), BF16)] + feed_back_out,
        [sc, *both(f), unit_a1, cotan, *up1, *down1, slope1, prm],
        [pltpu.VMEM((tokens, piece), F32)],
    )
    out_hidden = turned(out)
    weight_out = [sds((4 * piece, hidden), BF16)] * 2 + [sds((8, hidden), F32)]
    keep, send, hidden_sums1 = call(
        partial(k_feed_weight, m), weight_out, [df_low, g1, h1, du]
    )
    got = exchange(send, "col", 1)
    dh = pair_sum(dh, [got])
    stay1 = call(k_middle, [half_block] * 8, [keep, got], after=[dh])
    more1 = along_of(stay1[4:6])
    da, da_low, dx, grads1, sums_a1 = call(
        partial(k_attend_back, m, 1),
        [sds(tile, F32), low_tile, low_tile, qkv_out, sums_out],
        [*both(dh), df, unit_a1, *attn1, qkv1, p1, prm],
        after=more1,
    )
    keep, send, head_sums1 = call(
        partial(k_attend_weight, m),
        [sds((2 * piece, 4 * width), BF16)] * 2 + [sums_out],
        [x1, grads1, da_low, o1],
    )
    got = exchange(send, "col", 1)
    more1 += along_of(held(stay1[6:7], [dx]))
    (low,) = call(k_add, [half_block], [stay1[0], more1[0]], after=[dx])
    terms1 = [last_of_dp(low)]
    dx = pair_sum(dx, [got, more1[2], terms1[0][1]])
    (out_hidden,) = held([out_hidden], [dx])
    attn1_stay = call(k_middle, [half_block] * 4, [keep, got], after=[dx])
    more1 += along_of(held(stay1[7:], [dx]))
    attn1_more = along_of(attn1_stay[2:3])
    for i in (1, 2):
        (low,) = call(k_add, [half_block], [stay1[i], more1[i]], after=[dx])
        terms1 += [last_of_dp(low)]

    df, df_low, dh, du, sums_b0 = call(
        partial(k_feed_back, m, 0),
        feed_back_out,
        [*both(dx), da, unit_b0, *up0, *down0, slope0, prm],
        after=[more1[3], *attn1_more, terms1[1][1], terms1[2][1], out_hidden],
    )
    keep, send, hidden_sums0 = call(
        partial(k_feed_weight, m), weight_out, [df_low, g0, h0, du]
    )
    got = exchange(send, "col", 1)
    attn1_more += along_of(held(attn1_stay[3:], [dh]))
    (low,) = call(k_add, [half_block], [stay1[3], more1[3]], after=[dh])
    terms1 += [last_of_dp(low)]
    dh = pair_sum(dh, [got, attn1_more[1], terms1[3][1]])
    stay0 = call(
        k_middle, [half_block] * 4 + [low_block] + [half_block] * 2, [keep, got], after=[dh]
    )
    more0 = along_of(stay0[4:6])
    attn1_terms = []
    for i in range(2):
        (low,) = call(k_add, [half_block], [attn1_stay[i], attn1_more[i]], after=[dh])
        attn1_terms.append(last_of_dp(low))
    *dx, low_last, grads0, sums_a0 = call(
        partial(k_attend_back_last, n, m),
        [sds((tokens, piece), F32)]
        + [sds((tokens, piece), BF16)] * (n - 1)
        + [low_tile, qkv_out, sums_out],
        [sc, *both(dh), df, unit_a0, *attn0, qkv0, p0, prm],
        after=[*more0, attn1_terms[0][1], attn1_terms[1][1]],
    )
    more0 += along_of(held(stay0[6:], [dx[0]]))
    most = [sds((3 * piece // 2, hidden), BF16)]
    (low,) = call(k_add_whole, most, [*stay0[:3], *more0[:2]])
    most0_terms = last_of_dp(low)
    (grad_total,) = call(
        k_total,
        [sds((piece, tokens), F32)],
        [dx[0]] + [exchange(dx[k], "row", k) for k in range(1, n)],
    )
    (grad_input,) = held([turned(grad_total)], [])

    keep, send = call(
        partial(k_attend_weight_last, m),
        [sds((2 * (piece + 16), 4 * width), BF16)] * 2,
        [
            x,
            grads0,
            low_last,
            o0,
            hidden_sums0,
            hidden_sums1,
            head_sums1,
            sums_a0,
            sums_b0,
            sums_a1,
            sums_b1,
        ],
    )
    got = exchange(send, "col", 1)
    low_tail = sds((piece + 16, hidden), BF16)
    attn0_stay, attn0_go = call(k_middle, [low_tail] * 2, [keep, got])
    (attn0_more,) = along_of([attn0_go])
    (low,) = call(k_add, [half_block], [stay0[3], more0[2]])
    rest0_terms = last_of_dp(low)
    (low,) = call(k_add, [low_tail], [attn0_stay, attn0_more], after=[grad_total])
    attn0_terms = [last_of_dp(low)]
    def halves_of(array):
        return [(array, (piece // 2, hidden), (i, 0)) for i in range(3)]

    first = [halves_of(a) + [b] for a, b in zip(most0_terms, rest0_terms)]
    second = [[t[side] for t in terms1] for side in range(2)]
    grad_down, grad_up = call(
        k_feed_outputs,
        [sds((layers, piece, hidden), F32)] * 2,
        [*first[0], *second[0], *first[1], *second[1]],
        after=[grad_input],
        final=True,
    )
    grad_attn, grad_qv, grad_out, grad_gain, grad_shift, grad_b_up, grad_b_down = call(
        k_attend_outputs,
        [
            sds(w_attn.shape, F32),
            sds(b_qv.shape, F32),
            sds(b_out.shape, F32),
            sds(ln_gain.shape, F32),
            sds(ln_bias.shape, F32),
            sds(b_up.shape, F32),
            sds(b_down.shape, F32),
        ],
        [t[side] for terms in (attn0_terms, attn1_terms) for side in range(2) for t in terms],
        final=True,
    )
    return (
        out_hidden.T,
        grad_input.T,
        grad_attn,
        grad_qv,
        grad_out,
        grad_gain,
        grad_shift,
        grad_up,
        grad_b_up,
        grad_down,
        grad_b_down,
    )


def solution(mesh):
    in_specs = (
        P(("dp", "row"), "col"),
        P("dp"),
        P(None, "col", "row"),
        P(None, None, "row"),
        P(None, "col"),
        P(None, None, "col"),
        P(None, None, "col"),
        P(None, "col", "row"),
        P(None, "row"),
        P(None, "col", "row"),
        P(None, "col"),
        P(("dp", "row"), "col"),
    )
    out_specs = (
        P(("dp", "row"), "col"),
        P(("dp", "row"), "col"),
        P(None, "col", "row"),
        P(None, None, "row"),
        P(None, "col"),
        P(None, None, "col"),
        P(None, None, "col"),
        P(None, "col", "row"),
        P(None, "row"),
        P(None, "col", "row"),
        P(None, "col"),
    )
    return jax.shard_map(
        per_device, mesh=mesh, in_specs=in_specs, out_specs=out_specs, check_vma=False
    )
```

```python
import math
from functools import partial

import jax
import jax.numpy as jnp
from jax import lax
from jax.experimental import pallas as pl
from jax.experimental.pallas import tpu as pltpu
from jax.sharding import PartitionSpec as P


HEAD_DIM = 64
EPS = 1e-5
MASKED = -1e30
F32 = jnp.float32
BF16 = jnp.bfloat16


def exchange(x, axis, bit):
    n = lax.axis_size(axis)
    return lax.ppermute(x, axis, [(i, i ^ bit) for i in range(n)])


def turned(x):
    n = lax.axis_size("row")
    pairs = [(a * n + b, b * n + a) for a in range(n) for b in range(n)]
    return lax.ppermute(x, ("row", "col"), pairs)


def last_of_dp(low):
    bit = 1
    while 2 * bit < lax.axis_size("dp"):
        low = (low.astype(F32) + exchange(low, "dp", bit).astype(F32)).astype(BF16)
        bit *= 2
    return low, exchange(low, "dp", bit)


def sds(shape, dtype):
    return jax.ShapeDtypeStruct(shape, dtype)


def whole(array):
    return (array, array.shape, (0,) * array.ndim)


def call(kernel, outs, ins, scratch=(), after=(), final=False, vmem_mib=32):
    vmem = pl.BlockSpec(memory_space=pltpu.VMEM)
    specs, args = [], []
    moved = 0
    for item in ins:
        if isinstance(item, tuple):
            array, shape, index = item
            specs.append(pl.BlockSpec(shape, lambda i, index=index: index))
            moved += math.prod(shape) * array.dtype.itemsize
            args.append(array)
            continue
        if isinstance(item, list):
            args.append(item[0])
            specs.append(pl.BlockSpec(memory_space=pltpu.HBM))
            continue
        args.append(item)
        if item.dtype == jnp.int32:
            specs.append(pl.BlockSpec(memory_space=pltpu.SMEM))
        else:
            specs.append(vmem)
            moved += item.size * item.dtype.itemsize
    moved += sum(o.size * o.dtype.itemsize for o in outs)
    n_in, n_after, n_out = len(ins), len(after), len(outs)
    final = n_out if final is True else final

    def body(*refs):
        inputs = list(refs[:n_in])
        if args[0].dtype == jnp.int32:
            col = lax.axis_index("col")
            inputs[0] = (lax.axis_index("row"), col, refs[0][col])
        kernel(
            inputs,
            refs[n_in + n_after : n_in + n_after + n_out],
            refs[n_in + n_after + n_out :],
        )

    return pl.pallas_call(
        body,
        grid=(1,),
        out_shape=outs,
        in_specs=specs + [pl.BlockSpec(memory_space=pl.ANY)] * n_after,
        out_specs=[
            pl.BlockSpec(o.shape, lambda i, d=len(o.shape): (0,) * d)
            if final and i < final
            else vmem
            for i, o in enumerate(outs)
        ],
        scratch_shapes=list(scratch),
        compiler_params=pltpu.CompilerParams(vmem_limit_bytes=vmem_mib * 1024 * 1024),
        cost_estimate=pl.CostEstimate(
            flops=200_000_000, bytes_accessed=moved, transcendentals=0
        ),
    )(*args, *after)


def rows_of(refs):
    rows = refs[0].shape[0] // 64 * 64
    return jnp.concatenate([r[:rows, :] for r in refs], axis=0)


def dot(a, b):
    return jnp.dot(a, b, preferred_element_type=F32)


def dot_t(a, b):
    return lax.dot_general(a, b, (((1,), (1,)), ((), ())), preferred_element_type=F32)


def t_dot(a, b):
    return lax.dot_general(a, b, (((0,), (0,)), ((), ())), preferred_element_type=F32)


def f32(ref):
    return ref[...].astype(F32)


def tree(refs):
    values = [f32(r) for r in refs]
    while len(values) > 1:
        values = [values[i] + values[i + 1] for i in range(0, len(values), 2)]
    return values[0]


def params_of(prm, layer, which):
    rows = (2 * which + layer, 4 + 2 * layer + which, 8 + 2 * layer + which)
    return [prm[i : i + 1, :] for i in rows]


def norm_of(v):
    mean = jnp.mean(v, axis=-1, keepdims=True)
    centred = v - mean
    r = lax.rsqrt(jnp.mean(centred * centred, axis=-1, keepdims=True) + EPS)
    return centred * r, r


def norm_back(e, unit, r, gain):
    c = e * gain
    return r * (
        c
        - jnp.mean(c, axis=-1, keepdims=True)
        - unit * jnp.mean(c * unit, axis=-1, keepdims=True)
    )


def put_unit(ref, unit, r):
    model = unit.shape[1]
    ref[:, :model] = unit
    ref[:, model:] = jnp.broadcast_to(r, (unit.shape[0], 128))


def get_unit(ref):
    model = ref.shape[1] - 128
    return ref[:, :model], ref[:, model : model + 1]


def put_sums(ref, e, unit, low):
    ref[0:1, :] = jnp.sum(e * unit, axis=0, keepdims=True)
    ref[1:2, :] = jnp.sum(e, axis=0, keepdims=True)
    ref[2:3, :] = jnp.sum(low.astype(F32), axis=0, keepdims=True)
    ref[3:8, :] = jnp.zeros((5, ref.shape[1]), F32)


def place_features(sc, pieces, target):
    place = sc[0] ^ sc[1]
    width = pieces[0].shape[1]
    for k, piece in enumerate(pieces):
        for j in range(len(pieces)):

            @pl.when((place ^ k) == j)
            def _():
                target[:, j * width : (j + 1) * width] = piece[...].astype(target.dtype)


def pick_features(at, count, value, target):
    width = value.shape[1] // count
    for j in range(count):

        @pl.when(at == j)
        def _():
            target[...] = value[:, j * width : (j + 1) * width].astype(target.dtype)


def project(sc, layer, x, w, rowwise, qkv_ref, p_ref):
    tokens = x.shape[0]
    width = w.shape[1] // 4
    b = rowwise[2 + layer : 3 + layer, : 2 * width].astype(F32)
    shift = jnp.concatenate([b[:, :width], jnp.zeros((1, width), F32), b[:, width:]], axis=1)
    qkv = (dot(x, w[:, : 3 * width]) + shift).astype(BF16)
    qkv_ref[...] = qkv
    visible = lax.broadcasted_iota(jnp.int32, (tokens, tokens), 1) < sc[2]
    mixed = []
    for h in range(width // HEAD_DIM):
        q = qkv[:, h * HEAD_DIM : (h + 1) * HEAD_DIM]
        k = qkv[:, width + h * HEAD_DIM : width + (h + 1) * HEAD_DIM]
        v = qkv[:, 2 * width + h * HEAD_DIM : 2 * width + (h + 1) * HEAD_DIM]
        s = jnp.where(visible, dot_t(q, k) * HEAD_DIM ** (-0.5), MASKED)
        e = jnp.exp(s - jnp.max(s, axis=-1, keepdims=True))
        p = e / jnp.sum(e, axis=-1, keepdims=True)
        p_ref[h] = p
        mixed.append(dot(p.astype(BF16), v))
    return jnp.concatenate(mixed, axis=1).astype(BF16)


def mix_out(o, w):
    return dot_t(o, w[:, 3 * (w.shape[1] // 4) :])


def attend_back(d, w, qkv_ref, p_ref):
    width = w.shape[1] // 4
    do = dot(d, w[:, 3 * width :]).astype(BF16)
    qkv = qkv_ref[...]
    dq, dk, dv = [], [], []
    for h in range(width // HEAD_DIM):
        q = qkv[:, h * HEAD_DIM : (h + 1) * HEAD_DIM]
        k = qkv[:, width + h * HEAD_DIM : width + (h + 1) * HEAD_DIM]
        v = qkv[:, 2 * width + h * HEAD_DIM : 2 * width + (h + 1) * HEAD_DIM]
        g = do[:, h * HEAD_DIM : (h + 1) * HEAD_DIM]
        p = p_ref[h]
        dv.append(t_dot(p.astype(BF16), g))
        dp = dot_t(g, v)
        ds = (p * (dp - jnp.sum(p * dp, axis=-1, keepdims=True))).astype(BF16)
        dq.append(dot(ds, k) * HEAD_DIM ** (-0.5))
        dk.append(t_dot(ds, q) * HEAD_DIM ** (-0.5))
    return jnp.concatenate(dq + dk + dv, axis=1).astype(BF16)


def heads_back(low, w):
    return dot_t(low, w[:, : 3 * (w.shape[1] // 4)])


def raise_hidden(layer, h, up, rowwise):
    u = dot(h, up) + rowwise[layer : layer + 1, :].astype(F32)
    cdf = 0.5 * (1.0 + lax.erf(u * (0.5**0.5)))
    slope = cdf + u * (jnp.exp(-0.5 * u * u) * 0.3989422804014327)
    return (u * cdf).astype(BF16), slope


def split_blocks(grad, count, part, parts, keep, send):
    block = grad.shape[0] // count
    each = keep.shape[0] // (2 * parts)
    for k in range(count):
        target = send if k % 2 else keep
        start = ((k // 2) * parts + part) * each
        target[start : start + block, :] = grad[k * block : (k + 1) * block].astype(BF16)


def k_start(ins, outs, scr):
    attn, hidden_in, small = ins[0], ins[1], scr[:-1]
    block, rowwise, x = outs
    fetched = [
        pltpu.make_async_copy(a, b, scr[-1].at[i]) for i, (a, b) in enumerate(zip(ins[2:], small))
    ]
    for copy in fetched:
        copy.start()
    rows = attn.shape[1]
    block[:rows, :] = attn[0]
    x[...] = hidden_in[...].astype(F32).T.astype(BF16)
    for copy in fetched:
        copy.wait()
    b_out, b_down, gain, shift, b_up, b_qv = small
    piece = b_out.shape[1]
    norms = [b_out[...], b_down[...], gain[0], gain[1], shift[0], shift[1]]
    norms = jnp.concatenate([x.astype(F32) for x in norms] + [jnp.zeros((4, piece), F32)], axis=0)
    block[rows:, :piece] = norms.astype(BF16)
    block[rows:, piece:] = jnp.zeros((16, block.shape[1] - piece), BF16)
    qv = [b_qv[i].astype(F32) for i in range(2)]
    qv = [jnp.concatenate([x[0:1], x[1:2]], axis=1) for x in qv]
    rest = b_up.shape[1] - qv[0].shape[1]
    qv = jnp.concatenate([jnp.concatenate(qv, axis=0), jnp.zeros((2, rest), F32)], axis=1)
    low = jnp.concatenate([b_up[...].astype(F32), qv, jnp.zeros((12, b_up.shape[1]), F32)], axis=0)
    rowwise[...] = low.astype(BF16)


def k_results(ins, outs, scr):
    piece = outs[0].shape[0]
    outs[0][...] = ins[0][piece:, :]
    outs[1][...] = ins[0][:piece, :].astype(F32)
    outs[2][...] = jnp.zeros(outs[2].shape, F32)


def k_split(ins, outs, scr):
    attn, up, down = ins
    half = outs[0].shape[0]
    for i, (ref, layer) in enumerate(((down, 0), (attn, 1), (up, 1), (down, 1))):
        for j in range(2):
            outs[2 * i + j][...] = ref[layer, j * half : (j + 1) * half, :]


def k_pack(ins, outs, scr):
    at = 0
    for ref in ins:
        value = ref[0] if len(ref.shape) == 3 else ref[...]
        outs[0][at : at + value.shape[0], :] = value
        at += value.shape[0]


def k_turned(ins, outs, scr):
    outs[0][...] = ins[0][...].astype(F32).T.astype(BF16)


def k_prep(ins, outs, scr):
    sc, *pieces = ins
    place_features(sc, pieces, outs[0])


def k_sum(ins, outs, scr):
    outs[0][...] = (f32(ins[0]) + f32(ins[1])).astype(BF16)


def k_attend_first(m, ins, outs, scr):
    sc, x = ins[:2]
    w_refs, rowwise = ins[2 : 2 + m], ins[2 + m]
    z_ref, prm, o_ref, qkv, p = outs
    piece = w_refs[0].shape[0] - 16
    prm[...] = jnp.concatenate([w[piece:, :piece].astype(F32) for w in w_refs], axis=1)
    w = rows_of(w_refs)
    o = project(sc, 0, x[...], w, rowwise, qkv, p)
    o_ref[...] = o
    z_ref[...] = mix_out(o, w).astype(BF16)


def k_feed(m, layer, ins, outs, scr):
    z, z_other, base = ins[:3]
    up, down = ins[3 : 3 + m], ins[3 + m : 3 + 2 * m]
    rowwise, prm = ins[3 + 2 * m :]
    f_ref, unit_ref, h_ref, g_ref, slope_ref = outs
    if layer:
        _, gain, shift = params_of(prm, layer - 1, 1)
        x = get_unit(base)[0] * gain + shift
    else:
        x = f32(base)
    bias, gain, shift = params_of(prm, layer, 0)
    unit, r = norm_of(x + (f32(z) + f32(z_other) + bias))
    put_unit(unit_ref, unit, r)
    h = (unit * gain + shift).astype(BF16)
    h_ref[...] = h
    g, slope = raise_hidden(layer, h, rows_of(up), rowwise)
    g_ref[...] = g
    slope_ref[...] = slope
    f_ref[...] = dot_t(g, rows_of(down)).astype(BF16)


def k_attend(m, layer, ins, outs, scr):
    sc, f, f_other, unit_ref = ins[:4]
    own = ins[4 : 4 + m]
    rowwise, prm = ins[4 + m :]
    z_ref, unit_out, x_ref, o_ref, qkv, p = outs
    _, gain, shift = params_of(prm, layer - 1, 0)
    h = get_unit(unit_ref)[0] * gain + shift
    bias, gain, shift = params_of(prm, layer - 1, 1)
    unit, r = norm_of(h + (f32(f) + f32(f_other) + bias))
    put_unit(unit_out, unit, r)
    x = (unit * gain + shift).astype(BF16)
    x_ref[...] = x
    w = rows_of(own)
    o = project(sc, layer, x, w, rowwise, qkv, p)
    o_ref[...] = o
    z_ref[...] = mix_out(o, w).astype(BF16)


def feed_back(e, unit, r, gain, ws, slope, outs):
    up, down = ws
    df_ref, low_ref, dh_ref, du_ref, sums = outs
    df = norm_back(e, unit, r, gain)
    low = df.astype(BF16)
    df_ref[...] = df
    low_ref[...] = low
    put_sums(sums, e, unit, low)
    du = (dot(low, rows_of(down)) * slope[...]).astype(BF16)
    du_ref[...] = du
    dh_ref[...] = dot_t(du, rows_of(up)).astype(BF16)


def k_turn(m, layer, ins, outs, scr):
    sc, f, f_other, unit_ref, cotan = ins[:5]
    ws = [ins[5 + i * m : 5 + (i + 1) * m] for i in range(2)]
    slope, prm = ins[5 + 2 * m :]
    _, gain, shift = params_of(prm, layer, 0)
    h = get_unit(unit_ref)[0] * gain + shift
    bias, gain, shift = params_of(prm, layer, 1)
    unit, r = norm_of(h + (f32(f) + f32(f_other) + bias))
    pick_features(sc[0] ^ sc[1], m, unit * gain + shift, scr[0])
    outs[0][...] = scr[0][...].T.astype(BF16)
    feed_back(f32(cotan), unit, r, gain, ws, slope, outs[1:])


def k_feed_back(m, layer, ins, outs, scr):
    dx, dx_other, da, full = ins[:4]
    ws = [ins[4 + i * m : 4 + (i + 1) * m] for i in range(2)]
    slope, prm = ins[4 + 2 * m :]
    _, gain, _ = params_of(prm, layer, 1)
    e = da[...] + (f32(dx) + f32(dx_other))
    unit, r = get_unit(full)
    feed_back(e, unit, r, gain, ws, slope, outs)


def k_attend_back(m, layer, ins, outs, scr):
    dh, dh_other, df, unit_ref = ins[:4]
    qkv, p, prm = ins[4 + m :]
    da_ref, low_ref, dx_ref, grads_ref, sums = outs
    _, gain, _ = params_of(prm, layer, 0)
    e = df[...] + (f32(dh) + f32(dh_other))
    unit, r = get_unit(unit_ref)
    da = norm_back(e, unit, r, gain)
    low = da.astype(BF16)
    da_ref[...] = da
    low_ref[...] = low
    put_sums(sums, e, unit, low)
    w = rows_of(ins[4 : 4 + m])
    grads = attend_back(low, w, qkv, p)
    grads_ref[...] = grads
    dx_ref[...] = heads_back(grads, w).astype(BF16)


def k_attend_back_last(n, m, ins, outs, scr):
    sc, dh, dh_other, df, unit_ref = ins[:5]
    qkv, p, prm = ins[5 + m :]
    low_ref, grads_ref, sums = outs[n:]
    _, gain, _ = params_of(prm, 0, 0)
    e = df[...] + (f32(dh) + f32(dh_other))
    unit, r = get_unit(unit_ref)
    da = norm_back(e, unit, r, gain)
    low = da.astype(BF16)
    low_ref[...] = low
    put_sums(sums, e, unit, low)
    w = rows_of(ins[5 : 5 + m])
    grads = attend_back(low, w, qkv, p)
    grads_ref[...] = grads
    dx = heads_back(grads, w)
    place = sc[0] ^ sc[1]
    pick_features(place, m, da + dx, outs[0])
    for k in range(1, n):
        pick_features(place ^ k, m, dx, outs[k])


def k_total(ins, outs, scr):
    piece = ins[0].shape[1]
    total = ins[0][...] + ((f32(ins[1]) + f32(ins[2])) + f32(ins[3]))
    outs[0][:piece, :] = total.T.astype(BF16)
    outs[0][piece:, :] = ins[4][...]


def k_feed_weight(m, ins, outs, scr):
    low, g, h, du = ins
    keep, send, sums = outs
    split_blocks(t_dot(low[...], g[...]), m, 0, 2, keep, send)
    split_blocks(t_dot(h[...], du[...]), m, 1, 2, keep, send)
    sums[0:1, :] = jnp.sum(f32(du), axis=0, keepdims=True)
    sums[1:8, :] = jnp.zeros((7, sums.shape[1]), F32)


def k_attend_weight(m, ins, outs, scr):
    x, grads, low, o = ins[:4]
    keep, send, sums = outs
    first = t_dot(x[...], grads[...])
    second = t_dot(low[...], o[...])
    split_blocks(jnp.concatenate([first, second], axis=1), m, 0, 1, keep, send)
    sums[...] = jnp.zeros(sums.shape, F32)
    sums[0:1, : grads.shape[1]] = jnp.sum(f32(grads), axis=0, keepdims=True)


def k_attend_weight_last(m, ins, outs, scr):
    x, grads, low, o = ins[:4]
    hidden_sums, head_sums, norm_sums = ins[4:6], ins[6], ins[7:]
    keep, send = outs
    first = t_dot(x[...], grads[...])
    second = t_dot(low[...], o[...])
    split_blocks(jnp.concatenate([first, second], axis=1), m, 0, 1, keep, send)
    model = x.shape[1]
    piece = model // m
    width = grads.shape[1]
    own = jnp.sum(f32(grads), axis=0, keepdims=True)
    own = jnp.concatenate([own, jnp.zeros((1, model - width), F32)], axis=1)
    common = [r[0:1, :] for r in hidden_sums] + [own, head_sums[0:1, :]]
    common = jnp.concatenate(common, axis=0)
    each = jnp.concatenate([r[0:3, :] for r in norm_sums], axis=0)
    rows = keep.shape[0] // 2
    for k in range(m):
        target = send if k % 2 else keep
        start = (k // 2) * rows + piece
        block = jnp.concatenate(
            [each[:, k * piece : (k + 1) * piece], jnp.zeros((each.shape[0], model - piece), F32)],
            axis=1,
        )
        target[start : start + 16, :] = jnp.concatenate([common, block], axis=0).astype(BF16)


def k_middle(ins, outs, scr):
    keep, got = ins
    total = f32(keep) + f32(got)
    at = 0
    for out in outs:
        out[...] = total[at : at + out.shape[0]].astype(BF16)
        at += out.shape[0]


def k_add(ins, outs, scr):
    count = len(ins) // 2
    at = 0
    for first, second in zip(ins[:count], ins[count:]):
        rows = first.shape[0]
        outs[0][at : at + rows, :] = (f32(first) + f32(second)).astype(BF16)
        at += rows


def k_add_whole(ins, outs, scr):
    at = 0
    for ref in ins[:3]:
        outs[0][at : at + ref.shape[0], :] = ref[...]
        at += ref.shape[0]
    at = 0
    for ref in ins[3:]:
        rows = ref.shape[0]
        total = f32(outs[0].at[at : at + rows]) + f32(ref)
        outs[0][at : at + rows, :] = total.astype(BF16)
        at += rows


def k_feed_outputs(ins, outs, scr):
    half = ins[0].shape[0]
    for layer in range(2):
        for i, out in enumerate(outs):
            for j in range(2):
                at = 4 * layer + 2 * i + j
                out[layer, j * half : (j + 1) * half, :] = f32(ins[at]) + f32(ins[8 + at])


def k_attend_outputs(ins, outs, scr):
    grad_w, qv, b_out, gains, shifts, b_up, b_down = outs
    piece = grad_w.shape[1]
    total = f32(ins[0]) + f32(ins[1])
    grad_w[0] = total[:piece]
    half = piece // 2
    grad_w[1, :half, :] = f32(ins[2]) + f32(ins[4])
    grad_w[1, half:, :] = f32(ins[3]) + f32(ins[5])
    small = total[piece:]
    b_up[...] = small[0:2]
    for layer in range(2):
        heads = small[2 + layer : 3 + layer]
        qv[layer, 0:1, :] = heads[:, :piece]
        qv[layer, 1:2, :] = heads[:, 2 * piece : 3 * piece]
        at = 4 + 6 * layer
        b_out[layer : layer + 1, :] = small[at + 2 : at + 3, :piece]
        b_down[layer : layer + 1, :] = small[at + 5 : at + 6, :piece]
        for which in range(2):
            start = at + 3 * which
            gains[layer, which : which + 1, :] = small[start : start + 1, :piece]
            shifts[layer, which : which + 1, :] = small[start + 1 : start + 2, :piece]


def per_device(
    hidden_in, lengths, w_attn, b_qv, b_out, ln_gain, ln_bias, w_up, b_up, w_down, b_down, cotangent
):
    layers = w_attn.shape[0]
    n, m = lax.axis_size("row"), lax.axis_size("col")
    tokens, piece = hidden_in.shape
    model = piece * m
    hidden = w_up.shape[2]
    width = w_attn.shape[2] // 4
    heads = width // HEAD_DIM
    sc = lengths

    tile = (tokens, model)

    def layer_of(array, layer):
        return (array, (1,) + array.shape[1:], (layer, 0, 0))

    half_block, low_block = sds((piece // 2, hidden), BF16), sds((piece, hidden), BF16)

    def pack(rows, arrays, after=()):
        return call(k_pack, [sds((rows, hidden), BF16)], arrays, after=after, final=True)[0]

    def held(arrays, after):
        return [
            call(k_pack, [sds(a.shape, a.dtype)], [whole(a)], after=after, final=True)[0]
            for a in arrays
        ]

    def along_of(arrays):
        return [exchange(a, "col", 2) for a in arrays]

    def gathered(own, along, rows=piece, after=()):
        both = pack(2 * rows, [whole(a) for a in [*own, *along]], after)
        near = exchange(both, "col", 1)
        views = [(both, 0), (near, 0), (both, 1), (near, 1)]
        return [(a, (rows, hidden), (i, 0)) for a, i in views]

    def pair_sum(value, after=()):
        return call(k_sum, [low_tile], [value, exchange(value, "row", 1)], after=after)[0]

    def both(value):
        return [value, exchange(value, "row", 2)]

    smalls = [b_out, b_down, ln_gain, ln_bias, b_up, b_qv]
    block, rowwise, mine = call(
        k_start,
        [sds((piece + 16, hidden), BF16), sds((16, hidden), BF16), sds((tokens, piece), BF16)],
        [layer_of(w_attn, 0), whole(hidden_in.T), *[[a] for a in smalls]],
        [pltpu.VMEM(a.shape, a.dtype) for a in smalls] + [pltpu.SemaphoreType.DMA((6,))],
        final=True,
        vmem_mib=60,
    )
    along = exchange(block, "col", 2)
    mine = turned(mine)
    x_in = [mine] + [exchange(mine, "row", k) for k in range(1, n)]
    (x,) = call(k_prep, [sds(tile, BF16)], [sc, *x_in])
    weights = [whole(a) for a in (w_attn, w_up, w_down)]
    halves = call(k_split, [half_block] * 8, weights, after=x_in[1:], final=True)
    down0, attn1, up1, down1 = [halves[2 * i : 2 * i + 2] for i in range(4)]
    up0 = pack(piece, [layer_of(w_up, 0)], [mine])
    (up0_along,) = along_of([up0])
    near = exchange(block, "col", 1)
    (low,) = held([along], [*x_in[1:], up0_along])
    sources = (block, near, along, exchange(low, "col", 1))
    attn0 = [(a, (piece + 16, hidden), (0, 0)) for a in sources]

    low_tile = sds(tile, BF16)
    unit_out = sds((tokens, model + 128), F32)
    qkv_out, p_out, o_out = (
        sds((tokens, 3 * width), BF16),
        sds((heads, tokens, tokens), F32),
        sds((tokens, width), BF16),
    )
    g_out, slope_out = sds((tokens, hidden), BF16), sds((tokens, hidden), F32)
    feed_out = [low_tile, unit_out, low_tile, g_out, slope_out]

    z, prm, o0, qkv0, p0 = call(
        partial(k_attend_first, m),
        [low_tile, sds((16, model), F32), o_out, qkv_out, p_out],
        [sc, x, *attn0, rowwise],
        after=[down0[0]],
    )
    down0_along = along_of(down0)
    (low,) = call(k_turned, [sds((tokens, piece), BF16)], [whole(cotangent.T)], after=[z], final=True)
    cotan = turned(low)
    z = pair_sum(z, [*down0_along, cotan])
    up0 = gathered([up0], [up0_along], after=[z])
    down0 = gathered(down0, down0_along, after=[z])
    attn1_along = along_of(attn1)
    f, unit_a0, h0, g0, slope0 = call(
        partial(k_feed, m, 0),
        feed_out,
        [*both(z), x, *up0, *down0, rowwise, prm],
        after=attn1_along,
    )
    attn1 = gathered(attn1, attn1_along, after=[f])
    up1_along = along_of(up1[:1])
    f = pair_sum(f, [attn1[1][0], *up1_along])
    up1_along += along_of(up1[1:])
    down1_along = along_of(down1[:1])
    z, unit_b0, x1, o1, qkv1, p1 = call(
        partial(k_attend, m, 1),
        [low_tile, unit_out, low_tile, o_out, qkv_out, p_out],
        [sc, *both(f), unit_a0, *attn1, rowwise, prm],
        after=[up1_along[1], *down1_along],
    )
    down1_along += along_of(down1[1:])
    up1 = gathered(up1, up1_along, after=[z])
    z = pair_sum(z, [down1_along[1], up1[1][0]])
    down1 = gathered(down1, down1_along, after=[z])
    f, unit_a1, h1, g1, slope1 = call(
        partial(k_feed, m, 1),
        feed_out,
        [*both(z), unit_b0, *up1, *down1, rowwise, prm],
    )
    (again,) = held([cotan], [f])
    cotan = [cotan, None] + [exchange(again, "row", k) for k in range(2, n)]
    f = pair_sum(f, cotan[2:])
    cotan[1] = exchange(held([again], [f])[0], "row", 1)
    (cotan,) = call(k_prep, [sds(tile, BF16)], [sc, *cotan], after=[f])

    sums_out = sds((8, model), F32)
    feed_back_out = [sds(tile, F32), low_tile, low_tile, sds((tokens, hidden), BF16), sums_out]
    out, df, df_low, dh, du, sums_b1 = call(
        partial(k_turn, m, 1),
        [sds((piece, tokens), BF16)] + feed_back_out,
        [sc, *both(f), unit_a1, cotan, *up1, *down1, slope1, prm],
        [pltpu.VMEM((tokens, piece), F32)],
    )
    weight_out = [sds((4 * piece, hidden), BF16)] * 2 + [sds((8, hidden), F32)]
    keep, send, hidden_sums1 = call(
        partial(k_feed_weight, m), weight_out, [df_low, g1, h1, du]
    )
    got = exchange(send, "col", 1)
    dh = pair_sum(dh, [got])
    stay1 = call(k_middle, [half_block] * 8, [keep, got], after=[dh])
    more1 = along_of(stay1[4:6])
    da, da_low, dx, grads1, sums_a1 = call(
        partial(k_attend_back, m, 1),
        [sds(tile, F32), low_tile, low_tile, qkv_out, sums_out],
        [*both(dh), df, unit_a1, *attn1, qkv1, p1, prm],
        after=more1,
    )
    keep, send, head_sums1 = call(
        partial(k_attend_weight, m),
        [sds((2 * piece, 4 * width), BF16)] * 2 + [sums_out],
        [x1, grads1, da_low, o1],
    )
    got = exchange(send, "col", 1)
    more1 += along_of(held(stay1[6:7], [dx]))
    (low,) = call(k_add, [half_block], [stay1[0], more1[0]], after=[dx])
    terms1 = [last_of_dp(low)]
    dx = pair_sum(dx, [got, more1[2], terms1[0][1]])
    attn1_stay = call(k_middle, [half_block] * 4, [keep, got], after=[dx])
    more1 += along_of(held(stay1[7:], [dx]))
    attn1_more = along_of(attn1_stay[2:3])
    for i in (1, 2):
        (low,) = call(k_add, [half_block], [stay1[i], more1[i]], after=[dx])
        terms1 += [last_of_dp(low)]

    df, df_low, dh, du, sums_b0 = call(
        partial(k_feed_back, m, 0),
        feed_back_out,
        [*both(dx), da, unit_b0, *up0, *down0, slope0, prm],
        after=[more1[3], *attn1_more, terms1[1][1], terms1[2][1]],
    )
    keep, send, hidden_sums0 = call(
        partial(k_feed_weight, m), weight_out, [df_low, g0, h0, du]
    )
    got = exchange(send, "col", 1)
    attn1_more += along_of(held(attn1_stay[3:], [dh]))
    (low,) = call(k_add, [half_block], [stay1[3], more1[3]], after=[dh])
    terms1 += [last_of_dp(low)]
    dh = pair_sum(dh, [got, attn1_more[1], terms1[3][1]])
    stay0 = call(
        k_middle, [half_block] * 4 + [low_block] + [half_block] * 2, [keep, got], after=[dh]
    )
    more0 = along_of(stay0[4:6])
    attn1_terms = []
    for i in range(2):
        (low,) = call(k_add, [half_block], [attn1_stay[i], attn1_more[i]], after=[dh])
        attn1_terms.append(last_of_dp(low))
    *dx, low_last, grads0, sums_a0 = call(
        partial(k_attend_back_last, n, m),
        [sds((tokens, piece), F32)]
        + [sds((tokens, piece), BF16)] * (n - 1)
        + [low_tile, qkv_out, sums_out],
        [sc, *both(dh), df, unit_a0, *attn0, qkv0, p0, prm],
        after=[*more0, attn1_terms[0][1], attn1_terms[1][1]],
    )
    more0 += along_of(held(stay0[6:], [dx[0]]))
    most = [sds((3 * piece // 2, hidden), BF16)]
    (low,) = call(k_add_whole, most, [*stay0[:3], *more0[:2]])
    most0_terms = last_of_dp(low)
    (results,) = call(
        k_total,
        [sds((2 * piece, tokens), BF16)],
        [dx[0]] + [exchange(dx[k], "row", k) for k in range(1, n)] + [out],
    )
    out_hidden, grad_input, token = call(
        k_results,
        [sds((piece, tokens), BF16), sds((piece, tokens), F32), sds((8, 128), F32)],
        [turned(results)],
        final=2,
    )

    keep, send = call(
        partial(k_attend_weight_last, m),
        [sds((2 * (piece + 16), 4 * width), BF16)] * 2,
        [
            x,
            grads0,
            low_last,
            o0,
            hidden_sums0,
            hidden_sums1,
            head_sums1,
            sums_a0,
            sums_b0,
            sums_a1,
            sums_b1,
        ],
    )
    got = exchange(send, "col", 1)
    low_tail = sds((piece + 16, hidden), BF16)
    attn0_stay, attn0_go = call(k_middle, [low_tail] * 2, [keep, got])
    (attn0_more,) = along_of([attn0_go])
    (low,) = call(k_add, [half_block], [stay0[3], more0[2]])
    rest0_terms = last_of_dp(low)
    (low,) = call(k_add, [low_tail], [attn0_stay, attn0_more], after=[results])
    attn0_terms = [last_of_dp(low)]
    def halves_of(array):
        return [(array, (piece // 2, hidden), (i, 0)) for i in range(3)]

    first = [halves_of(a) + [b] for a, b in zip(most0_terms, rest0_terms)]
    second = [[t[side] for t in terms1] for side in range(2)]
    grad_down, grad_up = call(
        k_feed_outputs,
        [sds((layers, piece, hidden), F32)] * 2,
        [*first[0], *second[0], *first[1], *second[1]],
        after=[token],
        final=True,
    )
    grad_attn, grad_qv, grad_out, grad_gain, grad_shift, grad_b_up, grad_b_down = call(
        k_attend_outputs,
        [
            sds(w_attn.shape, F32),
            sds(b_qv.shape, F32),
            sds(b_out.shape, F32),
            sds(ln_gain.shape, F32),
            sds(ln_bias.shape, F32),
            sds(b_up.shape, F32),
            sds(b_down.shape, F32),
        ],
        [t[side] for terms in (attn0_terms, attn1_terms) for side in range(2) for t in terms],
        final=True,
    )
    return (
        out_hidden.T,
        grad_input.T,
        grad_attn,
        grad_qv,
        grad_out,
        grad_gain,
        grad_shift,
        grad_up,
        grad_b_up,
        grad_down,
        grad_b_down,
    )


def solution(mesh):
    in_specs = (
        P(("dp", "row"), "col"),
        P("dp"),
        P(None, "col", "row"),
        P(None, None, "row"),
        P(None, "col"),
        P(None, None, "col"),
        P(None, None, "col"),
        P(None, "col", "row"),
        P(None, "row"),
        P(None, "col", "row"),
        P(None, "col"),
        P(("dp", "row"), "col"),
    )
    out_specs = (
        P(("dp", "row"), "col"),
        P(("dp", "row"), "col"),
        P(None, "col", "row"),
        P(None, None, "row"),
        P(None, "col"),
        P(None, None, "col"),
        P(None, None, "col"),
        P(None, "col", "row"),
        P(None, "row"),
        P(None, "col", "row"),
        P(None, "col"),
    )
    return jax.shard_map(
        per_device, mesh=mesh, in_specs=in_specs, out_specs=out_specs, check_vma=False
    )
```

```python
import math
from functools import partial

import jax
import jax.numpy as jnp
from jax import lax
from jax.experimental import pallas as pl
from jax.experimental.pallas import tpu as pltpu
from jax.sharding import PartitionSpec as P


HEAD_DIM = 64
EPS = 1e-5
MASKED = -1e30
F32 = jnp.float32
BF16 = jnp.bfloat16


def exchange(x, axis, bit):
    n = lax.axis_size(axis)
    return lax.ppermute(x, axis, [(i, i ^ bit) for i in range(n)])


def turned(x):
    n = lax.axis_size("row")
    pairs = [(a * n + b, b * n + a) for a in range(n) for b in range(n)]
    return lax.ppermute(x, ("row", "col"), pairs)


def last_of_dp(low):
    bit = 1
    while 2 * bit < lax.axis_size("dp"):
        low = (low.astype(F32) + exchange(low, "dp", bit).astype(F32)).astype(BF16)
        bit *= 2
    return low, exchange(low, "dp", bit)


def sds(shape, dtype):
    return jax.ShapeDtypeStruct(shape, dtype)


def whole(array):
    return (array, array.shape, (0,) * array.ndim)


def call(kernel, outs, ins, scratch=(), after=(), final=False, vmem_mib=32):
    vmem = pl.BlockSpec(memory_space=pltpu.VMEM)
    specs, args = [], []
    moved = 0
    for item in ins:
        if isinstance(item, tuple):
            array, shape, index = item
            specs.append(pl.BlockSpec(shape, lambda i, index=index: index))
            moved += math.prod(shape) * array.dtype.itemsize
            args.append(array)
            continue
        if isinstance(item, list):
            args.append(item[0])
            specs.append(pl.BlockSpec(memory_space=pltpu.HBM))
            continue
        args.append(item)
        if item.dtype == jnp.int32:
            specs.append(pl.BlockSpec(memory_space=pltpu.SMEM))
        else:
            specs.append(vmem)
            moved += item.size * item.dtype.itemsize
    moved += sum(o.size * o.dtype.itemsize for o in outs)
    n_in, n_after, n_out = len(ins), len(after), len(outs)
    final = n_out if final is True else final

    def body(*refs):
        inputs = list(refs[:n_in])
        if args[0].dtype == jnp.int32:
            col = lax.axis_index("col")
            inputs[0] = (lax.axis_index("row"), col, refs[0][col])
        kernel(
            inputs,
            refs[n_in + n_after : n_in + n_after + n_out],
            refs[n_in + n_after + n_out :],
        )

    return pl.pallas_call(
        body,
        grid=(1,),
        out_shape=outs,
        in_specs=specs + [pl.BlockSpec(memory_space=pl.ANY)] * n_after,
        out_specs=[
            pl.BlockSpec(o.shape, lambda i, d=len(o.shape): (0,) * d)
            if final and i < final
            else vmem
            for i, o in enumerate(outs)
        ],
        scratch_shapes=list(scratch),
        compiler_params=pltpu.CompilerParams(vmem_limit_bytes=vmem_mib * 1024 * 1024),
        cost_estimate=pl.CostEstimate(
            flops=200_000_000, bytes_accessed=moved, transcendentals=0
        ),
    )(*args, *after)


def rows_of(refs):
    rows = refs[0].shape[0] // 64 * 64
    return jnp.concatenate([r[:rows, :] for r in refs], axis=0)


def dot(a, b):
    return jnp.dot(a, b, preferred_element_type=F32)


def dot_t(a, b):
    return lax.dot_general(a, b, (((1,), (1,)), ((), ())), preferred_element_type=F32)


def t_dot(a, b):
    return lax.dot_general(a, b, (((0,), (0,)), ((), ())), preferred_element_type=F32)


def f32(ref):
    return ref[...].astype(F32)


def tree(refs):
    values = [f32(r) for r in refs]
    while len(values) > 1:
        values = [values[i] + values[i + 1] for i in range(0, len(values), 2)]
    return values[0]


def params_of(prm, layer, which):
    rows = (2 * which + layer, 4 + 2 * layer + which, 8 + 2 * layer + which)
    return [prm[i : i + 1, :] for i in rows]


def norm_of(v):
    mean = jnp.mean(v, axis=-1, keepdims=True)
    centred = v - mean
    r = lax.rsqrt(jnp.mean(centred * centred, axis=-1, keepdims=True) + EPS)
    return centred * r, r


def norm_back(e, unit, r, gain):
    c = e * gain
    return r * (
        c
        - jnp.mean(c, axis=-1, keepdims=True)
        - unit * jnp.mean(c * unit, axis=-1, keepdims=True)
    )


def put_unit(ref, unit, r):
    model = unit.shape[1]
    ref[:, :model] = unit
    ref[:, model:] = jnp.broadcast_to(r, (unit.shape[0], 128))


def get_unit(ref):
    model = ref.shape[1] - 128
    return ref[:, :model], ref[:, model : model + 1]


def put_sums(ref, e, unit, low):
    ref[0:1, :] = jnp.sum(e * unit, axis=0, keepdims=True)
    ref[1:2, :] = jnp.sum(e, axis=0, keepdims=True)
    ref[2:3, :] = jnp.sum(low.astype(F32), axis=0, keepdims=True)
    ref[3:8, :] = jnp.zeros((5, ref.shape[1]), F32)


def place_features(sc, pieces, target):
    place = sc[0] ^ sc[1]
    width = pieces[0].shape[1]
    for k, piece in enumerate(pieces):
        for j in range(len(pieces)):

            @pl.when((place ^ k) == j)
            def _():
                target[:, j * width : (j + 1) * width] = piece[...].astype(target.dtype)


def pick_features(at, count, value, target):
    width = value.shape[1] // count
    for j in range(count):

        @pl.when(at == j)
        def _():
            target[...] = value[:, j * width : (j + 1) * width].astype(target.dtype)


def project(sc, layer, x, w, rowwise, qkv_ref, p_ref):
    tokens = x.shape[0]
    width = w.shape[1] // 4
    b = rowwise[2 + layer : 3 + layer, : 2 * width].astype(F32)
    shift = jnp.concatenate([b[:, :width], jnp.zeros((1, width), F32), b[:, width:]], axis=1)
    qkv = (dot(x, w[:, : 3 * width]) + shift).astype(BF16)
    qkv_ref[...] = qkv
    visible = lax.broadcasted_iota(jnp.int32, (tokens, tokens), 1) < sc[2]
    mixed = []
    for h in range(width // HEAD_DIM):
        q = qkv[:, h * HEAD_DIM : (h + 1) * HEAD_DIM]
        k = qkv[:, width + h * HEAD_DIM : width + (h + 1) * HEAD_DIM]
        v = qkv[:, 2 * width + h * HEAD_DIM : 2 * width + (h + 1) * HEAD_DIM]
        s = jnp.where(visible, dot_t(q, k) * HEAD_DIM ** (-0.5), MASKED)
        e = jnp.exp(s - jnp.max(s, axis=-1, keepdims=True))
        p = e / jnp.sum(e, axis=-1, keepdims=True)
        p_ref[h] = p
        mixed.append(dot(p.astype(BF16), v))
    return jnp.concatenate(mixed, axis=1).astype(BF16)


def mix_out(o, w):
    return dot_t(o, w[:, 3 * (w.shape[1] // 4) :])


def attend_back(d, w, qkv_ref, p_ref):
    width = w.shape[1] // 4
    do = dot(d, w[:, 3 * width :]).astype(BF16)
    qkv = qkv_ref[...]
    dq, dk, dv = [], [], []
    for h in range(width // HEAD_DIM):
        q = qkv[:, h * HEAD_DIM : (h + 1) * HEAD_DIM]
        k = qkv[:, width + h * HEAD_DIM : width + (h + 1) * HEAD_DIM]
        v = qkv[:, 2 * width + h * HEAD_DIM : 2 * width + (h + 1) * HEAD_DIM]
        g = do[:, h * HEAD_DIM : (h + 1) * HEAD_DIM]
        p = p_ref[h]
        dv.append(t_dot(p.astype(BF16), g))
        dp = dot_t(g, v)
        ds = (p * (dp - jnp.sum(p * dp, axis=-1, keepdims=True))).astype(BF16)
        dq.append(dot(ds, k) * HEAD_DIM ** (-0.5))
        dk.append(t_dot(ds, q) * HEAD_DIM ** (-0.5))
    return jnp.concatenate(dq + dk + dv, axis=1).astype(BF16)


def heads_back(low, w):
    return dot_t(low, w[:, : 3 * (w.shape[1] // 4)])


def raise_hidden(layer, h, up, rowwise):
    u = dot(h, up) + rowwise[layer : layer + 1, :].astype(F32)
    cdf = 0.5 * (1.0 + lax.erf(u * (0.5**0.5)))
    slope = cdf + u * (jnp.exp(-0.5 * u * u) * 0.3989422804014327)
    return (u * cdf).astype(BF16), slope


def split_blocks(grad, count, part, parts, keep, send):
    block = grad.shape[0] // count
    each = keep.shape[0] // (2 * parts)
    for k in range(count):
        target = send if k % 2 else keep
        start = ((k // 2) * parts + part) * each
        target[start : start + block, :] = grad[k * block : (k + 1) * block].astype(BF16)


def k_start(ins, outs, scr):
    attn, hidden_in, small = ins[0], ins[1], scr[:-1]
    block, rowwise, x = outs
    fetched = [
        pltpu.make_async_copy(a, b, scr[-1].at[i]) for i, (a, b) in enumerate(zip(ins[2:], small))
    ]
    for copy in fetched:
        copy.start()
    rows = attn.shape[1]
    block[:rows, :] = attn[0]
    x[...] = hidden_in[...].astype(F32).T.astype(BF16)
    for copy in fetched:
        copy.wait()
    b_out, b_down, gain, shift, b_up, b_qv = small
    piece = b_out.shape[1]
    norms = [b_out[...], b_down[...], gain[0], gain[1], shift[0], shift[1]]
    norms = jnp.concatenate([x.astype(F32) for x in norms] + [jnp.zeros((4, piece), F32)], axis=0)
    block[rows:, :piece] = norms.astype(BF16)
    block[rows:, piece:] = jnp.zeros((16, block.shape[1] - piece), BF16)
    qv = [b_qv[i].astype(F32) for i in range(2)]
    qv = [jnp.concatenate([x[0:1], x[1:2]], axis=1) for x in qv]
    rest = b_up.shape[1] - qv[0].shape[1]
    qv = jnp.concatenate([jnp.concatenate(qv, axis=0), jnp.zeros((2, rest), F32)], axis=1)
    low = jnp.concatenate([b_up[...].astype(F32), qv, jnp.zeros((12, b_up.shape[1]), F32)], axis=0)
    rowwise[...] = low.astype(BF16)


def k_results(ins, outs, scr):
    piece = outs[0].shape[0]
    outs[0][...] = ins[0][piece:, :]
    outs[1][...] = ins[0][:piece, :].astype(F32)
    outs[2][...] = jnp.zeros(outs[2].shape, F32)


def k_split(ins, outs, scr):
    attn, up, down = ins
    half = outs[0].shape[0]
    for i, (ref, layer) in enumerate(((down, 0), (attn, 1), (up, 1), (down, 1))):
        for j in range(2):
            outs[2 * i + j][...] = ref[layer, j * half : (j + 1) * half, :]


def k_pack(ins, outs, scr):
    at = 0
    for ref in ins:
        value = ref[0] if len(ref.shape) == 3 else ref[...]
        outs[0][at : at + value.shape[0], :] = value
        at += value.shape[0]


def k_turned(ins, outs, scr):
    outs[0][...] = ins[0][...].astype(F32).T.astype(BF16)


def k_prep(ins, outs, scr):
    sc, *pieces = ins
    place_features(sc, pieces, outs[0])


def k_sum(ins, outs, scr):
    outs[0][...] = (f32(ins[0]) + f32(ins[1])).astype(BF16)


def k_attend_first(m, ins, outs, scr):
    sc, x = ins[:2]
    w_refs, rowwise = ins[2 : 2 + m], ins[2 + m]
    z_ref, prm, o_ref, qkv, p = outs
    piece = w_refs[0].shape[0] - 16
    prm[...] = jnp.concatenate([w[piece:, :piece].astype(F32) for w in w_refs], axis=1)
    w = rows_of(w_refs)
    o = project(sc, 0, x[...], w, rowwise, qkv, p)
    o_ref[...] = o
    z_ref[...] = mix_out(o, w).astype(BF16)


def k_feed(m, layer, ins, outs, scr):
    z, z_other, base = ins[:3]
    up, down = ins[3 : 3 + m], ins[3 + m : 3 + 2 * m]
    rowwise, prm = ins[3 + 2 * m :]
    f_ref, unit_ref, h_ref, g_ref, slope_ref = outs
    if layer:
        _, gain, shift = params_of(prm, layer - 1, 1)
        x = get_unit(base)[0] * gain + shift
    else:
        x = f32(base)
    bias, gain, shift = params_of(prm, layer, 0)
    unit, r = norm_of(x + (f32(z) + f32(z_other) + bias))
    put_unit(unit_ref, unit, r)
    h = (unit * gain + shift).astype(BF16)
    h_ref[...] = h
    g, slope = raise_hidden(layer, h, rows_of(up), rowwise)
    g_ref[...] = g
    slope_ref[...] = slope
    f_ref[...] = dot_t(g, rows_of(down)).astype(BF16)


def k_attend(m, layer, ins, outs, scr):
    sc, f, f_other, unit_ref = ins[:4]
    own = ins[4 : 4 + m]
    rowwise, prm = ins[4 + m :]
    z_ref, unit_out, x_ref, o_ref, qkv, p = outs
    _, gain, shift = params_of(prm, layer - 1, 0)
    h = get_unit(unit_ref)[0] * gain + shift
    bias, gain, shift = params_of(prm, layer - 1, 1)
    unit, r = norm_of(h + (f32(f) + f32(f_other) + bias))
    put_unit(unit_out, unit, r)
    x = (unit * gain + shift).astype(BF16)
    x_ref[...] = x
    w = rows_of(own)
    o = project(sc, layer, x, w, rowwise, qkv, p)
    o_ref[...] = o
    z_ref[...] = mix_out(o, w).astype(BF16)


def feed_back(e, unit, r, gain, ws, slope, outs):
    up, down = ws
    df_ref, low_ref, dh_ref, du_ref, sums = outs
    df = norm_back(e, unit, r, gain)
    low = df.astype(BF16)
    df_ref[...] = df
    low_ref[...] = low
    put_sums(sums, e, unit, low)
    du = (dot(low, rows_of(down)) * slope[...]).astype(BF16)
    du_ref[...] = du
    dh_ref[...] = dot_t(du, rows_of(up)).astype(BF16)


def k_turn(m, layer, ins, outs, scr):
    sc, f, f_other, unit_ref, cotan = ins[:5]
    ws = [ins[5 + i * m : 5 + (i + 1) * m] for i in range(2)]
    slope, prm = ins[5 + 2 * m :]
    _, gain, shift = params_of(prm, layer, 0)
    h = get_unit(unit_ref)[0] * gain + shift
    bias, gain, shift = params_of(prm, layer, 1)
    unit, r = norm_of(h + (f32(f) + f32(f_other) + bias))
    pick_features(sc[0] ^ sc[1], m, unit * gain + shift, scr[0])
    outs[0][...] = scr[0][...].T.astype(BF16)
    feed_back(f32(cotan), unit, r, gain, ws, slope, outs[1:])


def k_feed_back(m, layer, ins, outs, scr):
    dx, dx_other, da, full = ins[:4]
    ws = [ins[4 + i * m : 4 + (i + 1) * m] for i in range(2)]
    slope, prm = ins[4 + 2 * m :]
    _, gain, _ = params_of(prm, layer, 1)
    e = da[...] + (f32(dx) + f32(dx_other))
    unit, r = get_unit(full)
    feed_back(e, unit, r, gain, ws, slope, outs)


def k_attend_back(m, layer, ins, outs, scr):
    dh, dh_other, df, unit_ref = ins[:4]
    qkv, p, prm = ins[4 + m :]
    da_ref, low_ref, dx_ref, grads_ref, sums = outs
    _, gain, _ = params_of(prm, layer, 0)
    e = df[...] + (f32(dh) + f32(dh_other))
    unit, r = get_unit(unit_ref)
    da = norm_back(e, unit, r, gain)
    low = da.astype(BF16)
    da_ref[...] = da
    low_ref[...] = low
    put_sums(sums, e, unit, low)
    w = rows_of(ins[4 : 4 + m])
    grads = attend_back(low, w, qkv, p)
    grads_ref[...] = grads
    dx_ref[...] = heads_back(grads, w).astype(BF16)


def k_attend_back_last(n, m, ins, outs, scr):
    sc, dh, dh_other, df, unit_ref = ins[:5]
    qkv, p, prm = ins[5 + m :]
    low_ref, grads_ref, sums = outs[n:]
    _, gain, _ = params_of(prm, 0, 0)
    e = df[...] + (f32(dh) + f32(dh_other))
    unit, r = get_unit(unit_ref)
    da = norm_back(e, unit, r, gain)
    low = da.astype(BF16)
    low_ref[...] = low
    put_sums(sums, e, unit, low)
    w = rows_of(ins[5 : 5 + m])
    grads = attend_back(low, w, qkv, p)
    grads_ref[...] = grads
    dx = heads_back(grads, w)
    place = sc[0] ^ sc[1]
    piece = outs[0].shape[1]
    low_dx = dx.astype(BF16)
    for j in range(m):

        @pl.when(place == j)
        def _():
            outs[0][...] = (da + dx)[:, j * piece : (j + 1) * piece]
            for k in range(1, n):
                at = (j ^ k) * piece
                outs[k][...] = low_dx[:, at : at + piece]


def k_total(ins, outs, scr):
    piece = ins[0].shape[1]
    total = ins[0][...] + ((f32(ins[1]) + f32(ins[2])) + f32(ins[3]))
    outs[0][:piece, :] = total.T.astype(BF16)
    outs[0][piece:, :] = ins[4][...]


def k_feed_weight(m, ins, outs, scr):
    low, g, h, du = ins
    keep, send, sums = outs
    split_blocks(t_dot(low[...], g[...]), m, 0, 2, keep, send)
    split_blocks(t_dot(h[...], du[...]), m, 1, 2, keep, send)
    sums[0:1, :] = jnp.sum(f32(du), axis=0, keepdims=True)
    sums[1:8, :] = jnp.zeros((7, sums.shape[1]), F32)


def k_attend_weight(m, ins, outs, scr):
    x, grads, low, o = ins[:4]
    keep, send, sums = outs
    first = t_dot(x[...], grads[...])
    second = t_dot(low[...], o[...])
    split_blocks(jnp.concatenate([first, second], axis=1), m, 0, 1, keep, send)
    sums[...] = jnp.zeros(sums.shape, F32)
    sums[0:1, : grads.shape[1]] = jnp.sum(f32(grads), axis=0, keepdims=True)


def k_attend_weight_last(m, ins, outs, scr):
    x, grads, low, o = ins[:4]
    hidden_sums, head_sums, norm_sums = ins[4:6], ins[6], ins[7:]
    keep, send = outs
    first = t_dot(x[...], grads[...])
    second = t_dot(low[...], o[...])
    split_blocks(jnp.concatenate([first, second], axis=1), m, 0, 1, keep, send)
    model = x.shape[1]
    piece = model // m
    width = grads.shape[1]
    own = jnp.sum(f32(grads), axis=0, keepdims=True)
    own = jnp.concatenate([own, jnp.zeros((1, model - width), F32)], axis=1)
    common = [r[0:1, :] for r in hidden_sums] + [own, head_sums[0:1, :]]
    common = jnp.concatenate(common, axis=0)
    each = jnp.concatenate([r[0:3, :] for r in norm_sums], axis=0)
    rows = keep.shape[0] // 2
    for k in range(m):
        target = send if k % 2 else keep
        start = (k // 2) * rows + piece
        block = jnp.concatenate(
            [each[:, k * piece : (k + 1) * piece], jnp.zeros((each.shape[0], model - piece), F32)],
            axis=1,
        )
        target[start : start + 16, :] = jnp.concatenate([common, block], axis=0).astype(BF16)


def k_middle(ins, outs, scr):
    keep, got = ins
    total = f32(keep) + f32(got)
    at = 0
    for out in outs:
        out[...] = total[at : at + out.shape[0]].astype(BF16)
        at += out.shape[0]


def k_add(ins, outs, scr):
    count = len(ins) // 2
    at = 0
    for first, second in zip(ins[:count], ins[count:]):
        rows = first.shape[0]
        outs[0][at : at + rows, :] = (f32(first) + f32(second)).astype(BF16)
        at += rows


def k_add_whole(ins, outs, scr):
    at = 0
    for ref in ins[:3]:
        outs[0][at : at + ref.shape[0], :] = ref[...]
        at += ref.shape[0]
    at = 0
    for ref in ins[3:]:
        rows = ref.shape[0]
        total = f32(outs[0].at[at : at + rows]) + f32(ref)
        outs[0][at : at + rows, :] = total.astype(BF16)
        at += rows


def k_feed_output(ins, outs, scr):
    half = ins[0].shape[0]
    for layer in range(2):
        for j in range(2):
            total = f32(ins[2 * layer + j]) + f32(ins[4 + 2 * layer + j])
            outs[0][layer, j * half : (j + 1) * half, :] = total


def with_token(kernel, ins, outs, scr):
    kernel(ins, outs[:-1], scr)
    outs[-1][...] = jnp.zeros(outs[-1].shape, F32)


def k_attend_outputs(ins, outs, scr):
    grad_w, qv, b_out, gains, shifts, b_up, b_down = outs
    piece = grad_w.shape[1]
    total = f32(ins[0]) + f32(ins[1])
    grad_w[0] = total[:piece]
    half = piece // 2
    grad_w[1, :half, :] = f32(ins[2]) + f32(ins[4])
    grad_w[1, half:, :] = f32(ins[3]) + f32(ins[5])
    small = total[piece:]
    b_up[...] = small[0:2]
    for layer in range(2):
        heads = small[2 + layer : 3 + layer]
        qv[layer, 0:1, :] = heads[:, :piece]
        qv[layer, 1:2, :] = heads[:, 2 * piece : 3 * piece]
        at = 4 + 6 * layer
        b_out[layer : layer + 1, :] = small[at + 2 : at + 3, :piece]
        b_down[layer : layer + 1, :] = small[at + 5 : at + 6, :piece]
        for which in range(2):
            start = at + 3 * which
            gains[layer, which : which + 1, :] = small[start : start + 1, :piece]
            shifts[layer, which : which + 1, :] = small[start + 1 : start + 2, :piece]


def per_device(
    hidden_in, lengths, w_attn, b_qv, b_out, ln_gain, ln_bias, w_up, b_up, w_down, b_down, cotangent
):
    layers = w_attn.shape[0]
    n, m = lax.axis_size("row"), lax.axis_size("col")
    tokens, piece = hidden_in.shape
    model = piece * m
    hidden = w_up.shape[2]
    width = w_attn.shape[2] // 4
    heads = width // HEAD_DIM
    sc = lengths

    tile = (tokens, model)

    def layer_of(array, layer):
        return (array, (1,) + array.shape[1:], (layer, 0, 0))

    half_block, low_block = sds((piece // 2, hidden), BF16), sds((piece, hidden), BF16)

    def pack(rows, arrays, after=()):
        return call(k_pack, [sds((rows, hidden), BF16)], arrays, after=after, final=True)[0]

    def held(arrays, after):
        return [
            call(k_pack, [sds(a.shape, a.dtype)], [whole(a)], after=after, final=True)[0]
            for a in arrays
        ]

    def along_of(arrays):
        return [exchange(a, "col", 2) for a in arrays]

    def gathered(own, along, rows=piece, after=()):
        both = pack(2 * rows, [whole(a) for a in [*own, *along]], after)
        near = exchange(both, "col", 1)
        views = [(both, 0), (near, 0), (both, 1), (near, 1)]
        return [(a, (rows, hidden), (i, 0)) for a, i in views]

    def pair_sum(value, after=()):
        return call(k_sum, [low_tile], [value, exchange(value, "row", 1)], after=after)[0]

    def both(value):
        return [value, exchange(value, "row", 2)]

    smalls = [b_out, b_down, ln_gain, ln_bias, b_up, b_qv]
    block, rowwise, mine = call(
        k_start,
        [sds((piece + 16, hidden), BF16), sds((16, hidden), BF16), sds((tokens, piece), BF16)],
        [layer_of(w_attn, 0), whole(hidden_in.T), *[[a] for a in smalls]],
        [pltpu.VMEM(a.shape, a.dtype) for a in smalls] + [pltpu.SemaphoreType.DMA((6,))],
        final=True,
        vmem_mib=60,
    )
    along = exchange(block, "col", 2)
    mine = turned(mine)
    x_in = [mine] + [exchange(mine, "row", k) for k in range(1, n)]
    (x,) = call(k_prep, [sds(tile, BF16)], [sc, *x_in])
    weights = [whole(a) for a in (w_attn, w_up, w_down)]
    halves = call(k_split, [half_block] * 8, weights, after=x_in[1:], final=True)
    down0, attn1, up1, down1 = [halves[2 * i : 2 * i + 2] for i in range(4)]
    up0 = pack(piece, [layer_of(w_up, 0)], [mine])
    (up0_along,) = along_of([up0])
    near = exchange(block, "col", 1)
    (low,) = held([along], [*x_in[1:], up0_along])
    sources = (block, near, along, exchange(low, "col", 1))
    attn0 = [(a, (piece + 16, hidden), (0, 0)) for a in sources]

    low_tile = sds(tile, BF16)
    unit_out = sds((tokens, model + 128), F32)
    qkv_out, p_out, o_out = (
        sds((tokens, 3 * width), BF16),
        sds((heads, tokens, tokens), F32),
        sds((tokens, width), BF16),
    )
    g_out, slope_out = sds((tokens, hidden), BF16), sds((tokens, hidden), F32)
    feed_out = [low_tile, unit_out, low_tile, g_out, slope_out]

    z, prm, o0, qkv0, p0 = call(
        partial(k_attend_first, m),
        [low_tile, sds((16, model), F32), o_out, qkv_out, p_out],
        [sc, x, *attn0, rowwise],
        after=[down0[0]],
    )
    down0_along = along_of(down0)
    (low,) = call(k_turned, [sds((tokens, piece), BF16)], [whole(cotangent.T)], after=[z], final=True)
    cotan = turned(low)
    z = pair_sum(z, down0_along)
    up0 = gathered([up0], [up0_along], after=[z])
    down0 = gathered(down0, down0_along, after=[z])
    attn1_along = along_of(attn1)
    f, unit_a0, h0, g0, slope0 = call(
        partial(k_feed, m, 0),
        feed_out,
        [*both(z), x, *up0, *down0, rowwise, prm],
        after=attn1_along,
    )
    attn1 = gathered(attn1, attn1_along, after=[f])
    up1_along = along_of(up1[:1])
    f = pair_sum(f, [attn1[1][0], *up1_along])
    up1_along += along_of(up1[1:])
    down1_along = along_of(down1[:1])
    z, unit_b0, x1, o1, qkv1, p1 = call(
        partial(k_attend, m, 1),
        [low_tile, unit_out, low_tile, o_out, qkv_out, p_out],
        [sc, *both(f), unit_a0, *attn1, rowwise, prm],
        after=[up1_along[1], *down1_along],
    )
    down1_along += along_of(down1[1:])
    up1 = gathered(up1, up1_along, after=[z])
    z = pair_sum(z, [down1_along[1], up1[1][0]])
    down1 = gathered(down1, down1_along, after=[z])
    f, unit_a1, h1, g1, slope1 = call(
        partial(k_feed, m, 1),
        feed_out,
        [*both(z), unit_b0, *up1, *down1, rowwise, prm],
        after=[cotan],
    )
    (again,) = held([cotan], [f])
    cotan = [cotan, None] + [exchange(again, "row", k) for k in range(2, n)]
    f = pair_sum(f, cotan[2:])
    cotan[1] = exchange(held([again], [f])[0], "row", 1)
    (cotan,) = call(k_prep, [sds(tile, BF16)], [sc, *cotan], after=[f])

    sums_out = sds((8, model), F32)
    feed_back_out = [sds(tile, F32), low_tile, low_tile, sds((tokens, hidden), BF16), sums_out]
    out, df, df_low, dh, du, sums_b1 = call(
        partial(k_turn, m, 1),
        [sds((piece, tokens), BF16)] + feed_back_out,
        [sc, *both(f), unit_a1, cotan, *up1, *down1, slope1, prm],
        [pltpu.VMEM((tokens, piece), F32)],
    )
    weight_out = [sds((4 * piece, hidden), BF16)] * 2 + [sds((8, hidden), F32)]
    keep, send, hidden_sums1 = call(
        partial(k_feed_weight, m), weight_out, [df_low, g1, h1, du]
    )
    got = exchange(send, "col", 1)
    dh = pair_sum(dh, [got])
    stay1 = call(k_middle, [half_block] * 8, [keep, got], after=[dh])
    more1 = along_of(stay1[4:6])
    da, da_low, dx, grads1, sums_a1 = call(
        partial(k_attend_back, m, 1),
        [sds(tile, F32), low_tile, low_tile, qkv_out, sums_out],
        [*both(dh), df, unit_a1, *attn1, qkv1, p1, prm],
        after=more1,
    )
    keep, send, head_sums1 = call(
        partial(k_attend_weight, m),
        [sds((2 * piece, 4 * width), BF16)] * 2 + [sums_out],
        [x1, grads1, da_low, o1],
    )
    got = exchange(send, "col", 1)
    more1 += along_of(held(stay1[6:7], [dx]))
    (low,) = call(k_add, [half_block], [stay1[0], more1[0]], after=[dx])
    terms1 = [last_of_dp(low)]
    dx = pair_sum(dx, [got, more1[2], terms1[0][1]])
    attn1_stay = call(k_middle, [half_block] * 4, [keep, got], after=[dx])
    more1 += along_of(held(stay1[7:], [dx]))
    attn1_more = along_of(attn1_stay[2:3])
    for i in (1, 2):
        (low,) = call(k_add, [half_block], [stay1[i], more1[i]], after=[dx])
        terms1 += [last_of_dp(low)]

    df, df_low, dh, du, sums_b0 = call(
        partial(k_feed_back, m, 0),
        feed_back_out,
        [*both(dx), da, unit_b0, *up0, *down0, slope0, prm],
        after=[more1[3], *attn1_more, terms1[1][1], terms1[2][1]],
    )
    keep, send, hidden_sums0 = call(
        partial(k_feed_weight, m), weight_out, [df_low, g0, h0, du]
    )
    got = exchange(send, "col", 1)
    attn1_more += along_of(held(attn1_stay[3:], [dh]))
    (low,) = call(k_add, [half_block], [stay1[3], more1[3]], after=[dh])
    terms1 += [last_of_dp(low)]
    dh = pair_sum(dh, [got, attn1_more[1], terms1[3][1]])
    stay0 = call(
        k_middle, [half_block] * 4 + [low_block] + [half_block] * 2, [keep, got], after=[dh]
    )
    more0 = along_of(stay0[4:6])
    attn1_terms = []
    for i in range(2):
        (low,) = call(k_add, [half_block], [attn1_stay[i], attn1_more[i]], after=[dh])
        attn1_terms.append(last_of_dp(low))
    *dx, low_last, grads0, sums_a0 = call(
        partial(k_attend_back_last, n, m),
        [sds((tokens, piece), F32)]
        + [sds((tokens, piece), BF16)] * (n - 1)
        + [low_tile, qkv_out, sums_out],
        [sc, *both(dh), df, unit_a0, *attn0, qkv0, p0, prm],
        after=[*more0, attn1_terms[0][1], attn1_terms[1][1]],
    )
    more0 += along_of(held(stay0[6:], [dx[0]]))
    most = [sds((3 * piece // 2, hidden), BF16)]
    (low,) = call(k_add_whole, most, [*stay0[:3], *more0[:2]])
    most0_terms = last_of_dp(low)
    (results,) = call(
        k_total,
        [sds((2 * piece, tokens), BF16)],
        [dx[0]] + [exchange(dx[k], "row", k) for k in range(1, n)] + [out],
    )
    out_hidden, grad_input, token = call(
        k_results,
        [sds((piece, tokens), BF16), sds((piece, tokens), F32), sds((8, 128), F32)],
        [turned(results)],
        final=2,
    )

    keep, send = call(
        partial(k_attend_weight_last, m),
        [sds((2 * (piece + 16), 4 * width), BF16)] * 2,
        [
            x,
            grads0,
            low_last,
            o0,
            hidden_sums0,
            hidden_sums1,
            head_sums1,
            sums_a0,
            sums_b0,
            sums_a1,
            sums_b1,
        ],
    )
    got = exchange(send, "col", 1)
    low_tail = sds((piece + 16, hidden), BF16)
    attn0_stay, attn0_go = call(k_middle, [low_tail] * 2, [keep, got])
    (attn0_more,) = along_of([attn0_go])
    (low,) = call(k_add, [half_block], [stay0[3], more0[2]])
    rest0_terms = last_of_dp(low)
    (low,) = call(k_add, [low_tail], [attn0_stay, attn0_more], after=[results])
    attn0_terms = [last_of_dp(low)]
    def halves_of(array):
        return [(array, (piece // 2, hidden), (i, 0)) for i in range(3)]

    first = [halves_of(a) + [b] for a, b in zip(most0_terms, rest0_terms)]
    second = [[t[side] for t in terms1] for side in range(2)]
    def feed_terms(which):
        return [
            halves[2 * which + j]
            for side in range(2)
            for halves in (first[side], second[side])
            for j in range(2)
        ]

    mark = sds((8, 128), F32)
    feed_grad = sds((layers, piece, hidden), F32)
    grad_down, down_token = call(
        partial(with_token, k_feed_output),
        [feed_grad, mark],
        feed_terms(0),
        after=[token],
        final=1,
    )
    (
        grad_attn,
        grad_qv,
        grad_out,
        grad_gain,
        grad_shift,
        grad_b_up,
        grad_b_down,
        attend_token,
    ) = call(
        partial(with_token, k_attend_outputs),
        [sds(a.shape, F32) for a in (w_attn, b_qv, b_out, ln_gain, ln_bias, b_up, b_down)]
        + [mark],
        [t[side] for terms in (attn0_terms, attn1_terms) for side in range(2) for t in terms],
        after=[down_token],
        final=7,
    )
    (grad_up,) = call(
        k_feed_output, [feed_grad], feed_terms(1), after=[attend_token], final=True
    )
    return (
        out_hidden.T,
        grad_input.T,
        grad_attn,
        grad_qv,
        grad_out,
        grad_gain,
        grad_shift,
        grad_up,
        grad_b_up,
        grad_down,
        grad_b_down,
    )


def solution(mesh):
    in_specs = (
        P(("dp", "row"), "col"),
        P("dp"),
        P(None, "col", "row"),
        P(None, None, "row"),
        P(None, "col"),
        P(None, None, "col"),
        P(None, None, "col"),
        P(None, "col", "row"),
        P(None, "row"),
        P(None, "col", "row"),
        P(None, "col"),
        P(("dp", "row"), "col"),
    )
    out_specs = (
        P(("dp", "row"), "col"),
        P(("dp", "row"), "col"),
        P(None, "col", "row"),
        P(None, None, "row"),
        P(None, "col"),
        P(None, None, "col"),
        P(None, None, "col"),
        P(None, "col", "row"),
        P(None, "row"),
        P(None, "col", "row"),
        P(None, "col"),
    )
    return jax.shard_map(
        per_device, mesh=mesh, in_specs=in_specs, out_specs=out_specs, check_vma=False
    )
```

```python
import math
from functools import partial

import jax
import jax.numpy as jnp
from jax import lax
from jax.experimental import pallas as pl
from jax.experimental.pallas import tpu as pltpu
from jax.sharding import PartitionSpec as P


HEAD_DIM = 64
EPS = 1e-5
MASKED = -1e30
F32 = jnp.float32
BF16 = jnp.bfloat16


def exchange(x, axis, bit):
    n = lax.axis_size(axis)
    return lax.ppermute(x, axis, [(i, i ^ bit) for i in range(n)])


def turned(x):
    n = lax.axis_size("row")
    pairs = [(a * n + b, b * n + a) for a in range(n) for b in range(n)]
    return lax.ppermute(x, ("row", "col"), pairs)


def last_of_dp(low):
    bit = 1
    while 2 * bit < lax.axis_size("dp"):
        low = (low.astype(F32) + exchange(low, "dp", bit).astype(F32)).astype(BF16)
        bit *= 2
    return low, exchange(low, "dp", bit)


def sds(shape, dtype):
    return jax.ShapeDtypeStruct(shape, dtype)


def whole(array):
    return (array, array.shape, (0,) * array.ndim)


def call(kernel, outs, ins, scratch=(), after=(), final=False, vmem_mib=32):
    vmem = pl.BlockSpec(memory_space=pltpu.VMEM)
    specs, args = [], []
    moved = 0
    for item in ins:
        if isinstance(item, tuple):
            array, shape, index = item
            specs.append(pl.BlockSpec(shape, lambda i, index=index: index))
            moved += math.prod(shape) * array.dtype.itemsize
            args.append(array)
            continue
        if isinstance(item, list):
            args.append(item[0])
            specs.append(pl.BlockSpec(memory_space=pltpu.HBM))
            continue
        args.append(item)
        if item.dtype == jnp.int32:
            specs.append(pl.BlockSpec(memory_space=pltpu.SMEM))
        else:
            specs.append(vmem)
            moved += item.size * item.dtype.itemsize
    moved += sum(o.size * o.dtype.itemsize for o in outs)
    n_in, n_after, n_out = len(ins), len(after), len(outs)
    final = n_out if final is True else final

    def body(*refs):
        inputs = list(refs[:n_in])
        if args[0].dtype == jnp.int32:
            col = lax.axis_index("col")
            inputs[0] = (lax.axis_index("row"), col, refs[0][col])
        kernel(
            inputs,
            refs[n_in + n_after : n_in + n_after + n_out],
            refs[n_in + n_after + n_out :],
        )

    return pl.pallas_call(
        body,
        grid=(1,),
        out_shape=outs,
        in_specs=specs + [pl.BlockSpec(memory_space=pl.ANY)] * n_after,
        out_specs=[
            pl.BlockSpec(o.shape, lambda i, d=len(o.shape): (0,) * d)
            if final and i < final
            else vmem
            for i, o in enumerate(outs)
        ],
        scratch_shapes=list(scratch),
        compiler_params=pltpu.CompilerParams(vmem_limit_bytes=vmem_mib * 1024 * 1024),
        cost_estimate=pl.CostEstimate(
            flops=200_000_000, bytes_accessed=moved, transcendentals=0
        ),
    )(*args, *after)


def rows_of(refs):
    rows = refs[0].shape[0] // 64 * 64
    return jnp.concatenate([r[:rows, :] for r in refs], axis=0)


def dot(a, b):
    return jnp.dot(a, b, preferred_element_type=F32)


def dot_t(a, b):
    return lax.dot_general(a, b, (((1,), (1,)), ((), ())), preferred_element_type=F32)


def t_dot(a, b):
    return lax.dot_general(a, b, (((0,), (0,)), ((), ())), preferred_element_type=F32)


def f32(ref):
    return ref[...].astype(F32)


def tree(refs):
    values = [f32(r) for r in refs]
    while len(values) > 1:
        values = [values[i] + values[i + 1] for i in range(0, len(values), 2)]
    return values[0]


def params_of(prm, layer, which):
    rows = (2 * which + layer, 4 + 2 * layer + which, 8 + 2 * layer + which)
    return [prm[i : i + 1, :] for i in rows]


def norm_of(v):
    mean = jnp.mean(v, axis=-1, keepdims=True)
    centred = v - mean
    r = lax.rsqrt(jnp.mean(centred * centred, axis=-1, keepdims=True) + EPS)
    return centred * r, r


def norm_back(e, unit, r, gain):
    c = e * gain
    return r * (
        c
        - jnp.mean(c, axis=-1, keepdims=True)
        - unit * jnp.mean(c * unit, axis=-1, keepdims=True)
    )


def put_unit(ref, unit, r):
    model = unit.shape[1]
    ref[:, :model] = unit
    ref[:, model:] = jnp.broadcast_to(r, (unit.shape[0], 128))


def get_unit(ref):
    model = ref.shape[1] - 128
    return ref[:, :model], ref[:, model : model + 1]


def put_sums(ref, e, unit, low):
    ref[0:1, :] = jnp.sum(e * unit, axis=0, keepdims=True)
    ref[1:2, :] = jnp.sum(e, axis=0, keepdims=True)
    ref[2:3, :] = jnp.sum(low.astype(F32), axis=0, keepdims=True)
    ref[3:8, :] = jnp.zeros((5, ref.shape[1]), F32)


def place_features(sc, pieces, target):
    place = sc[0] ^ sc[1]
    width = pieces[0].shape[1]
    for k, piece in enumerate(pieces):
        for j in range(len(pieces)):

            @pl.when((place ^ k) == j)
            def _():
                target[:, j * width : (j + 1) * width] = piece[...].astype(target.dtype)


def pick_features(at, count, value, target):
    width = value.shape[1] // count
    for j in range(count):

        @pl.when(at == j)
        def _():
            target[...] = value[:, j * width : (j + 1) * width].astype(target.dtype)


def project(sc, layer, x, w, rowwise, qkv_ref, p_ref):
    tokens = x.shape[0]
    width = w.shape[1] // 4
    b = rowwise[2 + layer : 3 + layer, : 2 * width].astype(F32)
    shift = jnp.concatenate([b[:, :width], jnp.zeros((1, width), F32), b[:, width:]], axis=1)
    qkv = (dot(x, w[:, : 3 * width]) + shift).astype(BF16)
    qkv_ref[...] = qkv
    visible = lax.broadcasted_iota(jnp.int32, (tokens, tokens), 1) < sc[2]
    mixed = []
    for h in range(width // HEAD_DIM):
        q = qkv[:, h * HEAD_DIM : (h + 1) * HEAD_DIM]
        k = qkv[:, width + h * HEAD_DIM : width + (h + 1) * HEAD_DIM]
        v = qkv[:, 2 * width + h * HEAD_DIM : 2 * width + (h + 1) * HEAD_DIM]
        s = jnp.where(visible, dot_t(q, k) * HEAD_DIM ** (-0.5), MASKED)
        e = jnp.exp(s - jnp.max(s, axis=-1, keepdims=True))
        p = e / jnp.sum(e, axis=-1, keepdims=True)
        p_ref[h] = p
        mixed.append(dot(p.astype(BF16), v))
    return jnp.concatenate(mixed, axis=1).astype(BF16)


def mix_out(o, w):
    return dot_t(o, w[:, 3 * (w.shape[1] // 4) :])


def attend_back(d, w, qkv_ref, p_ref):
    width = w.shape[1] // 4
    do = dot(d, w[:, 3 * width :]).astype(BF16)
    qkv = qkv_ref[...]
    dq, dk, dv = [], [], []
    for h in range(width // HEAD_DIM):
        q = qkv[:, h * HEAD_DIM : (h + 1) * HEAD_DIM]
        k = qkv[:, width + h * HEAD_DIM : width + (h + 1) * HEAD_DIM]
        v = qkv[:, 2 * width + h * HEAD_DIM : 2 * width + (h + 1) * HEAD_DIM]
        g = do[:, h * HEAD_DIM : (h + 1) * HEAD_DIM]
        p = p_ref[h]
        dv.append(t_dot(p.astype(BF16), g))
        dp = dot_t(g, v)
        ds = (p * (dp - jnp.sum(p * dp, axis=-1, keepdims=True))).astype(BF16)
        dq.append(dot(ds, k) * HEAD_DIM ** (-0.5))
        dk.append(t_dot(ds, q) * HEAD_DIM ** (-0.5))
    return jnp.concatenate(dq + dk + dv, axis=1).astype(BF16)


def heads_back(low, w):
    return dot_t(low, w[:, : 3 * (w.shape[1] // 4)])


def raise_hidden(layer, h, up, rowwise):
    u = dot(h, up) + rowwise[layer : layer + 1, :].astype(F32)
    cdf = 0.5 * (1.0 + lax.erf(u * (0.5**0.5)))
    slope = cdf + u * (jnp.exp(-0.5 * u * u) * 0.3989422804014327)
    return (u * cdf).astype(BF16), slope


def split_blocks(grad, count, part, parts, keep, send):
    block = grad.shape[0] // count
    each = keep.shape[0] // (2 * parts)
    for k in range(count):
        target = send if k % 2 else keep
        start = ((k // 2) * parts + part) * each
        target[start : start + block, :] = grad[k * block : (k + 1) * block].astype(BF16)


def k_start(ins, outs, scr):
    attn, hidden_in, small = ins[0], ins[1], scr[:-1]
    block, rowwise, x = outs
    fetched = [
        pltpu.make_async_copy(a, b, scr[-1].at[i]) for i, (a, b) in enumerate(zip(ins[2:], small))
    ]
    for copy in fetched:
        copy.start()
    rows = attn.shape[1]
    block[:rows, :] = attn[0]
    x[...] = hidden_in[...].astype(F32).T.astype(BF16)
    for copy in fetched:
        copy.wait()
    b_out, b_down, gain, shift, b_up, b_qv = small
    piece = b_out.shape[1]
    norms = [b_out[...], b_down[...], gain[0], gain[1], shift[0], shift[1]]
    norms = jnp.concatenate([x.astype(F32) for x in norms] + [jnp.zeros((4, piece), F32)], axis=0)
    block[rows:, :piece] = norms.astype(BF16)
    block[rows:, piece:] = jnp.zeros((16, block.shape[1] - piece), BF16)
    qv = [b_qv[i].astype(F32) for i in range(2)]
    qv = [jnp.concatenate([x[0:1], x[1:2]], axis=1) for x in qv]
    rest = b_up.shape[1] - qv[0].shape[1]
    qv = jnp.concatenate([jnp.concatenate(qv, axis=0), jnp.zeros((2, rest), F32)], axis=1)
    low = jnp.concatenate([b_up[...].astype(F32), qv, jnp.zeros((12, b_up.shape[1]), F32)], axis=0)
    rowwise[...] = low.astype(BF16)


def k_results(ins, outs, scr):
    piece = outs[0].shape[0]
    outs[0][...] = ins[0][piece:, :]
    outs[1][...] = ins[0][:piece, :].astype(F32)
    outs[2][...] = jnp.zeros(outs[2].shape, F32)


def k_split(ins, outs, scr):
    attn, up, down = ins
    half = outs[0].shape[0]
    for i, (ref, layer) in enumerate(((down, 0), (attn, 1), (up, 1), (down, 1))):
        for j in range(2):
            outs[2 * i + j][...] = ref[layer, j * half : (j + 1) * half, :]


def k_pack(ins, outs, scr):
    at = 0
    for ref in ins:
        value = ref[0] if len(ref.shape) == 3 else ref[...]
        outs[0][at : at + value.shape[0], :] = value
        at += value.shape[0]


def k_turned(ins, outs, scr):
    outs[0][...] = ins[0][...].astype(F32).T.astype(BF16)


def k_prep(ins, outs, scr):
    sc, *pieces = ins
    place_features(sc, pieces, outs[0])


def k_sum(ins, outs, scr):
    outs[0][...] = (f32(ins[0]) + f32(ins[1])).astype(BF16)


def k_attend_first(m, ins, outs, scr):
    sc, x = ins[:2]
    w_refs, rowwise = ins[2 : 2 + m], ins[2 + m]
    z_ref, prm, o_ref, qkv, p = outs
    piece = w_refs[0].shape[0] - 16
    prm[...] = jnp.concatenate([w[piece:, :piece].astype(F32) for w in w_refs], axis=1)
    w = rows_of(w_refs)
    o = project(sc, 0, x[...], w, rowwise, qkv, p)
    o_ref[...] = o
    z_ref[...] = mix_out(o, w).astype(BF16)


def k_feed(m, layer, ins, outs, scr):
    z, z_other, base = ins[:3]
    up, down = ins[3 : 3 + m], ins[3 + m : 3 + 2 * m]
    rowwise, prm = ins[3 + 2 * m :]
    f_ref, unit_ref, h_ref, g_ref, slope_ref = outs
    if layer:
        _, gain, shift = params_of(prm, layer - 1, 1)
        x = get_unit(base)[0] * gain + shift
    else:
        x = f32(base)
    bias, gain, shift = params_of(prm, layer, 0)
    unit, r = norm_of(x + (f32(z) + f32(z_other) + bias))
    put_unit(unit_ref, unit, r)
    h = (unit * gain + shift).astype(BF16)
    h_ref[...] = h
    g, slope = raise_hidden(layer, h, rows_of(up), rowwise)
    g_ref[...] = g
    slope_ref[...] = slope
    f_ref[...] = dot_t(g, rows_of(down)).astype(BF16)


def k_attend(m, layer, ins, outs, scr):
    sc, f, f_other, unit_ref = ins[:4]
    own = ins[4 : 4 + m]
    rowwise, prm = ins[4 + m :]
    z_ref, unit_out, x_ref, o_ref, qkv, p = outs
    _, gain, shift = params_of(prm, layer - 1, 0)
    h = get_unit(unit_ref)[0] * gain + shift
    bias, gain, shift = params_of(prm, layer - 1, 1)
    unit, r = norm_of(h + (f32(f) + f32(f_other) + bias))
    put_unit(unit_out, unit, r)
    x = (unit * gain + shift).astype(BF16)
    x_ref[...] = x
    w = rows_of(own)
    o = project(sc, layer, x, w, rowwise, qkv, p)
    o_ref[...] = o
    z_ref[...] = mix_out(o, w).astype(BF16)


def feed_back(e, unit, r, gain, ws, slope, outs):
    up, down = ws
    df_ref, low_ref, dh_ref, du_ref, sums = outs
    df = norm_back(e, unit, r, gain)
    low = df.astype(BF16)
    df_ref[...] = df
    low_ref[...] = low
    put_sums(sums, e, unit, low)
    du = (dot(low, rows_of(down)) * slope[...]).astype(BF16)
    du_ref[...] = du
    dh_ref[...] = dot_t(du, rows_of(up)).astype(BF16)


def k_turn(m, layer, ins, outs, scr):
    sc, f, f_other, unit_ref, cotan = ins[:5]
    ws = [ins[5 + i * m : 5 + (i + 1) * m] for i in range(2)]
    slope, prm = ins[5 + 2 * m :]
    _, gain, shift = params_of(prm, layer, 0)
    h = get_unit(unit_ref)[0] * gain + shift
    bias, gain, shift = params_of(prm, layer, 1)
    unit, r = norm_of(h + (f32(f) + f32(f_other) + bias))
    pick_features(sc[0] ^ sc[1], m, unit * gain + shift, scr[0])
    outs[0][...] = scr[0][...].T.astype(BF16)
    feed_back(f32(cotan), unit, r, gain, ws, slope, outs[1:])


def k_feed_back(m, layer, ins, outs, scr):
    dx, dx_other, da, full = ins[:4]
    ws = [ins[4 + i * m : 4 + (i + 1) * m] for i in range(2)]
    slope, prm = ins[4 + 2 * m :]
    _, gain, _ = params_of(prm, layer, 1)
    e = da[...] + (f32(dx) + f32(dx_other))
    unit, r = get_unit(full)
    feed_back(e, unit, r, gain, ws, slope, outs)


def k_attend_back(m, layer, ins, outs, scr):
    dh, dh_other, df, unit_ref = ins[:4]
    qkv, p, prm = ins[4 + m :]
    da_ref, low_ref, dx_ref, grads_ref, sums = outs
    _, gain, _ = params_of(prm, layer, 0)
    e = df[...] + (f32(dh) + f32(dh_other))
    unit, r = get_unit(unit_ref)
    da = norm_back(e, unit, r, gain)
    low = da.astype(BF16)
    da_ref[...] = da
    low_ref[...] = low
    put_sums(sums, e, unit, low)
    w = rows_of(ins[4 : 4 + m])
    grads = attend_back(low, w, qkv, p)
    grads_ref[...] = grads
    dx_ref[...] = heads_back(grads, w).astype(BF16)


def k_attend_back_last(n, m, ins, outs, scr):
    sc, dh, dh_other, df, unit_ref = ins[:5]
    qkv, p, prm = ins[5 + m :]
    low_ref, grads_ref, sums = outs[n:]
    _, gain, _ = params_of(prm, 0, 0)
    e = df[...] + (f32(dh) + f32(dh_other))
    unit, r = get_unit(unit_ref)
    da = norm_back(e, unit, r, gain)
    low = da.astype(BF16)
    low_ref[...] = low
    put_sums(sums, e, unit, low)
    w = rows_of(ins[5 : 5 + m])
    grads = attend_back(low, w, qkv, p)
    grads_ref[...] = grads
    dx = heads_back(grads, w)
    place = sc[0] ^ sc[1]
    piece = outs[0].shape[1]
    low_dx = dx.astype(BF16)
    for j in range(m):

        @pl.when(place == j)
        def _():
            outs[0][...] = (da + dx)[:, j * piece : (j + 1) * piece]
            for k in range(1, n):
                at = (j ^ k) * piece
                outs[k][...] = low_dx[:, at : at + piece]


def k_total(ins, outs, scr):
    piece = ins[0].shape[1]
    total = ins[0][...] + ((f32(ins[1]) + f32(ins[2])) + f32(ins[3]))
    outs[0][:piece, :] = total.T.astype(BF16)
    outs[0][piece:, :] = ins[4][...]


def k_feed_weight(m, ins, outs, scr):
    low, g, h, du = ins
    keep, send, sums = outs
    split_blocks(t_dot(low[...], g[...]), m, 0, 2, keep, send)
    split_blocks(t_dot(h[...], du[...]), m, 1, 2, keep, send)
    sums[0:1, :] = jnp.sum(f32(du), axis=0, keepdims=True)
    sums[1:8, :] = jnp.zeros((7, sums.shape[1]), F32)


def k_attend_weight(m, ins, outs, scr):
    x, grads, low, o = ins[:4]
    keep, send, sums = outs
    first = t_dot(x[...], grads[...])
    second = t_dot(low[...], o[...])
    split_blocks(jnp.concatenate([first, second], axis=1), m, 0, 1, keep, send)
    sums[...] = jnp.zeros(sums.shape, F32)
    sums[0:1, : grads.shape[1]] = jnp.sum(f32(grads), axis=0, keepdims=True)


def k_attend_weight_last(m, ins, outs, scr):
    x, grads, low, o = ins[:4]
    hidden_sums, head_sums, norm_sums = ins[4:6], ins[6], ins[7:]
    keep, send = outs
    first = t_dot(x[...], grads[...])
    second = t_dot(low[...], o[...])
    split_blocks(jnp.concatenate([first, second], axis=1), m, 0, 1, keep, send)
    model = x.shape[1]
    piece = model // m
    width = grads.shape[1]
    own = jnp.sum(f32(grads), axis=0, keepdims=True)
    own = jnp.concatenate([own, jnp.zeros((1, model - width), F32)], axis=1)
    common = [r[0:1, :] for r in hidden_sums] + [own, head_sums[0:1, :]]
    common = jnp.concatenate(common, axis=0)
    each = jnp.concatenate([r[0:3, :] for r in norm_sums], axis=0)
    rows = keep.shape[0] // 2
    for k in range(m):
        target = send if k % 2 else keep
        start = (k // 2) * rows + piece
        block = jnp.concatenate(
            [each[:, k * piece : (k + 1) * piece], jnp.zeros((each.shape[0], model - piece), F32)],
            axis=1,
        )
        target[start : start + 16, :] = jnp.concatenate([common, block], axis=0).astype(BF16)


def k_middle(ins, outs, scr):
    keep, got = ins
    total = f32(keep) + f32(got)
    at = 0
    for out in outs:
        out[...] = total[at : at + out.shape[0]].astype(BF16)
        at += out.shape[0]


def k_add(ins, outs, scr):
    count = len(ins) // 2
    at = 0
    for first, second in zip(ins[:count], ins[count:]):
        rows = first.shape[0]
        outs[0][at : at + rows, :] = (f32(first) + f32(second)).astype(BF16)
        at += rows


def k_add_whole(ins, outs, scr):
    at = 0
    for ref in ins[:3]:
        outs[0][at : at + ref.shape[0], :] = ref[...]
        at += ref.shape[0]
    at = 0
    for ref in ins[3:]:
        rows = ref.shape[0]
        total = f32(outs[0].at[at : at + rows]) + f32(ref)
        outs[0][at : at + rows, :] = total.astype(BF16)
        at += rows


def k_feed_output(ins, outs, scr):
    half = ins[0].shape[0]
    for layer in range(2):
        for j in range(2):
            total = f32(ins[2 * layer + j]) + f32(ins[4 + 2 * layer + j])
            outs[0][layer, j * half : (j + 1) * half, :] = total


def with_token(kernel, ins, outs, scr):
    kernel(ins, outs[:-1], scr)
    outs[-1][...] = jnp.zeros(outs[-1].shape, F32)


def k_attend_outputs(ins, outs, scr):
    grad_w, qv, b_out, gains, shifts, b_up, b_down = outs
    piece = grad_w.shape[1]
    total = f32(ins[0]) + f32(ins[1])
    grad_w[0] = total[:piece]
    half = piece // 2
    grad_w[1, :half, :] = f32(ins[2]) + f32(ins[4])
    grad_w[1, half:, :] = f32(ins[3]) + f32(ins[5])
    small = total[piece:]
    b_up[...] = small[0:2]
    for layer in range(2):
        heads = small[2 + layer : 3 + layer]
        qv[layer, 0:1, :] = heads[:, :piece]
        qv[layer, 1:2, :] = heads[:, 2 * piece : 3 * piece]
        at = 4 + 6 * layer
        b_out[layer : layer + 1, :] = small[at + 2 : at + 3, :piece]
        b_down[layer : layer + 1, :] = small[at + 5 : at + 6, :piece]
        for which in range(2):
            start = at + 3 * which
            gains[layer, which : which + 1, :] = small[start : start + 1, :piece]
            shifts[layer, which : which + 1, :] = small[start + 1 : start + 2, :piece]


def per_device(
    hidden_in, lengths, w_attn, b_qv, b_out, ln_gain, ln_bias, w_up, b_up, w_down, b_down, cotangent
):
    layers = w_attn.shape[0]
    n, m = lax.axis_size("row"), lax.axis_size("col")
    tokens, piece = hidden_in.shape
    model = piece * m
    hidden = w_up.shape[2]
    width = w_attn.shape[2] // 4
    heads = width // HEAD_DIM
    sc = lengths

    tile = (tokens, model)

    def layer_of(array, layer):
        return (array, (1,) + array.shape[1:], (layer, 0, 0))

    half_block, low_block = sds((piece // 2, hidden), BF16), sds((piece, hidden), BF16)

    def pack(rows, arrays, after=()):
        return call(k_pack, [sds((rows, hidden), BF16)], arrays, after=after, final=True)[0]

    def held(arrays, after):
        return [
            call(k_pack, [sds(a.shape, a.dtype)], [whole(a)], after=after, final=True)[0]
            for a in arrays
        ]

    def along_of(arrays):
        return [exchange(a, "col", 2) for a in arrays]

    def gathered(own, along, rows=piece, after=()):
        both = pack(2 * rows, [whole(a) for a in [*own, *along]], after)
        near = exchange(both, "col", 1)
        views = [(both, 0), (near, 0), (both, 1), (near, 1)]
        return [(a, (rows, hidden), (i, 0)) for a, i in views]

    def pair_sum(value, after=()):
        return call(k_sum, [low_tile], [value, exchange(value, "row", 1)], after=after)[0]

    def both(value):
        return [value, exchange(value, "row", 2)]

    smalls = [b_out, b_down, ln_gain, ln_bias, b_up, b_qv]
    block, rowwise, mine = call(
        k_start,
        [sds((piece + 16, hidden), BF16), sds((16, hidden), BF16), sds((tokens, piece), BF16)],
        [layer_of(w_attn, 0), whole(hidden_in.T), *[[a] for a in smalls]],
        [pltpu.VMEM(a.shape, a.dtype) for a in smalls] + [pltpu.SemaphoreType.DMA((6,))],
        final=True,
        vmem_mib=60,
    )
    along = exchange(block, "col", 2)
    mine = turned(mine)
    x_in = [mine] + [exchange(mine, "row", k) for k in range(1, n)]
    (x,) = call(k_prep, [sds(tile, BF16)], [sc, *x_in])
    weights = [whole(a) for a in (w_attn, w_up, w_down)]
    halves = call(k_split, [half_block] * 8, weights, after=x_in[1:], final=True)
    down0, attn1, up1, down1 = [halves[2 * i : 2 * i + 2] for i in range(4)]
    up0 = pack(piece, [layer_of(w_up, 0)], [mine])
    (up0_along,) = along_of([up0])
    near = exchange(block, "col", 1)
    (low,) = held([along], [*x_in[1:], up0_along])
    sources = (block, near, along, exchange(low, "col", 1))
    attn0 = [(a, (piece + 16, hidden), (0, 0)) for a in sources]

    low_tile = sds(tile, BF16)
    unit_out = sds((tokens, model + 128), F32)
    qkv_out, p_out, o_out = (
        sds((tokens, 3 * width), BF16),
        sds((heads, tokens, tokens), F32),
        sds((tokens, width), BF16),
    )
    g_out, slope_out = sds((tokens, hidden), BF16), sds((tokens, hidden), F32)
    feed_out = [low_tile, unit_out, low_tile, g_out, slope_out]

    z, prm, o0, qkv0, p0 = call(
        partial(k_attend_first, m),
        [low_tile, sds((16, model), F32), o_out, qkv_out, p_out],
        [sc, x, *attn0, rowwise],
        after=[down0[0]],
    )
    down0_along = along_of(down0)
    (low,) = call(k_turned, [sds((tokens, piece), BF16)], [whole(cotangent.T)], after=[z], final=True)
    cotan = turned(low)
    z = pair_sum(z, down0_along)
    together = pack(4 * piece, [whole(a) for a in [up0, *down0, up0_along, *down0_along]], [z])
    near = exchange(together, "col", 1)
    up0, down0 = [
        [
            (a, (piece, hidden), (i, 0))
            for a, i in ((together, k), (near, k), (together, 2 + k), (near, 2 + k))
        ]
        for k in range(2)
    ]
    attn1_along = along_of(attn1)
    f, unit_a0, h0, g0, slope0 = call(
        partial(k_feed, m, 0),
        feed_out,
        [*both(z), x, *up0, *down0, rowwise, prm],
        after=attn1_along,
    )
    attn1 = gathered(attn1, attn1_along, after=[f])
    up1_along = along_of(up1[:1])
    f = pair_sum(f, [attn1[1][0], *up1_along])
    up1_along += along_of(up1[1:])
    down1_along = along_of(down1[:1])
    z, unit_b0, x1, o1, qkv1, p1 = call(
        partial(k_attend, m, 1),
        [low_tile, unit_out, low_tile, o_out, qkv_out, p_out],
        [sc, *both(f), unit_a0, *attn1, rowwise, prm],
        after=[up1_along[1], *down1_along],
    )
    down1_along += along_of(down1[1:])
    up1 = gathered(up1, up1_along, after=[z])
    z = pair_sum(z, [down1_along[1], up1[1][0]])
    down1 = gathered(down1, down1_along, after=[z])
    f, unit_a1, h1, g1, slope1 = call(
        partial(k_feed, m, 1),
        feed_out,
        [*both(z), unit_b0, *up1, *down1, rowwise, prm],
        after=[cotan],
    )
    (again,) = held([cotan], [f])
    cotan = [cotan, None] + [exchange(again, "row", k) for k in range(2, n)]
    f = pair_sum(f, cotan[2:])
    cotan[1] = exchange(held([again], [f])[0], "row", 1)
    (cotan,) = call(k_prep, [sds(tile, BF16)], [sc, *cotan], after=[f])

    sums_out = sds((8, model), F32)
    feed_back_out = [sds(tile, F32), low_tile, low_tile, sds((tokens, hidden), BF16), sums_out]
    out, df, df_low, dh, du, sums_b1 = call(
        partial(k_turn, m, 1),
        [sds((piece, tokens), BF16)] + feed_back_out,
        [sc, *both(f), unit_a1, cotan, *up1, *down1, slope1, prm],
        [pltpu.VMEM((tokens, piece), F32)],
    )
    weight_out = [sds((4 * piece, hidden), BF16)] * 2 + [sds((8, hidden), F32)]
    keep, send, hidden_sums1 = call(
        partial(k_feed_weight, m), weight_out, [df_low, g1, h1, du]
    )
    got = exchange(send, "col", 1)
    dh = pair_sum(dh, [got])
    stay1 = call(k_middle, [half_block] * 8, [keep, got], after=[dh])
    more1 = along_of(stay1[4:6])
    da, da_low, dx, grads1, sums_a1 = call(
        partial(k_attend_back, m, 1),
        [sds(tile, F32), low_tile, low_tile, qkv_out, sums_out],
        [*both(dh), df, unit_a1, *attn1, qkv1, p1, prm],
        after=more1,
    )
    keep, send, head_sums1 = call(
        partial(k_attend_weight, m),
        [sds((2 * piece, 4 * width), BF16)] * 2 + [sums_out],
        [x1, grads1, da_low, o1],
    )
    got = exchange(send, "col", 1)
    more1 += along_of(held(stay1[6:7], [dx]))
    (low,) = call(k_add, [half_block], [stay1[0], more1[0]], after=[dx])
    terms1 = [last_of_dp(low)]
    dx = pair_sum(dx, [got, more1[2], terms1[0][1]])
    attn1_stay = call(k_middle, [half_block] * 4, [keep, got], after=[dx])
    more1 += along_of(held(stay1[7:], [dx]))
    attn1_more = along_of(attn1_stay[2:3])
    for i in (1, 2):
        (low,) = call(k_add, [half_block], [stay1[i], more1[i]], after=[dx])
        terms1 += [last_of_dp(low)]

    df, df_low, dh, du, sums_b0 = call(
        partial(k_feed_back, m, 0),
        feed_back_out,
        [*both(dx), da, unit_b0, *up0, *down0, slope0, prm],
        after=[more1[3], *attn1_more, terms1[1][1], terms1[2][1]],
    )
    keep, send, hidden_sums0 = call(
        partial(k_feed_weight, m), weight_out, [df_low, g0, h0, du]
    )
    got = exchange(send, "col", 1)
    attn1_more += along_of(held(attn1_stay[3:], [dh]))
    (low,) = call(k_add, [half_block], [stay1[3], more1[3]], after=[dh])
    terms1 += [last_of_dp(low)]
    dh = pair_sum(dh, [got, attn1_more[1], terms1[3][1]])
    stay0 = call(
        k_middle, [half_block] * 4 + [low_block] + [half_block] * 2, [keep, got], after=[dh]
    )
    more0 = along_of(stay0[4:6])
    attn1_terms = []
    for i in range(2):
        (low,) = call(k_add, [half_block], [attn1_stay[i], attn1_more[i]], after=[dh])
        attn1_terms.append(last_of_dp(low))
    *dx, low_last, grads0, sums_a0 = call(
        partial(k_attend_back_last, n, m),
        [sds((tokens, piece), F32)]
        + [sds((tokens, piece), BF16)] * (n - 1)
        + [low_tile, qkv_out, sums_out],
        [sc, *both(dh), df, unit_a0, *attn0, qkv0, p0, prm],
        after=[*more0, attn1_terms[0][1], attn1_terms[1][1]],
    )
    more0 += along_of(held(stay0[6:], [dx[0]]))
    most = [sds((3 * piece // 2, hidden), BF16)]
    (low,) = call(k_add_whole, most, [*stay0[:3], *more0[:2]])
    most0_terms = last_of_dp(low)
    (results,) = call(
        k_total,
        [sds((2 * piece, tokens), BF16)],
        [dx[0]] + [exchange(dx[k], "row", k) for k in range(1, n)] + [out],
    )
    out_hidden, grad_input, token = call(
        k_results,
        [sds((piece, tokens), BF16), sds((piece, tokens), F32), sds((8, 128), F32)],
        [turned(results)],
        final=2,
    )

    keep, send = call(
        partial(k_attend_weight_last, m),
        [sds((2 * (piece + 16), 4 * width), BF16)] * 2,
        [
            x,
            grads0,
            low_last,
            o0,
            hidden_sums0,
            hidden_sums1,
            head_sums1,
            sums_a0,
            sums_b0,
            sums_a1,
            sums_b1,
        ],
    )
    got = exchange(send, "col", 1)
    low_tail = sds((piece + 16, hidden), BF16)
    attn0_stay, attn0_go = call(k_middle, [low_tail] * 2, [keep, got])
    (attn0_more,) = along_of([attn0_go])
    (low,) = call(k_add, [half_block], [stay0[3], more0[2]])
    rest0_terms = last_of_dp(low)
    (low,) = call(k_add, [low_tail], [attn0_stay, attn0_more], after=[results])
    attn0_terms = [last_of_dp(low)]
    def halves_of(array):
        return [(array, (piece // 2, hidden), (i, 0)) for i in range(3)]

    first = [halves_of(a) + [b] for a, b in zip(most0_terms, rest0_terms)]
    second = [[t[side] for t in terms1] for side in range(2)]
    def feed_terms(which):
        return [
            halves[2 * which + j]
            for side in range(2)
            for halves in (first[side], second[side])
            for j in range(2)
        ]

    mark = sds((8, 128), F32)
    feed_grad = sds((layers, piece, hidden), F32)
    grad_down, down_token = call(
        partial(with_token, k_feed_output),
        [feed_grad, mark],
        feed_terms(0),
        after=[token],
        final=1,
    )
    (
        grad_attn,
        grad_qv,
        grad_out,
        grad_gain,
        grad_shift,
        grad_b_up,
        grad_b_down,
        attend_token,
    ) = call(
        partial(with_token, k_attend_outputs),
        [sds(a.shape, F32) for a in (w_attn, b_qv, b_out, ln_gain, ln_bias, b_up, b_down)]
        + [mark],
        [t[side] for terms in (attn0_terms, attn1_terms) for side in range(2) for t in terms],
        after=[down_token],
        final=7,
    )
    (grad_up,) = call(
        k_feed_output, [feed_grad], feed_terms(1), after=[attend_token], final=True
    )
    return (
        out_hidden.T,
        grad_input.T,
        grad_attn,
        grad_qv,
        grad_out,
        grad_gain,
        grad_shift,
        grad_up,
        grad_b_up,
        grad_down,
        grad_b_down,
    )


def solution(mesh):
    in_specs = (
        P(("dp", "row"), "col"),
        P("dp"),
        P(None, "col", "row"),
        P(None, None, "row"),
        P(None, "col"),
        P(None, None, "col"),
        P(None, None, "col"),
        P(None, "col", "row"),
        P(None, "row"),
        P(None, "col", "row"),
        P(None, "col"),
        P(("dp", "row"), "col"),
    )
    out_specs = (
        P(("dp", "row"), "col"),
        P(("dp", "row"), "col"),
        P(None, "col", "row"),
        P(None, None, "row"),
        P(None, "col"),
        P(None, None, "col"),
        P(None, None, "col"),
        P(None, "col", "row"),
        P(None, "row"),
        P(None, "col", "row"),
        P(None, "col"),
    )
    return jax.shard_map(
        per_device, mesh=mesh, in_specs=in_specs, out_specs=out_specs, check_vma=False
    )
```
